128 devices in a mesh: section: 2 (over core), ep: 64 (over y, z, x).
Axes of the slice: x: 4, y: 4, z: 4, core: 2. Of those that a mesh axis runs over, the one named last changes fastest.
Arguments:
- hidden_in: bfloat16 [2, 896, 7168], P(None, ('section', 'ep')), may hold values from -6 to 6
- ffn_gain: float32 [7168], replicated, may hold values from 0.5 to 1.5
- attn_gain: float32 [7168], replicated, may hold values from 0.5 to 1.5
- kv_gain: float32 [512], replicated, may hold values from 0.5 to 1.5
- expert_ids: int32 [2, 896, 4], P(None, ('section', 'ep')), may hold values from 0 to 15, all different within a row; in each aligned block of 7 rows (0 to 6, 7 to 13, ..., all dimensions but the last counted through in order) at most 3 rows name the same one
- route_weight: float32 [2, 896, 4], P(None, ('section', 'ep')), may hold values from 0.05 to 1
- expert_gate: bfloat16 [128, 7168, 256], P(('section', 'ep')), may hold values from -0.0625 to 0.0625
- expert_up: bfloat16 [128, 7168, 256], P(('section', 'ep')), may hold values from -0.0625 to 0.0625
- expert_down: bfloat16 [128, 256, 7168], P(('section', 'ep')), may hold values from -0.125 to 0.125
- kv_down: bfloat16 [7168, 576], P('section'), may hold values from -0.0625 to 0.0625
- resident_cache: bfloat16 [768, 512, 576], P(('section', 'ep')), may hold values from -6 to 6
- fresh_cache: bfloat16 [128, 512, 576], P(('section', 'ep')), may hold values from -6 to 6
- fresh_order: int32 [128], replicated, may hold values from 0 to 127, each once
- cache_len: int32 [896], P(('section', 'ep')), may hold values from 1 to 510, as said below
- queries: bfloat16 [2, 896, 128, 576], P(None, ('section', 'ep')), may hold values from -120 to 120
Outputs:
- layer_out: bfloat16 [2, 896, 7168], P(None, ('section', 'ep'))
- attn_latent: bfloat16 [2, 896, 65536], P(None, ('section', 'ep'))
The draws below stay inside these ranges and needn't reach their ends.
Inputs may be any that keep to these rules, and one draw needn't show every extreme that they name: `expert_ids`: in each aligned block of 7 rows of one step no expert is named by more than 3 rows, a bound that some block reaches. `fresh_order`: each number once. `cache_len`: some row reaches 510.
All inputs are finite; a program needn't handle non-finite values.
Results may differ from the reference program's by a relative error of at most 0.007.
Values may be sent and summed in bfloat16 or wider, within the bound.
No kernel may reach another device: no remote copies, remote signals or barrier semaphores. Data moves between devices by JAX's collectives and lax.ppermute only.
A program may use at most 192 MiB of HBM per device.

```python
import math
import jax
import jax.numpy as jnp
import numpy as np
from jax import lax

D = 7168
FF = 2048
HEADS = 128
LAT = 512
ROPE = 64
NOPE = 128
EXPERTS = 16
TOP = 4
CAP = 3
STEPS = 2
RES_DEV = 6
FRESH_DEV = 1
CTX = 512
ROWS_DEV = 7
ROWS = 896
RES = 768
FRESH = 128
FF_UNIT = 256
QK = 576
N_SECTION = 2
N_EP = 64
DEVICES = 128


def draw_cache_len(key, part):
    key = jax.random.fold_in(key, 11)
    first_key, second_key, third_key = jax.random.split(key, 3)
    resident_len = jax.random.randint(first_key, (ROWS,), 1, CTX - 1)
    fresh_len = jax.random.randint(second_key, (ROWS,), CTX // 2, CTX - 1)
    local_slot = jnp.arange(ROWS) % ROWS_DEV
    lengths = jnp.where(local_slot < RES_DEV, resident_len, fresh_len)
    longest = jax.random.randint(third_key, (), 0, ROWS)
    return lengths.at[longest].set(CTX - 2).astype(jnp.int32)


def draw_queries(key, part):
    key = jax.random.fold_in(key, 23)
    first_key = jax.random.fold_in(key, 0)
    shape = (STEPS, ROWS, HEADS, LAT + ROPE)
    return (0.8 * jax.random.truncated_normal(first_key, -6.0, 6.0, shape, jnp.float32)).astype(jnp.bfloat16)


def shard_levels(key, shape, shards, least, high):
    gain, own = 1.0, jax.random.fold_in(key, 6)
    for axis_at, shards_of in shards:
        steps = jnp.exp(jax.random.uniform(jax.random.fold_in(own, axis_at), (shards_of,), jnp.float32, least / len(shards), high / len(shards)))
        gain = gain * jnp.repeat(steps, shape[axis_at] // shards_of).reshape([-1 if axis == axis_at else 1 for axis in range(len(shape))])
    return gain


def shared_out(own_key, own, number, rows, number_of, top, bound, skew):
    ranking = jax.random.permutation(own_key, number_of)
    packed, common = portions_of(number_of, rows * top, bound, skew, True), portions_of(number_of, rows * top, bound, skew, False)
    places = jnp.arange(number_of)

    def named(tallies, turn):
        used = int((tallies > 0).sum())
        fixed = max(1, used // 4)
        shifted = fixed + (places - fixed + turn * (used - fixed)) % max(1, number_of - fixed)
        return jnp.zeros((number_of,), jnp.int32).at[ranking[jnp.where(places < fixed, places, shifted)]].set(jnp.asarray(tallies, jnp.int32))

    tallies = jnp.where(number % 4 == 0, named(packed, number // 4), named(common, number - number // 4 - 1))
    mixed = jax.random.permutation(jax.random.fold_in(own, 3), number_of)
    giver, taker = mixed[0:number_of // 2 * 2:2], mixed[1:number_of // 2 * 2:2]
    room = jnp.minimum(tallies[giver] - 1, bound - tallies[taker]) // 2
    room = jnp.where((giver == ranking[0]) | (taker == ranking[0]) | (tallies[taker] == 0), 0, jnp.maximum(room, 0))
    shifted = jax.random.randint(jax.random.fold_in(own, 4), (number_of // 2,), 0, 1 << 20) % (room + 1)
    tallies = tallies.at[giver].add(-shifted).at[taker].add(shifted)
    items = jnp.searchsorted(jnp.cumsum(tallies), jnp.arange(rows * top), side="right").astype(jnp.int32)
    listing = items.reshape(top, rows).T
    listing = listing[jax.random.permutation(jax.random.fold_in(own, 1), rows)]
    turn = jax.random.randint(jax.random.fold_in(own, 2), (rows, 1), 0, top)
    return jnp.take_along_axis(listing, (jnp.arange(top)[None, :] + turn) % top, axis=1)


def portions_of(amount, total, reach, skew, full):
    loads = [(1 << 20) // math.isqrt(standing ** skew) + 1 for standing in range(1, amount + 1)]
    largest = reach if full else min(reach, max(-(-total // amount), total * loads[0] // sum(loads)))
    least = 1 if total - largest >= amount - 1 else 0
    counts, surplus = [largest] + [least] * (amount - 1), total - largest - least * (amount - 1)
    while surplus > 0:
        candidates = [i for i in range(1, amount) if counts[i] < largest] or [i for i in range(1, amount) if counts[i] < reach]
        whole, budget = sum([loads[i] for i in candidates]), surplus
        for i in candidates:
            addition = min(reach - counts[i], max(1, budget * loads[i] // whole), surplus)
            counts[i] = counts[i] + addition
            surplus = surplus - addition
    return np.array(counts)


def centred(own_key, extent, scale, limit, shards=(), held_as=jnp.bfloat16):
    gain = shard_levels(own_key, extent, shards, -0.22, 0.18) if shards else 1.0
    values = jax.random.normal(own_key, extent, jnp.float32) * scale * gain
    return jnp.minimum(jnp.maximum(values, -limit), limit).astype(held_as)


def setup_inputs(seed: int = 0) -> dict:
    seeds = jax.random.split(jax.random.key(seed), 16)
    hidden_in = centred(seeds[0], (STEPS, ROWS, D), 1.0, 6.0, ((1, 128),))
    ffn_gain = jnp.clip(1.0 + 0.1 * jax.random.normal(seeds[1], (D,), jnp.float32), 0.5, 1.5)
    attn_gain = jnp.clip(1.0 + 0.1 * jax.random.normal(seeds[2], (D,), jnp.float32), 0.5, 1.5)
    kv_gain = jnp.clip(1.0 + 0.1 * jax.random.normal(seeds[3], (LAT,), jnp.float32), 0.5, 1.5)
    expert_ids_keys = jax.random.split(jax.random.fold_in(seeds[4], 1), STEPS * ROWS // ROWS_DEV)
    expert_ids_turns = jax.random.permutation(jax.random.fold_in(seeds[4], 3), STEPS * ROWS // ROWS_DEV)
    expert_ids = jax.vmap(lambda own, number: shared_out(jax.random.fold_in(seeds[4], 2), own, number, ROWS_DEV, EXPERTS, TOP, CAP, 2))(expert_ids_keys, expert_ids_turns).reshape((STEPS, ROWS, TOP))
    route_weight = jnp.clip(jnp.exp(math.log(1.0) - 2.9957323 * jax.random.uniform(seeds[5], (STEPS, ROWS, TOP), jnp.float32) ** shard_levels(seeds[5], (STEPS, ROWS, TOP), ((1, 128),), -0.2, 0.2)), 0.05, 1.0)
    expert_gate = centred(seeds[6], (DEVICES, D, FF_UNIT), D ** -0.5, 0.0625, ((0, 128),))
    expert_up = centred(seeds[7], (DEVICES, D, FF_UNIT), D ** -0.5, 0.0625, ((0, 128),))
    expert_down = centred(seeds[8], (DEVICES, FF_UNIT, D), FF ** -0.5, 0.125, ((0, 128),))
    kv_down = centred(seeds[9], (D, QK), D ** -0.5, 0.0625, ((0, 2),))
    resident_cache = centred(seeds[10], (RES, CTX, QK), 1.0, 6.0, ((0, 128),))
    fresh_cache = centred(seeds[11], (FRESH, CTX, QK), 1.0, 6.0, ((0, 128),))
    fresh_order = jax.random.permutation(seeds[12], FRESH).astype(jnp.int32)
    cache_len = draw_cache_len(jax.random.fold_in(seeds[15], 71), 0)
    queries = draw_queries(jax.random.fold_in(seeds[15], 71), 0)
    return {"hidden_in": hidden_in, "ffn_gain": ffn_gain, "attn_gain": attn_gain, "kv_gain": kv_gain, "expert_ids": expert_ids, "route_weight": route_weight, "expert_gate": expert_gate, "expert_up": expert_up, "expert_down": expert_down, "kv_down": kv_down, "resident_cache": resident_cache, "fresh_cache": fresh_cache, "fresh_order": fresh_order, "cache_len": cache_len, "queries": queries}


epsilon = 1e-06
route_scaling = 2.5
rope_base = 10000.0
masked_score = -1e+30

def rms_scale(values, gain_vector):
    values = values.astype(jnp.float32)
    return values * lax.rsqrt(lax.optimization_barrier(jnp.mean(values * values, axis=-1, keepdims=True)) + epsilon) * gain_vector

def rotate_pairs(values, positions):
    halfway = values.shape[-1] // 2
    frequency = rope_base ** (-2.0 * jnp.arange(halfway).astype(jnp.float32) / values.shape[-1])
    angles = positions[:, None] * frequency[None, :]
    cosine = jnp.cos(angles)
    sine_part = jnp.sin(angles)
    first_half = values[:, :halfway]
    second_half = values[:, halfway:]
    return jnp.concatenate([first_half * cosine - second_half * sine_part, second_half * cosine + first_half * sine_part], axis=-1)

def expert_layer(hidden, route_ids, weights, expert_gate, expert_up, expert_down, ffn_gain):
    devices = N_SECTION * N_EP
    subgroup = N_EP // EXPERTS
    pairs = ROWS_DEV * TOP
    normed = rms_scale(hidden, ffn_gain).astype(jnp.bfloat16)
    flat_ids = route_ids.reshape(devices, pairs).astype(jnp.int32)
    onehot = (flat_ids[:, :, None] == jnp.arange(EXPERTS, dtype=jnp.int32)[None, None, :]).astype(jnp.int32)
    before = jnp.cumsum(onehot, axis=1) - onehot
    slot_index = lax.optimization_barrier(jnp.sum(before * onehot, axis=2)).astype(jnp.int32)
    source = (jnp.arange(devices, dtype=jnp.int32)[:, None] * jnp.ones((1, pairs), jnp.int32)).astype(jnp.int32)
    rows_of = jnp.repeat(normed, TOP, axis=0).reshape(devices, pairs, D)
    buckets = jnp.zeros((EXPERTS, devices, CAP, D), jnp.bfloat16).at[flat_ids, source, slot_index].set(rows_of)

    def one_expert(expert):
        slot_rows = buckets[expert].reshape(devices * CAP, D)

        def one_sub(running, sub_index):
            pair_total = jnp.zeros((devices * CAP, D), jnp.float32)
            for core_index in range(N_SECTION):
                unit_index = core_index * N_EP + expert * subgroup + sub_index
                gate_value = jnp.dot(slot_rows, expert_gate[unit_index], preferred_element_type=jnp.float32)
                up_value = jnp.dot(slot_rows, expert_up[unit_index], preferred_element_type=jnp.float32)
                active = (jax.nn.silu(gate_value) * up_value).astype(jnp.bfloat16)
                partial_sum = jnp.dot(active, expert_down[unit_index], preferred_element_type=jnp.float32).astype(jnp.bfloat16)
                pair_total = pair_total + partial_sum.astype(jnp.float32)
            rounded = lax.optimization_barrier(pair_total.astype(jnp.bfloat16))
            return (running + rounded.astype(jnp.float32), None)
        return lax.scan(one_sub, jnp.zeros((devices * CAP, D), jnp.float32), jnp.arange(subgroup, dtype=jnp.int32))[0]
    combined = lax.map(one_expert, jnp.arange(EXPERTS, dtype=jnp.int32))
    picked = combined[flat_ids, source * CAP + slot_index]
    shares = weights / lax.optimization_barrier(jnp.sum(weights, axis=-1, keepdims=True)) * route_scaling
    shares = shares.reshape(devices, pairs)
    mixture = lax.optimization_barrier(jnp.sum((picked * shares[:, :, None]).reshape(ROWS, TOP, D), axis=1))
    return (hidden.astype(jnp.float32) + mixture).astype(jnp.bfloat16)

def attend(query_rows, cache_rows, visible, new_keys, score_scale):
    scores = jnp.einsum('rhq,rcq->rhc', query_rows, cache_rows) * score_scale
    scores = jnp.where(visible, scores, masked_score)
    own_scores = jnp.einsum('rhq,krq->rhk', query_rows, new_keys) * score_scale
    highest = jnp.maximum(lax.optimization_barrier(jnp.max(scores, axis=-1)), lax.optimization_barrier(jnp.max(own_scores, axis=-1)))
    cache_weight = jnp.where(visible, jnp.exp(scores - highest[..., None]), 0.0)
    own_weight = jnp.exp(own_scores - highest[..., None])
    denominator = lax.optimization_barrier(jnp.sum(cache_weight, axis=-1)) + lax.optimization_barrier(jnp.sum(own_weight, axis=-1))
    cache_probs = (cache_weight / denominator[..., None]).astype(jnp.bfloat16).astype(jnp.float32)
    own_probs = (own_weight / denominator[..., None]).astype(jnp.bfloat16).astype(jnp.float32)
    mixture = jnp.einsum('rhc,rcl->rhl', cache_probs, cache_rows[:, :, :LAT])
    mixture = mixture + jnp.einsum('rhk,krl->rhl', own_probs, new_keys[:, :, :LAT])
    return mixture.reshape(mixture.shape[0], HEADS * LAT).astype(jnp.bfloat16)

def reference(hidden_in, ffn_gain, attn_gain, kv_gain, expert_ids, route_weight, expert_gate, expert_up, expert_down, kv_down, resident_cache, fresh_cache, fresh_order, cache_len, queries):
    devices = N_SECTION * N_EP
    score_scale = (NOPE + ROPE) ** (-0.5)
    layer_out = jnp.stack([expert_layer(hidden_in[step_index], expert_ids[step_index], route_weight[step_index], expert_gate, expert_up, expert_down, ffn_gain) for step_index in range(STEPS)])
    normed = rms_scale(layer_out, attn_gain).astype(jnp.bfloat16).reshape(STEPS * ROWS, D)
    projected = jnp.dot(normed, kv_down, preferred_element_type=jnp.float32).reshape(STEPS, ROWS, LAT + ROPE)
    latent_part = rms_scale(projected[..., :LAT], kv_gain)
    positions = cache_len.astype(jnp.float32)[None, :] + jnp.arange(STEPS).astype(jnp.float32)[:, None]
    rotated = rotate_pairs(projected[..., LAT:].reshape(STEPS * ROWS, ROPE), positions.reshape(-1)).reshape(STEPS, ROWS, ROPE)
    new_keys = jnp.concatenate([latent_part, rotated], axis=-1).astype(jnp.bfloat16)

    def per_device(device):
        resident = lax.dynamic_slice_in_dim(resident_cache, (device * RES_DEV).astype(jnp.int32), RES_DEV, 0)
        chosen_fresh = lax.dynamic_slice_in_dim(fresh_order, (device * FRESH_DEV).astype(jnp.int32), FRESH_DEV, 0)
        fresh_rows = jnp.take(fresh_cache, chosen_fresh.astype(jnp.int32), axis=0)
        caches = jnp.concatenate([resident, fresh_rows], axis=0).astype(jnp.float32)
        lengths = lax.dynamic_slice_in_dim(cache_len, (device * ROWS_DEV).astype(jnp.int32), ROWS_DEV, 0)
        query_rows = lax.dynamic_slice_in_dim(queries, (device * ROWS_DEV).astype(jnp.int32), ROWS_DEV, 1).astype(jnp.float32)
        keys_new = lax.dynamic_slice_in_dim(new_keys, (device * ROWS_DEV).astype(jnp.int32), ROWS_DEV, 1).astype(jnp.float32)
        visible = jnp.arange(CTX, dtype=jnp.int32)[None, None, :] < lengths[:, None, None]
        outputs = []
        for step_index in range(STEPS):
            outputs.append(attend(query_rows[step_index], caches, visible, keys_new[:step_index + 1], score_scale))
        return jnp.stack(outputs)
    result = lax.map(per_device, jnp.arange(devices, dtype=jnp.int32))
    attended = jnp.transpose(result, (1, 0, 2, 3)).reshape(STEPS, ROWS, HEADS * LAT)
    return (layer_out, attended)
```

```python
import jax
import jax.numpy as jnp
from jax import lax
from jax.sharding import Mesh, PartitionSpec as P

LAT = 512
ROPE = 64
NOPE = 128
EXPERTS = 16
TOP = 4
CAP = 3
BLOCK = 8
META = 128


epsilon = 1e-06
route_scaling = 2.5
rope_base = 10000.0
masked_score = -1e30
f32 = jnp.float32
bf16 = jnp.bfloat16


def rms_scale(values, gain_vector):
    values = values.astype(jnp.float32)
    return (
        values
        * lax.rsqrt(jnp.mean(values * values, axis=-1, keepdims=True) + epsilon)
        * gain_vector
    )


def rotate_pairs(values, positions):
    halfway = values.shape[-1] // 2
    frequency = rope_base ** (-2.0 * jnp.arange(halfway).astype(jnp.float32) / values.shape[-1])
    angles = positions[:, None] * frequency[None, :]
    cosine = jnp.cos(angles)
    sine_part = jnp.sin(angles)
    first_half = values[:, :halfway]
    second_half = values[:, halfway:]
    return jnp.concatenate(
        [
            first_half * cosine - second_half * sine_part,
            second_half * cosine + first_half * sine_part,
        ],
        axis=-1,
    )


def attend(query_rows, cache_rows, key_position, lengths, new_keys, score_scale):
    scores = (
        jnp.einsum("rhq,rcq->rhc", query_rows, cache_rows, preferred_element_type=jnp.float32)
        * score_scale
    )
    visible = key_position[None, None, :] < lengths[:, None, None]
    scores = jnp.where(visible, scores, masked_score)
    own_scores = (
        jnp.einsum("rhq,krq->rhk", query_rows, new_keys, preferred_element_type=jnp.float32)
        * score_scale
    )
    highest = jnp.maximum(jnp.max(scores, axis=-1), jnp.max(own_scores, axis=-1))
    cache_weight = jnp.where(visible, jnp.exp(scores - highest[..., None]), 0.0)
    own_weight = jnp.exp(own_scores - highest[..., None])
    denominator = jnp.sum(cache_weight, axis=-1) + jnp.sum(own_weight, axis=-1)
    cache_probs = (cache_weight / denominator[..., None]).astype(jnp.bfloat16)
    own_probs = (own_weight / denominator[..., None]).astype(jnp.bfloat16)
    mixture = jnp.einsum(
        "rhc,rcl->rhl", cache_probs, cache_rows[:, :, :LAT], preferred_element_type=jnp.float32
    )
    mixture = mixture + jnp.einsum(
        "rhk,krl->rhl", own_probs, new_keys[:, :, :LAT], preferred_element_type=jnp.float32
    )
    return mixture.reshape(mixture.shape[0], -1).astype(jnp.bfloat16)


def shift(values, axis, by):
    size = lax.axis_size(axis)
    return lax.ppermute(values, axis, [(i, (i + by) % size) for i in range(size)])


def add(*terms):
    return sum(term.astype(f32) for term in terms).astype(bf16)


def select_tables(meta):
    high, low = meta[:, :EXPERTS], meta[:, EXPERTS : 2 * EXPERTS]
    rows = meta.shape[0]
    named = (high > 0).astype(bf16)
    one = jnp.arange(rows)
    lower = ((one[None, :] < one[:, None]) & (one[None, :] // BLOCK == one[:, None] // BLOCK)).astype(bf16)
    before = jnp.dot(lower, named, preferred_element_type=f32).astype(bf16)
    slots = jnp.arange(4 * 4 * CAP)
    expert = lax.axis_index("y") * 4 + (lax.axis_index("z") + slots // (4 * CAP)) % 4
    pick = (expert[:, None] == jnp.arange(EXPERTS)[None, :]).astype(bf16)

    def of_slot(table):
        return lax.dot_general(pick, table, (((1,), (1,)), ((), ())), preferred_element_type=f32)

    here = (
        (of_slot(named) > 0.5)
        & (of_slot(before) == (slots % CAP)[:, None].astype(f32))
        & ((slots // CAP % 4)[:, None] == (one // BLOCK)[None, :])
    )
    zero = jnp.zeros((), f32)
    return (
        here.astype(bf16),
        jnp.where(here, of_slot(high), zero).astype(bf16),
        jnp.where(here, of_slot(low), zero).astype(bf16),
    )


def fold(values):
    half = values.shape[1] // 2
    return jnp.concatenate([values[:, :half], values[:, half:]], axis=0)


def unfold(values):
    half = values.shape[0] // 2
    return jnp.concatenate([values[:half], values[half:]], axis=1)


def spread_y(rows):
    return jnp.concatenate([rows, shift(rows, "y", 1), shift(rows, "y", 3), shift(rows, "y", 2)], axis=0)


def spread_z(slots):
    part = 4 * CAP
    parts = [slots[i * part : (i + 1) * part] for i in range(4)]
    moved = [unfold(shift(fold(parts[i]), "z", i)) for i in (1, 3, 2)]
    return jnp.concatenate([parts[0], moved[0], moved[2], moved[1]], axis=0)


def back_z(slots):
    part = 4 * CAP
    parts = [slots[i * part : (i + 1) * part] for i in range(4)]
    moved = [unfold(shift(fold(parts[i]), "z", 4 - i)) for i in (1, 3, 2)]
    return jnp.concatenate([parts[0], moved[0], moved[2], moved[1]], axis=0)


def spread_x(own):
    half = own.shape[0] // 2
    left = shift(own, "x", 1)
    right = shift(own, "x", 3)
    far_a = shift(left[:half], "x", 1)
    far_b = shift(right[half:], "x", 3)
    return [own, left, right, jnp.concatenate([far_a, far_b], axis=0)]


def back_x(own, left, right, far):
    half = own.shape[0] // 2
    got_a = shift(far[:half], "x", 1)
    got_b = shift(far[half:], "x", 3)
    from_left_b = shift(right[half:], "x", 1)
    from_right_a = shift(left[:half], "x", 3)
    from_left_a = shift(add(right[:half], got_a), "x", 1)
    from_right_b = shift(add(left[half:], got_b), "x", 3)
    return jnp.concatenate(
        [
            add(own[:half], from_left_a, from_right_a),
            add(own[half:], from_left_b, from_right_b),
        ],
        axis=0,
    )


def swap(values):
    return shift(values, "c", 1)


def expert_rows(slot_rows, gate_unit, up_unit, down_unit):
    gate_value = jnp.dot(slot_rows, gate_unit, preferred_element_type=f32)
    up_value = jnp.dot(slot_rows, up_unit, preferred_element_type=f32)
    active = (jax.nn.silu(gate_value) * up_value).astype(bf16)
    return jnp.dot(active, down_unit, preferred_element_type=f32).astype(bf16)


def shards(
    hidden_in,
    ffn_gain,
    attn_gain,
    kv_gain,
    expert_ids,
    route_weight,
    expert_gate,
    expert_up,
    expert_down,
    kv_down,
    resident_cache,
    fresh_cache,
    fresh_order,
    cache_len,
    queries,
):
    steps_count, local_rows, model_width = hidden_in.shape
    resident_rows = resident_cache.shape[0]
    score_scale = (NOPE + ROPE) ** (-0.5)
    gate_unit = expert_gate[0]
    up_unit = expert_up[0]
    down_unit = expert_down[0]

    spread = lax.all_to_all(fresh_cache, ("c", "y", "z", "x"), split_axis=1, concat_axis=0, tiled=True)
    ordered = jnp.take(spread, fresh_order, axis=0)
    fresh_rows = lax.all_to_all(ordered, ("c", "y", "z", "x"), split_axis=0, concat_axis=1, tiled=True)

    shares = route_weight / jnp.sum(route_weight, axis=-1, keepdims=True) * route_scaling
    dense_share = jnp.sum(
        jnp.where(
            expert_ids[..., None] == jnp.arange(EXPERTS, dtype=jnp.int32), shares[..., None], 0.0
        ),
        axis=2,
    )
    high = dense_share.astype(bf16)
    low = (dense_share - high.astype(f32)).astype(bf16)
    normed = rms_scale(hidden_in, ffn_gain).astype(bf16)
    meta_rows = jnp.concatenate(
        [high, low, jnp.zeros((steps_count, local_rows, META - 2 * EXPERTS), bf16)], axis=2
    )
    payload = jnp.pad(
        jnp.concatenate([normed, meta_rows], axis=2), ((0, 0), (0, BLOCK - local_rows), (0, 0))
    )

    tables = []
    shared = []
    for step in range(steps_count):
        held = spread_y(payload[step])
        table = select_tables(held[:, model_width:])
        slots = jnp.dot(table[0], held[:, :model_width], preferred_element_type=f32).astype(bf16)
        tables.append(table)
        shared.append(spread_x(spread_z(slots)))
    returned = []
    for step in range(steps_count):
        own_core = jnp.concatenate(shared[step], axis=0)
        other_core = swap(own_core)
        partial = expert_rows(jnp.concatenate([own_core, other_core], axis=0), gate_unit, up_unit, down_unit)
        many = own_core.shape[0]
        summed = add(partial[:many], swap(partial[many:]))
        quarter = many // 4
        returned.append(back_x(*[summed[i * quarter : (i + 1) * quarter] for i in range(4)]))
    outputs_hidden = []
    for step in range(steps_count):
        slots = back_z(returned[step])
        _, table_high, table_low = tables[step]
        over_slots = (((0,), (0,)), ((), ()))
        combined = lax.dot_general(table_high, slots, over_slots, preferred_element_type=f32)
        combined = combined + lax.dot_general(table_low, slots, over_slots, preferred_element_type=f32)
        combined_low = combined.astype(bf16)
        mixture = (
            combined[:BLOCK]
            + shift(combined_low[BLOCK : 2 * BLOCK], "y", 3).astype(f32)
            + shift(combined_low[2 * BLOCK : 3 * BLOCK], "y", 1).astype(f32)
            + shift(combined_low[3 * BLOCK :], "y", 2).astype(f32)
        )
        outputs_hidden.append((hidden_in[step].astype(f32) + mixture[:local_rows]).astype(bf16))
    layer_out = jnp.stack(outputs_hidden)
    normed_all = (
        rms_scale(layer_out, attn_gain).astype(bf16).reshape(steps_count * local_rows, model_width)
    )
    other_down = swap(kv_down)
    core = lax.axis_index("c")
    first_down = jnp.where(core == 0, kv_down, other_down)
    second_down = jnp.where(core == 0, other_down, kv_down)
    half = kv_down.shape[0]
    projected = jnp.dot(normed_all[:, :half], first_down, preferred_element_type=f32) + jnp.dot(
        normed_all[:, half:], second_down, preferred_element_type=f32
    )
    projected = projected.reshape(steps_count, local_rows, -1)
    latent_part = rms_scale(projected[..., :LAT], kv_gain)
    positions = cache_len.astype(f32)[None, :] + jnp.arange(steps_count).astype(f32)[:, None]
    rotated = rotate_pairs(projected[..., LAT:].reshape(-1, ROPE), positions.reshape(-1)).reshape(
        steps_count, local_rows, ROPE
    )
    new_keys = jnp.concatenate([latent_part, rotated], axis=-1).astype(bf16)
    fresh_position = jnp.arange(fresh_rows.shape[1], dtype=jnp.int32)
    resident_position = jnp.arange(resident_cache.shape[1], dtype=jnp.int32)
    attended = []
    for step_index in range(steps_count):
        keys_now = new_keys[: step_index + 1]
        query_now = queries[step_index]
        first_block = attend(
            query_now[:resident_rows],
            resident_cache,
            resident_position,
            cache_len[:resident_rows],
            keys_now[:, :resident_rows],
            score_scale,
        )
        second_block = attend(
            query_now[resident_rows:],
            fresh_rows,
            fresh_position,
            cache_len[resident_rows:],
            keys_now[:, resident_rows:],
            score_scale,
        )
        attended.append(jnp.concatenate([first_block, second_block], axis=0))
    return (layer_out, jnp.stack(attended))


def solution(mesh):
    grid = Mesh(mesh.devices.reshape(2, 4, 4, 4), ("c", "y", "z", "x"))
    every = ("c", "y", "z", "x")
    placed = (
        P(None, every, None),
        P(),
        P(),
        P(),
        P(None, every, None),
        P(None, every, None),
        P(every, None, None),
        P(every, None, None),
        P(every, None, None),
        P("c", None),
        P(every, None, None),
        P(every, None, None),
        P(),
        P(every),
        P(None, every, None, None),
    )
    return jax.shard_map(
        shards,
        mesh=grid,
        in_specs=placed,
        out_specs=(P(None, every, None), P(None, every, None)),
        check_vma=False,
    )
```

```python
import functools

import jax
import jax.numpy as jnp
import numpy as np
from jax import lax
from jax.experimental import pallas as pl
from jax.experimental.pallas import tpu as pltpu
from jax.sharding import Mesh, PartitionSpec as P

LAT = 512
ROPE = 64
NOPE = 128
EXPERTS = 16
CAP = 3
BLOCK = 8
META = 128
SIDE = 4
PART = SIDE * CAP
SLOTS = SIDE * PART


epsilon = 1e-06
route_scaling = 2.5
rope_base = 10000.0
masked_score = -1e30
f32 = jnp.float32
bf16 = jnp.bfloat16
NT = (((1,), (1,)), ((), ()))
TN = (((0,), (0,)), ((), ()))


def rms_scale(values, gain_vector):
    values = values.astype(f32)
    return (
        values
        * lax.rsqrt(jnp.mean(values * values, axis=-1, keepdims=True) + epsilon)
        * gain_vector
    )


def shift(values, axis, by):
    size = lax.axis_size(axis)
    return lax.ppermute(values, axis, [(i, (i + by) % size) for i in range(size)])


def add(*terms):
    return sum(term.astype(f32) for term in terms).astype(bf16)


def swap(values):
    return shift(values, "c", 1)


def dot(a, b, dims=(((1,), (0,)), ((), ()))):
    return lax.dot_general(a, b, dims, preferred_element_type=f32)


def call(kernel, outs, *args, smem=0, flops=0, limit=32):
    specs = [pl.BlockSpec(memory_space=pltpu.SMEM)] * smem
    specs += [pl.BlockSpec(memory_space=pltpu.VMEM)] * (len(args) - smem)
    moved = sum(a.size * a.dtype.itemsize for a in args)
    return pl.pallas_call(
        kernel,
        out_shape=[jax.ShapeDtypeStruct(shape, dtype) for shape, dtype in outs],
        in_specs=specs,
        out_specs=[pl.BlockSpec(memory_space=pltpu.VMEM)] * len(outs),
        compiler_params=pltpu.CompilerParams(vmem_limit_bytes=limit * 2**20),
        cost_estimate=pl.CostEstimate(flops=flops, bytes_accessed=moved, transcendentals=0),
    )(*args)


FOLD_ROW = np.arange(SIDE * 2 * PART)
FOLD_BLOCK = FOLD_ROW // (2 * PART)
FOLD_HALF = FOLD_ROW % (2 * PART) // PART
FOLD_SLOT = FOLD_ROW % PART
PLACE = np.stack(
    [
        (np.arange(SLOTS)[:, None] == (FOLD_BLOCK * PART + FOLD_SLOT)[None, :]) & (FOLD_HALF == half)[None, :]
        for half in (0, 1)
    ]
).astype(np.float32)


def fold_tables():
    expert = lax.axis_index("y") * SIDE + (lax.axis_index("z") + FOLD_BLOCK) % SIDE
    lanes = jnp.arange(META)[None, :]
    pick = jnp.stack([expert[:, None] == lanes, expert[:, None] + EXPERTS == lanes]).astype(bf16)
    columns = np.arange(SIDE * BLOCK)
    same = ((FOLD_SLOT // CAP)[:, None] == (columns // BLOCK)[None, :]).astype(np.float32)
    turn = np.broadcast_to((FOLD_SLOT % CAP)[:, None], same.shape).astype(np.float32)
    half = np.broadcast_to(FOLD_HALF[:, None], same.shape).astype(np.float32)
    lower = (columns[None, :] < columns[:, None]) & (
        columns[None, :] // BLOCK == columns[:, None] // BLOCK
    )
    return pick, jnp.asarray(np.stack([same, turn, half])), jnp.asarray(lower.astype(np.float32), bf16)


def select_kernel(pick, fixed, lower, b0, b1, b2, b3, o0, o1, o2, o3, weights):
    held = jnp.concatenate([b[...].astype(f32) for b in (b0, b1, b2, b3)], axis=0)
    width = held.shape[1] - META
    half = width // 2
    meta = held[:, width:]
    lane = lax.broadcasted_iota(jnp.int32, meta.shape, 1)
    named = jnp.where((meta > 0) & (lane < EXPERTS), 1.0, 0.0).astype(bf16)
    meta = meta.astype(bf16)
    before = dot(lower[...], named).astype(bf16)
    here = (dot(pick[0], named, NT) > 0.5) & (dot(pick[0], before, NT) == fixed[1]) & (fixed[0] > 0.5)
    second = fixed[2] > 0.5
    sel = jnp.where(here, 1.0, 0.0)
    low_half = jnp.where(second, 0.0, sel).astype(bf16)
    high_half = jnp.where(second, sel, 0.0).astype(bf16)
    weights[0] = jnp.where(here, dot(pick[0], meta, NT), 0.0)
    weights[1] = jnp.where(here, dot(pick[1], meta, NT), 0.0)
    slots = dot(low_half, held[:, :half].astype(bf16)) + dot(high_half, held[:, half:width].astype(bf16))
    for i, o in enumerate((o0, o1, o2, o3)):
        o[...] = slots[i * 2 * PART : (i + 1) * 2 * PART].astype(bf16)


def assemble_kernel(place, f0, f1, f2, f3, out):
    half = f0.shape[1]
    for h in range(2):
        total = 0.0
        for i, f in enumerate((f0, f1, f2, f3)):
            total = total + dot(place[h, i], f[...])
        out[:, h * half : (h + 1) * half] = total.astype(bf16)


def finish_kernel(place, own, la, ra, lb, rb, o0, o1, o2, o3):
    quarter = la.shape[0]
    half = own.shape[1] // 2
    total = [0.0] * SIDE
    for h in range(2):
        cols = slice(h * half, (h + 1) * half)
        first = own[:quarter, cols].astype(f32) + la[:, cols].astype(f32) + ra[:, cols].astype(f32)
        second = own[quarter:, cols].astype(f32) + lb[:, cols].astype(f32) + rb[:, cols].astype(f32)
        summed = jnp.concatenate([first, second], axis=0).astype(bf16)
        for i in range(SIDE):
            total[i] = total[i] + dot(place[h, i], summed, TN)
    for i, o in enumerate((o0, o1, o2, o3)):
        o[...] = total[i].astype(bf16)


def combine_kernel(fixed, weights, f0, f1, f2, f3, own, o1, o2, o3):
    half = f0.shape[1]
    many = 2 * PART
    for h in range(2):
        cols = slice(h * half, (h + 1) * half)
        total = 0.0
        for i, f in enumerate((f0, f1, f2, f3)):
            rows = slice(i * many, (i + 1) * many)
            mine = (fixed[2, rows] > 0.5) if h else (fixed[2, rows] < 0.5)
            for k in range(2):
                share = jnp.where(mine, weights[k, rows], 0.0).astype(bf16)
                total = total + dot(share, f[...], TN)
        own[:, cols] = total[:BLOCK]
        for i, o in enumerate((o1, o2, o3)):
            o[:, cols] = total[(i + 1) * BLOCK : (i + 2) * BLOCK].astype(bf16)


CHUNK = 512


def expert_kernel(pieces, chunks, *refs):
    xs, others = refs[:pieces], refs[pieces : 2 * pieces]
    gate, up, down, mine, theirs, gate_sum, up_sum, active = refs[2 * pieces :]
    step = pl.program_id(0)

    @pl.when(step == 0)
    def _():
        gate_sum[...] = jnp.zeros_like(gate_sum)
        up_sum[...] = jnp.zeros_like(up_sum)

    @pl.when(step < chunks)
    def _():
        at = 0
        rows = jnp.concatenate([x[...].astype(f32) for x in xs + others], axis=0).astype(bf16)
        gate_sum[...] += dot(rows, gate[0])
        up_sum[...] += dot(rows, up[0])

    @pl.when(step == chunks)
    def _():
        value = gate_sum[...]
        active[...] = (value / (1.0 + jnp.exp(-value)) * up_sum[...]).astype(bf16)

    @pl.when(step >= chunks)
    def _():
        many = mine.shape[0]
        result = dot(active[...], down[0])
        mine[...] = result[:many].astype(bf16)
        theirs[...] = result[many:].astype(bf16)


def experts(xs, others, gate, up, down):
    pieces = len(xs)
    many = sum(x.shape[0] for x in xs)
    width, units = gate.shape[1:]
    chunks = width // CHUNK

    def first(s):
        return jnp.minimum(s, chunks - 1)

    def second(s):
        return jnp.maximum(s - chunks, 0)

    in_specs = [pl.BlockSpec((x.shape[0], CHUNK), lambda s: (0, first(s))) for x in xs + others]
    in_specs += [pl.BlockSpec((1, CHUNK, units), lambda s: (0, first(s), 0))] * 2
    in_specs += [pl.BlockSpec((1, units, CHUNK), lambda s: (0, 0, second(s)))]
    return pl.pallas_call(
        functools.partial(expert_kernel, pieces, chunks),
        grid=(2 * chunks,),
        out_shape=[jax.ShapeDtypeStruct((many, width), bf16)] * 2,
        in_specs=in_specs,
        out_specs=[pl.BlockSpec((many, CHUNK), lambda s: (0, second(s)))] * 2,
        scratch_shapes=[
            pltpu.VMEM((2 * many, units), f32),
            pltpu.VMEM((2 * many, units), f32),
            pltpu.VMEM((2 * many, units), bf16),
        ],
        compiler_params=pltpu.CompilerParams(vmem_limit_bytes=32 * 2**20),
        cost_estimate=pl.CostEstimate(
            flops=12 * many * width * units, bytes_accessed=6 * width * units + 8 * many * width, transcendentals=0
        ),
    )(*xs, *others, gate, up, down)


def past_kernel(scale, lengths, queries, keys, acc, top, total):
    request = pl.program_id(0)
    length = lengths[request]
    held = keys[0]
    steps = queries.shape[0]
    for t in range(steps):
        scores = dot(queries[t, 0], held, TN) * scale
        lane = lax.broadcasted_iota(jnp.int32, scores.shape, 1)
        visible = lane < length
        scores = jnp.where(visible, scores, masked_score)
        highest = jnp.max(scores, axis=-1, keepdims=True)
        weight = jnp.where(visible, jnp.exp(scores - highest), 0.0)
        acc[0, t] = dot(weight.astype(bf16), held[:LAT], NT)
        top[0, t] = highest
        total[0, t] = jnp.sum(weight, axis=-1, keepdims=True)


def past(lengths, queries, keys, scale, start):
    count, width, context = keys.shape
    steps, _, _, heads = queries.shape
    return pl.pallas_call(
        functools.partial(past_kernel, scale),
        grid_spec=pltpu.PrefetchScalarGridSpec(
            num_scalar_prefetch=1,
            grid=(count,),
            in_specs=[
                pl.BlockSpec((steps, 1, width, heads), lambda r, _: (0, r + start, 0, 0)),
                pl.BlockSpec((1, width, context), lambda r, _: (r, 0, 0)),
            ],
            out_specs=[
                pl.BlockSpec((1, steps, heads, LAT), lambda r, _: (r, 0, 0, 0)),
                pl.BlockSpec((1, steps, heads, 1), lambda r, _: (r, 0, 0, 0)),
                pl.BlockSpec((1, steps, heads, 1), lambda r, _: (r, 0, 0, 0)),
            ],
        ),
        out_shape=[
            jax.ShapeDtypeStruct((count, steps, heads, LAT), f32),
            jax.ShapeDtypeStruct((count, steps, heads, 1), f32),
            jax.ShapeDtypeStruct((count, steps, heads, 1), f32),
        ],
        compiler_params=pltpu.CompilerParams(vmem_limit_bytes=32 * 2**20),
        cost_estimate=pl.CostEstimate(
            flops=2 * count * steps * heads * context * (width + LAT),
            bytes_accessed=count * (2 * width * (context + steps * heads) + 4 * steps * heads * LAT),
            transcendentals=count * steps * heads * context,
        ),
    )(lengths, queries, keys)


def merge_kernel(scale, queries, new_keys, acc, top, total, out):
    steps, _, _, heads = queries.shape
    for t in range(steps):
        raw = dot(new_keys[0], queries[t, 0]) * scale
        pad = jnp.zeros((heads - raw.shape[0], heads), f32)
        own = jnp.concatenate([raw, pad], axis=0).T
        highest = top[0, t]
        columns = [own[:, k : k + 1] for k in range(t + 1)]
        peak = highest
        for column in columns:
            peak = jnp.maximum(peak, column)
        keep = jnp.exp(highest - peak)
        weights = [jnp.exp(column - peak) for column in columns]
        below = total[0, t] * keep + sum(weights)
        value = acc[0, t] * (keep / below)
        for k in range(t + 1):
            share = (weights[k] / below).astype(bf16).astype(f32)
            value = value + share * new_keys[0, k : k + 1, :LAT].astype(f32)
        out[0, t] = value.astype(bf16)


def merge(queries, new_keys, acc, top, total, scale, start):
    count, steps, heads, _ = acc.shape
    width = queries.shape[2]
    per = new_keys.shape[1]
    return pl.pallas_call(
        functools.partial(merge_kernel, scale),
        grid=(count,),
        in_specs=[
            pl.BlockSpec((steps, 1, width, heads), lambda r: (0, r + start, 0, 0)),
            pl.BlockSpec((1, per, width), lambda r: (r + start, 0, 0)),
            pl.BlockSpec((1, steps, heads, LAT), lambda r: (r, 0, 0, 0)),
            pl.BlockSpec((1, steps, heads, 1), lambda r: (r, 0, 0, 0)),
            pl.BlockSpec((1, steps, heads, 1), lambda r: (r, 0, 0, 0)),
        ],
        out_specs=pl.BlockSpec((1, steps, heads, LAT), lambda r: (r, 0, 0, 0)),
        out_shape=jax.ShapeDtypeStruct((count, steps, heads, LAT), bf16),
        compiler_params=pltpu.CompilerParams(vmem_limit_bytes=32 * 2**20),
    )(queries, new_keys, acc, top, total)


def project_kernel(core, hidden, own0, a0, b0, c0, own1, a1, b1, c1, gain, kv_own, kv_other, kv_gain, turns, layer, keys):
    rows = []
    for t, (own, a, b, c) in enumerate(((own0, a0, b0, c0), (own1, a1, b1, c1))):
        mixture = own[...] + a[...].astype(f32) + b[...].astype(f32) + c[...].astype(f32)
        rows.append(hidden[t].astype(f32) + mixture)
    both = jnp.concatenate(rows, axis=0).astype(bf16)
    layer[...] = both
    normed = rms_scale(both, gain[...]).astype(bf16)
    half = normed.shape[1] // 2
    swapped = core[0] > 0
    low, high = normed[:, :half].astype(f32), normed[:, half:].astype(f32)
    first = jnp.where(swapped, high, low).astype(bf16)
    second = jnp.where(swapped, low, high).astype(bf16)
    projected = dot(first, kv_own[...], NT) + dot(second, kv_other[...], NT)
    keys[:, :LAT] = rms_scale(projected[:, :LAT], kv_gain[...]).astype(bf16)
    rope = projected[:, LAT:]
    crossed = jnp.concatenate([-rope[:, ROPE // 2 :], rope[:, : ROPE // 2]], axis=1)
    keys[:, LAT:] = (rope * turns[0] + crossed * turns[1]).astype(bf16)


def spread_x(own):
    half = own.shape[0] // 2
    left = shift(own, "x", 1)
    right = shift(own, "x", 3)
    far_a = shift(left[:half], "x", 1)
    far_b = shift(right[half:], "x", 3)
    return [own, left, right, far_a, far_b]


def back_x(place, summed):
    half = SLOTS // 2
    own, left, right, far = [summed[i * SLOTS : (i + 1) * SLOTS] for i in range(SIDE)]
    got_a = shift(far[:half], "x", 1)
    got_b = shift(far[half:], "x", 3)
    from_left_b = shift(right[half:], "x", 1)
    from_right_a = shift(left[:half], "x", 3)
    from_left_a = shift(add(right[:half], got_a), "x", 1)
    from_right_b = shift(add(left[half:], got_b), "x", 3)
    outs = [((2 * PART, own.shape[1] // 2), bf16)] * SIDE
    return call(finish_kernel, outs, place, own, from_left_a, from_right_a, from_left_b, from_right_b)


def fresh_keys(fresh_cache, fresh_order):
    chips = ("y", "z", "x")
    count = lax.axis_size(chips)
    _, width, context = fresh_cache.shape
    tiles = width * context // 1024
    each = -(-tiles // count)

    def to_tiles(array):
        return array.reshape(width // 8, 8, context // 128, 128).swapaxes(1, 2).reshape(tiles, 8, 128)

    def from_tiles(array):
        return array.reshape(width // 8, context // 128, 8, 128).swapaxes(1, 2).reshape(width, context)

    cut = jnp.pad(to_tiles(fresh_cache[0]), ((0, each * count - tiles), (0, 0), (0, 0)))
    cut = cut.reshape(count, each * 8, 128)
    here = lax.all_to_all(cut, chips, split_axis=0, concat_axis=0, tiled=True)
    there = swap(here)
    core = lax.axis_index("c")
    wanted = lax.dynamic_slice_in_dim(fresh_order, core * count, count, 0)
    own_core = (wanted >= count) == (core > 0)
    index = wanted % count
    ordered = jnp.where(own_core[:, None, None], jnp.take(here, index, axis=0), jnp.take(there, index, axis=0))
    whole = lax.all_to_all(ordered, chips, split_axis=0, concat_axis=0, tiled=True)
    return from_tiles(whole.reshape(count * each, 8, 128)[:tiles])[None]


def shards(
    hidden_in,
    ffn_gain,
    attn_gain,
    kv_gain,
    expert_ids,
    route_weight,
    expert_gate,
    expert_up,
    expert_down,
    kv_down,
    resident_cache,
    fresh_cache,
    fresh_order,
    cache_len,
    queries,
):
    steps_count, local_rows, model_width = hidden_in.shape
    resident_rows = resident_cache.shape[0]
    score_scale = (NOPE + ROPE) ** (-0.5)
    core = lax.axis_index("c").astype(jnp.int32).reshape(1)

    shares = route_weight / jnp.sum(route_weight, axis=-1, keepdims=True) * route_scaling
    dense_share = jnp.sum(
        jnp.where(
            expert_ids[..., None] == jnp.arange(EXPERTS, dtype=jnp.int32), shares[..., None], 0.0
        ),
        axis=2,
    )
    high = dense_share.astype(bf16)
    low = (dense_share - high.astype(f32)).astype(bf16)
    normed = rms_scale(hidden_in, ffn_gain).astype(bf16)
    meta_rows = jnp.concatenate(
        [high, low, jnp.zeros((steps_count, local_rows, META - 2 * EXPERTS), bf16)], axis=2
    )
    payload = jnp.pad(
        jnp.concatenate([normed, meta_rows], axis=2), ((0, 0), (0, BLOCK - local_rows), (0, 0))
    )
    hidden_rows = jnp.pad(hidden_in, ((0, 0), (0, BLOCK - local_rows), (0, 0)))

    pick, fixed, lower = fold_tables()
    place = jnp.asarray(
        PLACE.reshape(2, SLOTS, SIDE, 2 * PART).transpose(0, 2, 1, 3), bf16
    )
    folded = ((2 * PART, model_width // 2), bf16)
    query_t = queries.swapaxes(2, 3)
    resident_t = resident_cache.swapaxes(1, 2)

    weights = []
    shared = []
    for step in range(steps_count):
        mine = payload[step]
        held = [mine, shift(mine, "y", 1), shift(mine, "y", 3), shift(mine, "y", 2)]
        *parts, weight = call(
            select_kernel, [folded] * SIDE + [((2, SIDE * 2 * PART, SIDE * BLOCK), f32)],
            pick, fixed, lower, *held,
        )
        weights.append(weight)
        parts = [parts[0], shift(parts[1], "z", 1), shift(parts[2], "z", 2), shift(parts[3], "z", 3)]
        (slots,) = call(assemble_kernel, [((SLOTS, model_width), bf16)], place, *parts)
        shared.append(spread_x(slots))

    fresh_t = fresh_keys(fresh_cache.swapaxes(1, 2), fresh_order)
    other_down = swap(kv_down.T)

    returned = []
    for step in range(steps_count):
        others = [swap(piece) for piece in shared[step]]
        kept, sent = experts(shared[step], others, expert_gate, expert_up, expert_down)
        returned.append(back_x(place, add(kept, swap(sent))))

    past_resident = past(cache_len, query_t, resident_t, score_scale, 0)
    past_fresh = past(cache_len[resident_rows:], query_t, fresh_t, score_scale, resident_rows)

    mixed = []
    for step in range(steps_count):
        parts = returned[step]
        parts = [parts[0], shift(parts[1], "z", 3), shift(parts[2], "z", 2), shift(parts[3], "z", 1)]
        rows = (BLOCK, model_width)
        own, one, two, three = call(
            combine_kernel, [(rows, f32), (rows, bf16), (rows, bf16), (rows, bf16)],
            fixed, weights[step], *parts,
        )
        mixed += [own, shift(one, "y", 3), shift(two, "y", 1), shift(three, "y", 2)]

    positions = jnp.pad(cache_len, (0, BLOCK - local_rows)).astype(f32)[None, :]
    positions = (positions + jnp.arange(steps_count).astype(f32)[:, None]).reshape(-1)
    halfway = ROPE // 2
    frequency = rope_base ** (-2.0 * jnp.arange(halfway).astype(f32) / ROPE)
    angles = positions[:, None] * frequency[None, :]
    turns = jnp.stack([jnp.tile(jnp.cos(angles), (1, 2)), jnp.tile(jnp.sin(angles), (1, 2))])
    many = steps_count * BLOCK
    layer, keys = call(
        project_kernel,
        [((many, model_width), bf16), ((many, LAT + ROPE), bf16)],
        core, hidden_rows, *mixed, attn_gain[None], kv_down.T, other_down, kv_gain[None], turns,
        smem=1, limit=40,
    )
    layer_out = layer.reshape(steps_count, BLOCK, model_width)[:, :local_rows]
    new_keys = jnp.pad(
        keys.reshape(steps_count, BLOCK, LAT + ROPE).swapaxes(0, 1), ((0, 0), (0, BLOCK - steps_count), (0, 0))
    )
    first = merge(query_t, new_keys, *past_resident, score_scale, 0)
    second = merge(query_t, new_keys, *past_fresh, score_scale, resident_rows)
    attended = jnp.concatenate([first, second], axis=0).swapaxes(0, 1)
    return layer_out, attended.reshape(steps_count, local_rows, -1)


def solution(mesh):
    grid = Mesh(mesh.devices.reshape(2, 4, 4, 4), ("c", "y", "z", "x"))
    every = ("c", "y", "z", "x")
    placed = (
        P(None, every, None),
        P(),
        P(),
        P(),
        P(None, every, None),
        P(None, every, None),
        P(every, None, None),
        P(every, None, None),
        P(every, None, None),
        P("c", None),
        P(every, None, None),
        P(every, None, None),
        P(),
        P(every),
        P(None, every, None, None),
    )
    return jax.shard_map(
        shards,
        mesh=grid,
        in_specs=placed,
        out_specs=(P(None, every, None), P(None, every, None)),
        check_vma=False,
    )
```

```python
import functools

import jax
import jax.numpy as jnp
import numpy as np
from jax import lax
from jax.experimental import pallas as pl
from jax.experimental.pallas import tpu as pltpu
from jax.sharding import Mesh, PartitionSpec as P

LAT = 512
ROPE = 64
NOPE = 128
EXPERTS = 16
CAP = 3
BLOCK = 8
META = 128
SIDE = 4
PART = SIDE * CAP
SLOTS = SIDE * PART


epsilon = 1e-06
route_scaling = 2.5
rope_base = 10000.0
masked_score = -1e30
f32 = jnp.float32
bf16 = jnp.bfloat16
NT = (((1,), (1,)), ((), ()))
TN = (((0,), (0,)), ((), ()))


def rms_scale(values, gain_vector):
    values = values.astype(f32)
    return (
        values
        * lax.rsqrt(jnp.mean(values * values, axis=-1, keepdims=True) + epsilon)
        * gain_vector
    )


def shift(values, axis, by):
    size = lax.axis_size(axis)
    return lax.ppermute(values, axis, [(i, (i + by) % size) for i in range(size)])


def add(*terms):
    return sum(term.astype(f32) for term in terms).astype(bf16)


def swap(values):
    return shift(values, "c", 1)


def dot(a, b, dims=(((1,), (0,)), ((), ()))):
    return lax.dot_general(a, b, dims, preferred_element_type=f32)


def call(kernel, outs, *args, smem=0, flops=0, limit=32, scratch=()):
    specs = [pl.BlockSpec(memory_space=pltpu.SMEM)] * smem
    specs += [pl.BlockSpec(memory_space=pltpu.VMEM)] * (len(args) - smem)
    moved = sum(a.size * a.dtype.itemsize for a in args)
    return pl.pallas_call(
        kernel,
        out_shape=[jax.ShapeDtypeStruct(shape, dtype) for shape, dtype in outs],
        in_specs=specs,
        out_specs=[pl.BlockSpec(memory_space=pltpu.VMEM)] * len(outs),
        scratch_shapes=list(scratch),
        compiler_params=pltpu.CompilerParams(vmem_limit_bytes=limit * 2**20),
        cost_estimate=pl.CostEstimate(flops=flops, bytes_accessed=moved, transcendentals=0),
    )(*args)


FOLD_ROW = np.arange(SIDE * 2 * PART)
FOLD_BLOCK = FOLD_ROW // (2 * PART)
FOLD_HALF = FOLD_ROW % (2 * PART) // PART
FOLD_SLOT = FOLD_ROW % PART
PLACE = np.stack(
    [
        (np.arange(SLOTS)[:, None] == (FOLD_BLOCK * PART + FOLD_SLOT)[None, :]) & (FOLD_HALF == half)[None, :]
        for half in (0, 1)
    ]
).astype(np.float32)


def fold_tables():
    expert = lax.axis_index("y") * SIDE + (lax.axis_index("z") + FOLD_BLOCK) % SIDE
    lanes = jnp.arange(META)[None, :]
    pick = jnp.stack([expert[:, None] == lanes, expert[:, None] + EXPERTS == lanes]).astype(bf16)
    columns = np.arange(SIDE * BLOCK)
    same = ((FOLD_SLOT // CAP)[:, None] == (columns // BLOCK)[None, :]).astype(np.float32)
    turn = np.broadcast_to((FOLD_SLOT % CAP)[:, None], same.shape).astype(np.float32)
    half = np.broadcast_to(FOLD_HALF[:, None], same.shape).astype(np.float32)
    lower = (columns[None, :] < columns[:, None]) & (
        columns[None, :] // BLOCK == columns[:, None] // BLOCK
    )
    return pick, jnp.asarray(np.stack([same, turn, half])), jnp.asarray(lower.astype(np.float32), bf16)


def select_kernel(pick, fixed, lower, b0, b1, b2, b3, o0, o1, o2, o3, weights):
    held = jnp.concatenate([b[...].astype(f32) for b in (b0, b1, b2, b3)], axis=0)
    width = held.shape[1] - META
    half = width // 2
    meta = held[:, width:]
    lane = lax.broadcasted_iota(jnp.int32, meta.shape, 1)
    named = jnp.where((meta > 0) & (lane < EXPERTS), 1.0, 0.0).astype(bf16)
    meta = meta.astype(bf16)
    before = dot(lower[...], named).astype(bf16)
    here = (dot(pick[0], named, NT) > 0.5) & (dot(pick[0], before, NT) == fixed[1]) & (fixed[0] > 0.5)
    second = fixed[2] > 0.5
    sel = jnp.where(here, 1.0, 0.0)
    low_half = jnp.where(second, 0.0, sel).astype(bf16)
    high_half = jnp.where(second, sel, 0.0).astype(bf16)
    weights[0] = jnp.where(here, dot(pick[0], meta, NT), 0.0)
    weights[1] = jnp.where(here, dot(pick[1], meta, NT), 0.0)
    slots = dot(low_half, held[:, :half].astype(bf16)) + dot(high_half, held[:, half:width].astype(bf16))
    for i, o in enumerate((o0, o1, o2, o3)):
        o[...] = slots[i * 2 * PART : (i + 1) * 2 * PART].astype(bf16)


def assemble_kernel(place, f0, f1, f2, f3, out):
    half = f0.shape[1]
    for h in range(2):
        total = 0.0
        for i, f in enumerate((f0, f1, f2, f3)):
            total = total + dot(place[h, i], f[...])
        out[:, h * half : (h + 1) * half] = total.astype(bf16)


def finish_kernel(place, own, plus, minus, la, rb, o0, o1, o2, o3):
    quarter = la.shape[0]
    half = own.shape[1] // 2
    total = [0.0] * SIDE
    for h in range(2):
        cols = slice(h * half, (h + 1) * half)
        mine = own[:, cols].astype(f32)
        first = mine[:quarter] + la[:, cols].astype(f32) + minus[:, cols].astype(f32)[:quarter]
        second = mine[quarter:] + plus[:, cols].astype(f32)[:quarter] + rb[:, cols].astype(f32)
        summed = jnp.concatenate([first, second], axis=0).astype(bf16)
        for i in range(SIDE):
            total[i] = total[i] + dot(place[h, i], summed, TN)
    for i, o in enumerate((o0, o1, o2, o3)):
        o[...] = total[i].astype(bf16)


def pair_kernel(kept, got, own, lb, ra, plus, minus):
    total = kept[...].astype(f32) + got[...].astype(f32)
    quarter = lb.shape[0]
    piece = [total[i * quarter : (i + 1) * quarter] for i in range(8)]
    own[...] = total[: 2 * quarter].astype(bf16)
    lb[...] = piece[2].astype(bf16)
    ra[...] = piece[3].astype(bf16)
    plus[...] = jnp.concatenate([piece[4], piece[6]], axis=0).astype(bf16)
    minus[...] = jnp.concatenate([piece[5], piece[7]], axis=0).astype(bf16)


def pair_sums(kept, got):
    many, width = kept.shape
    rows = (many // 4, many // 8, many // 8, many // 4, many // 4)
    chunk = 1024
    return pl.pallas_call(
        pair_kernel,
        grid=(width // chunk,),
        out_shape=[jax.ShapeDtypeStruct((r, width), bf16) for r in rows],
        in_specs=[pl.BlockSpec((many, chunk), lambda s: (0, s))] * 2,
        out_specs=[pl.BlockSpec((r, chunk), lambda s: (0, s)) for r in rows],
        compiler_params=pltpu.CompilerParams(vmem_limit_bytes=24 * 2**20),
        cost_estimate=pl.CostEstimate(flops=many * width, bytes_accessed=6 * many * width, transcendentals=0),
    )(kept, got)


def combine_kernel(fixed, weights, f0, f1, f2, f3, own, o1, o2, o3):
    half = f0.shape[1]
    many = 2 * PART
    for h in range(2):
        cols = slice(h * half, (h + 1) * half)
        total = 0.0
        for i, f in enumerate((f0, f1, f2, f3)):
            rows = slice(i * many, (i + 1) * many)
            mine = (fixed[2, rows] > 0.5) if h else (fixed[2, rows] < 0.5)
            for k in range(2):
                share = jnp.where(mine, weights[k, rows], 0.0).astype(bf16)
                total = total + dot(share, f[...], TN)
        own[:, cols] = total[:BLOCK]
        for i, o in enumerate((o1, o2, o3)):
            o[:, cols] = total[(i + 1) * BLOCK : (i + 2) * BLOCK].astype(bf16)


CHUNK = 1024


def expert_kernel(pieces, chunks, *refs):
    xs, others = refs[:pieces], refs[pieces : 2 * pieces]
    gate, up, down, mine, theirs, rows, gate_sum, up_sum, active = refs[2 * pieces :]
    step = pl.program_id(0)

    @pl.when(step == 0)
    def _():
        gate_sum[...] = jnp.zeros_like(gate_sum)
        up_sum[...] = jnp.zeros_like(up_sum)

    @pl.when(step < chunks)
    def _():
        at = 0
        for x in xs + others:
            rows[at : at + x.shape[0]] = x[...]
            at += x.shape[0]
        gate_sum[...] += dot(rows[...], gate[0])
        up_sum[...] += dot(rows[...], up[0])

    @pl.when(step == chunks)
    def _():
        value = gate_sum[...]
        active[...] = (value / (1.0 + jnp.exp(-value)) * up_sum[...]).astype(bf16)

    @pl.when(step >= chunks)
    def _():
        many = mine.shape[0]
        result = dot(active[...], down[0])
        mine[...] = result[:many].astype(bf16)
        theirs[...] = result[many:].astype(bf16)


def experts(xs, others, gate, up, down):
    pieces = len(xs)
    many = sum(x.shape[0] for x in xs)
    width, units = gate.shape[1:]
    chunks = width // CHUNK

    def first(s):
        return jnp.minimum(s, chunks - 1)

    def second(s):
        return jnp.maximum(s - chunks, 0)

    in_specs = [pl.BlockSpec((x.shape[0], CHUNK), lambda s: (0, first(s))) for x in xs + others]
    in_specs += [pl.BlockSpec((1, CHUNK, units), lambda s: (0, first(s), 0))] * 2
    in_specs += [pl.BlockSpec((1, units, CHUNK), lambda s: (0, 0, second(s)))]
    return pl.pallas_call(
        functools.partial(expert_kernel, pieces, chunks),
        grid=(2 * chunks,),
        out_shape=[jax.ShapeDtypeStruct((many, width), bf16)] * 2,
        in_specs=in_specs,
        out_specs=[pl.BlockSpec((many, CHUNK), lambda s: (0, second(s)))] * 2,
        scratch_shapes=[
            pltpu.VMEM((2 * many, CHUNK), bf16),
            pltpu.VMEM((2 * many, units), f32),
            pltpu.VMEM((2 * many, units), f32),
            pltpu.VMEM((2 * many, units), bf16),
        ],
        compiler_params=pltpu.CompilerParams(vmem_limit_bytes=32 * 2**20),
        cost_estimate=pl.CostEstimate(
            flops=12 * many * width * units, bytes_accessed=6 * width * units + 8 * many * width, transcendentals=0
        ),
    )(*xs, *others, gate, up, down)


def past_kernel(scale, lengths, queries, keys, acc, top, total):
    request = pl.program_id(0)
    length = lengths[request]
    held = keys[0]
    steps = queries.shape[0]
    for t in range(steps):
        scores = dot(queries[t, 0], held, TN) * scale
        lane = lax.broadcasted_iota(jnp.int32, scores.shape, 1)
        visible = lane < length
        scores = jnp.where(visible, scores, masked_score)
        highest = jnp.max(scores, axis=-1, keepdims=True)
        weight = jnp.where(visible, jnp.exp(scores - highest), 0.0)
        acc[0, t] = dot(weight.astype(bf16), held[:LAT], NT)
        top[0, t] = highest
        total[0, t] = jnp.sum(weight, axis=-1, keepdims=True)


def past(lengths, queries, keys, scale, start):
    count, width, context = keys.shape
    steps, _, _, heads = queries.shape
    return pl.pallas_call(
        functools.partial(past_kernel, scale),
        grid_spec=pltpu.PrefetchScalarGridSpec(
            num_scalar_prefetch=1,
            grid=(count,),
            in_specs=[
                pl.BlockSpec((steps, 1, width, heads), lambda r, _: (0, r + start, 0, 0)),
                pl.BlockSpec((1, width, context), lambda r, _: (r, 0, 0)),
            ],
            out_specs=[
                pl.BlockSpec((1, steps, heads, LAT), lambda r, _: (r, 0, 0, 0)),
                pl.BlockSpec((1, steps, heads, 1), lambda r, _: (r, 0, 0, 0)),
                pl.BlockSpec((1, steps, heads, 1), lambda r, _: (r, 0, 0, 0)),
            ],
        ),
        out_shape=[
            jax.ShapeDtypeStruct((count, steps, heads, LAT), f32),
            jax.ShapeDtypeStruct((count, steps, heads, 1), f32),
            jax.ShapeDtypeStruct((count, steps, heads, 1), f32),
        ],
        compiler_params=pltpu.CompilerParams(vmem_limit_bytes=32 * 2**20),
        cost_estimate=pl.CostEstimate(
            flops=2 * count * steps * heads * context * (width + LAT),
            bytes_accessed=count * (2 * width * (context + steps * heads) + 4 * steps * heads * LAT),
            transcendentals=count * steps * heads * context,
        ),
    )(lengths, queries, keys)


def merge_kernel(scale, count, queries, new_keys, acc, top, total, last_acc, last_top, last_total, out, rows):
    steps, _, _, heads = queries.shape
    lanes = LAT // 128
    request = pl.program_id(0)

    def one(acc, top, total):
        for t in range(steps):
            raw = dot(new_keys[0], queries[t, 0]) * scale
            pad = jnp.zeros((heads - raw.shape[0], heads), f32)
            own = jnp.concatenate([raw, pad], axis=0).T
            highest = top[0, t]
            columns = [own[:, k : k + 1] for k in range(t + 1)]
            peak = highest
            for column in columns:
                peak = jnp.maximum(peak, column)
            keep = jnp.exp(highest - peak)
            weights = [jnp.exp(column - peak) for column in columns]
            below = total[0, t] * keep + sum(weights)
            value = acc[0, t] * (keep / below)
            for k in range(t + 1):
                share = (weights[k] / below).astype(bf16).astype(f32)
                value = value + share * new_keys[0, k : k + 1, :LAT].astype(f32)
            for j in range(lanes):
                rows[pl.ds(j * steps + t, heads, stride=lanes * steps), :] = value[:, j * 128 : (j + 1) * 128]
        out[0] = rows[...].astype(bf16)

    @pl.when(request < count)
    def _():
        one(acc, top, total)

    @pl.when(request >= count)
    def _():
        one(last_acc, last_top, last_total)


def merge(queries, new_keys, first, last, scale):
    count, steps, heads, _ = first[0].shape
    rows = count + last[0].shape[0]
    width = queries.shape[2]
    per = new_keys.shape[1]
    tall = heads * steps * LAT // 128

    def early(r):
        return (jnp.minimum(r, count - 1), 0, 0, 0)

    def late(r):
        return (jnp.maximum(r - count, 0), 0, 0, 0)

    parts = [
        pl.BlockSpec((1, steps, heads, size), where) for where in (early, late) for size in (LAT, 1, 1)
    ]
    return pl.pallas_call(
        functools.partial(merge_kernel, scale, count),
        grid=(rows,),
        in_specs=[
            pl.BlockSpec((steps, 1, width, heads), lambda r: (0, r, 0, 0)),
            pl.BlockSpec((1, per, width), lambda r: (r, 0, 0)),
            *parts,
        ],
        out_specs=pl.BlockSpec((1, tall, 128), lambda r: (r, 0, 0)),
        out_shape=jax.ShapeDtypeStruct((rows, tall, 128), bf16),
        scratch_shapes=[pltpu.VMEM((tall, 128), f32)],
        compiler_params=pltpu.CompilerParams(vmem_limit_bytes=32 * 2**20),
    )(queries, new_keys, *first, *last)


def project_kernel(core, hidden, own0, a0, b0, c0, own1, a1, b1, c1, gain, kv_own, kv_other, kv_gain, turns, layer, keys, stage):
    rows = []
    for t, (own, a, b, c) in enumerate(((own0, a0, b0, c0), (own1, a1, b1, c1))):
        mixture = own[...] + a[...].astype(f32) + b[...].astype(f32) + c[...].astype(f32)
        rows.append(hidden[t].astype(f32) + mixture)
    both = jnp.concatenate(rows, axis=0).astype(bf16)
    many, width = both.shape
    wide = both.astype(f32)
    for k in range(width // 128):
        for t in range(2):
            stage[pl.ds(2 * k + t, BLOCK, stride=width // 64), :] = wide[
                t * BLOCK : (t + 1) * BLOCK, k * 128 : (k + 1) * 128
            ]
    layer[...] = stage[...].astype(bf16)
    normed = rms_scale(both, gain[...]).astype(bf16)
    half = normed.shape[1] // 2
    swapped = core[0] > 0
    low, high = normed[:, :half].astype(f32), normed[:, half:].astype(f32)
    first = jnp.where(swapped, high, low).astype(bf16)
    second = jnp.where(swapped, low, high).astype(bf16)
    projected = (dot(kv_own[...], first, NT) + dot(kv_other[...], second, NT)).T
    keys[:, :LAT] = rms_scale(projected[:, :LAT], kv_gain[...]).astype(bf16)
    rope = projected[:, LAT:]
    crossed = jnp.concatenate([-rope[:, ROPE // 2 :], rope[:, : ROPE // 2]], axis=1)
    keys[:, LAT:] = (rope * turns[0] + crossed * turns[1]).astype(bf16)


def hold(*values):
    return lax.optimization_barrier(values)


def steps_y(mine):
    return [mine, shift(mine, "y", 1), shift(mine, "y", 3), shift(mine, "y", 2)]


def steps_z(parts, sign):
    return [parts[0]] + [shift(parts[i], "z", sign * i % SIDE) for i in (1, 2, 3)]


def near_rows(own, left, right):
    half = own.shape[0] // 2
    return jnp.concatenate([own, left[half:], right[:half], right[half:], left[:half]], axis=0)


CHIPS = ("y", "z", "x")


def fresh_cut(fresh_t):
    width, context = fresh_t.shape
    count = lax.axis_size(CHIPS)
    tiles = width * context // 1024
    each = -(-tiles // count)
    cut = fresh_t.reshape(width // 8, 8, context // 128, 128).swapaxes(1, 2).reshape(tiles, 8, 128)
    cut = jnp.pad(cut, ((0, each * count - tiles), (0, 0), (0, 0)))
    return cut.reshape(count, each * 8, 128)


def fresh_join(whole, width, context):
    tiles = width * context // 1024
    whole = whole.reshape(-1, 8, 128)[:tiles].reshape(width // 8, context // 128, 8, 128)
    return whole.swapaxes(1, 2).reshape(width, context)


def fresh_sort(here, there, fresh_order):
    core = lax.axis_index("c")
    count = here.shape[0]
    wanted = lax.dynamic_slice_in_dim(fresh_order, core * count, count, 0)
    own_core = (wanted >= count) == (core > 0)
    index = wanted % count
    return jnp.where(
        own_core[:, None, None], jnp.take(here, index, axis=0), jnp.take(there, index, axis=0)
    )


def to_chips(pieces):
    return lax.all_to_all(pieces, CHIPS, split_axis=0, concat_axis=0, tiled=True)


def shards(
    hidden_in,
    ffn_gain,
    attn_gain,
    kv_gain,
    expert_ids,
    route_weight,
    expert_gate,
    expert_up,
    expert_down,
    kv_down,
    resident_cache,
    fresh_cache,
    fresh_order,
    cache_len,
    queries,
):
    steps_count, local_rows, model_width = hidden_in.shape
    resident_rows = resident_cache.shape[0]
    score_scale = (NOPE + ROPE) ** (-0.5)
    core = lax.axis_index("c").astype(jnp.int32).reshape(1)

    shares = route_weight / jnp.sum(route_weight, axis=-1, keepdims=True) * route_scaling
    dense_share = jnp.sum(
        jnp.where(
            expert_ids[..., None] == jnp.arange(EXPERTS, dtype=jnp.int32), shares[..., None], 0.0
        ),
        axis=2,
    )
    high = dense_share.astype(bf16)
    low = (dense_share - high.astype(f32)).astype(bf16)
    normed = rms_scale(hidden_in, ffn_gain).astype(bf16)
    meta_rows = jnp.concatenate(
        [high, low, jnp.zeros((steps_count, local_rows, META - 2 * EXPERTS), bf16)], axis=2
    )
    payload = jnp.pad(
        jnp.concatenate([normed, meta_rows], axis=2), ((0, 0), (0, BLOCK - local_rows), (0, 0))
    )
    hidden_rows = jnp.pad(hidden_in, ((0, 0), (0, BLOCK - local_rows), (0, 0)))

    pick, fixed, lower = fold_tables()
    place = jnp.asarray(
        PLACE.reshape(2, SLOTS, SIDE, 2 * PART).transpose(0, 2, 1, 3), bf16
    )
    folded = ((2 * PART, model_width // 2), bf16)
    query_t = queries.swapaxes(2, 3)
    resident_t = resident_cache.swapaxes(1, 2)

    slot_half = SLOTS // 2
    rows = (BLOCK, model_width)

    def select(held):
        *parts, weight = call(
            select_kernel, [folded] * SIDE + [((2, SIDE * 2 * PART, SIDE * BLOCK), f32)],
            pick, fixed, lower, *held,
        )
        return parts, weight

    def assemble(parts):
        return call(assemble_kernel, [((SLOTS, model_width), bf16)], place, *parts)[0]

    def combine(weight, parts):
        return call(
            combine_kernel, [(rows, f32), (rows, bf16), (rows, bf16), (rows, bf16)],
            fixed, weight, *parts,
        )

    def back_y(own, one, two, three):
        return [own, shift(one, "y", 3), shift(two, "y", 1), shift(three, "y", 2)]

    def finish(own, plus, minus, la, rb):
        return call(finish_kernel, [folded] * SIDE, place, own, plus, minus, la, rb)

    def run_experts(near, near_swapped, far, far_swapped):
        return experts([near, far], [near_swapped, far_swapped], expert_gate, expert_up, expert_down)

    def meet(ra, lb, plus, minus):
        return add(ra, plus[slot_half:]), add(lb, minus[slot_half:])

    held = steps_y(payload[0])
    pieces = fresh_cut(fresh_cache[0].T)
    held, payload1, pieces = hold(held, payload[1], pieces)
    parts, weight0 = select(held)
    parts = steps_z(parts, 1)
    held = steps_y(payload1)
    here = to_chips(pieces)
    parts, held, weight0, here = hold(parts, held, weight0, here)
    own0 = assemble(parts)
    left0, right0 = shift(own0, "x", 1), shift(own0, "x", 3)
    parts, weight1 = select(held)
    parts = steps_z(parts, 1)
    there = swap(here)
    past_resident = past(cache_len, query_t, resident_t, score_scale, 0)
    own0, left0, right0, parts, weight1, here, there, past_resident = hold(
        own0, left0, right0, parts, weight1, here, there, past_resident
    )
    far_a, far_b = shift(left0[:slot_half], "x", 1), shift(right0[slot_half:], "x", 3)
    near0 = near_rows(own0, left0, right0)
    near0_swapped = swap(near0)
    own1 = assemble(parts)
    sorted_pieces = fresh_sort(here, there, fresh_order)
    far_a, far_b, near0, near0_swapped, own1, sorted_pieces = hold(
        far_a, far_b, near0, near0_swapped, own1, sorted_pieces
    )
    left1, right1 = shift(own1, "x", 1), shift(own1, "x", 3)
    far0 = jnp.concatenate([far_a, far_b], axis=0)
    kept0, sent0 = run_experts(near0, near0_swapped, far0, swap(far0))
    left1, right1, kept0, sent0, sorted_pieces = hold(left1, right1, kept0, sent0, sorted_pieces)
    far_a, far_b = shift(left1[:slot_half], "x", 1), shift(right1[slot_half:], "x", 3)
    got0 = swap(sent0)
    near1 = near_rows(own1, left1, right1)
    near1_swapped = swap(near1)
    own0, lb0, ra0, plus0, minus0 = pair_sums(kept0, got0)
    far_a, far_b, near1, near1_swapped, own0, lb0, ra0, plus0, minus0, sorted_pieces = hold(
        far_a, far_b, near1, near1_swapped, own0, lb0, ra0, plus0, minus0, sorted_pieces
    )
    plus0, minus0 = shift(plus0, "x", 1), shift(minus0, "x", 3)
    far1 = jnp.concatenate([far_a, far_b], axis=0)
    kept1, sent1 = run_experts(near1, near1_swapped, far1, swap(far1))
    plus0, minus0, kept1, sent1, sorted_pieces = hold(plus0, minus0, kept1, sent1, sorted_pieces)
    ra0, lb0 = meet(ra0, lb0, plus0, minus0)
    la0, rb0 = shift(ra0, "x", 1), shift(lb0, "x", 3)
    got1 = swap(sent1)
    own1, lb1, ra1, plus1, minus1 = pair_sums(kept1, got1)
    la0, rb0, own1, lb1, ra1, plus1, minus1, sorted_pieces = hold(
        la0, rb0, own1, lb1, ra1, plus1, minus1, sorted_pieces
    )
    plus1, minus1 = shift(plus1, "x", 1), shift(minus1, "x", 3)
    parts = steps_z(finish(own0, plus0, minus0, la0, rb0), -1)
    whole = to_chips(sorted_pieces)
    plus1, minus1, parts, whole = hold(plus1, minus1, parts, whole)
    ra1, lb1 = meet(ra1, lb1, plus1, minus1)
    la1, rb1 = shift(ra1, "x", 1), shift(lb1, "x", 3)
    mixed0 = back_y(*combine(weight0, parts))
    fresh_t = fresh_join(whole, LAT + ROPE, fresh_cache.shape[1])[None]
    past_fresh = past(cache_len[resident_rows:], query_t, fresh_t, score_scale, resident_rows)
    la1, rb1, mixed0, past_fresh = hold(la1, rb1, mixed0, past_fresh)
    parts = steps_z(finish(own1, plus1, minus1, la1, rb1), -1)
    other_down = swap(kv_down.T)
    mixed = mixed0 + back_y(*combine(weight1, parts))

    positions = jnp.pad(cache_len, (0, BLOCK - local_rows)).astype(f32)[None, :]
    positions = (positions + jnp.arange(steps_count).astype(f32)[:, None]).reshape(-1)
    halfway = ROPE // 2
    frequency = rope_base ** (-2.0 * jnp.arange(halfway).astype(f32) / ROPE)
    angles = positions[:, None] * frequency[None, :]
    turns = jnp.stack([jnp.tile(jnp.cos(angles), (1, 2)), jnp.tile(jnp.sin(angles), (1, 2))])
    many = steps_count * BLOCK
    layer, keys = call(
        project_kernel,
        [((many * model_width // 128, 128), bf16), ((many, LAT + ROPE), bf16)],
        core, hidden_rows, *mixed, attn_gain[None], kv_down.T, other_down, kv_gain[None], turns,
        smem=1, limit=40, scratch=[pltpu.VMEM((many * model_width // 128, 128), f32)],
    )
    tall = model_width // 128
    layer = layer[: local_rows * steps_count * tall].reshape(local_rows, tall, steps_count, 128)
    layer_out = layer.transpose(2, 0, 1, 3).reshape(steps_count, local_rows, model_width)
    new_keys = jnp.pad(
        keys.reshape(steps_count, BLOCK, LAT + ROPE).swapaxes(0, 1), ((0, 0), (0, BLOCK - steps_count), (0, 0))
    )
    attended = merge(query_t, new_keys, past_resident, past_fresh, score_scale)
    attended = attended.reshape(local_rows, -1, steps_count, 128).transpose(2, 0, 1, 3)
    return layer_out, attended.reshape(steps_count, local_rows, -1)


def solution(mesh):
    grid = Mesh(mesh.devices.reshape(2, 4, 4, 4), ("c", "y", "z", "x"))
    every = ("c", "y", "z", "x")
    placed = (
        P(None, every, None),
        P(),
        P(),
        P(),
        P(None, every, None),
        P(None, every, None),
        P(every, None, None),
        P(every, None, None),
        P(every, None, None),
        P("c", None),
        P(every, None, None),
        P(every, None, None),
        P(),
        P(every),
        P(None, every, None, None),
    )
    return jax.shard_map(
        shards,
        mesh=grid,
        in_specs=placed,
        out_specs=(P(None, every, None), P(None, every, None)),
        check_vma=False,
    )
```

```python
import functools

import jax
import jax.numpy as jnp
import numpy as np
from jax import lax
from jax.experimental import pallas as pl
from jax.experimental.pallas import tpu as pltpu
from jax.sharding import Mesh, PartitionSpec as P

LAT = 512
ROPE = 64
NOPE = 128
EXPERTS = 16
CAP = 3
BLOCK = 8
META = 128
SIDE = 4
PART = SIDE * CAP
SLOTS = SIDE * PART


epsilon = 1e-06
route_scaling = 2.5
rope_base = 10000.0
masked_score = -1e30
f32 = jnp.float32
bf16 = jnp.bfloat16
NT = (((1,), (1,)), ((), ()))
TN = (((0,), (0,)), ((), ()))


def rms_scale(values, gain_vector):
    values = values.astype(f32)
    return (
        values
        * lax.rsqrt(jnp.mean(values * values, axis=-1, keepdims=True) + epsilon)
        * gain_vector
    )


def shift(values, axis, by):
    size = lax.axis_size(axis)
    return lax.ppermute(values, axis, [(i, (i + by) % size) for i in range(size)])


def add(*terms):
    return sum(term.astype(f32) for term in terms).astype(bf16)


def swap(values):
    return shift(values, "c", 1)


def dot(a, b, dims=(((1,), (0,)), ((), ()))):
    return lax.dot_general(a, b, dims, preferred_element_type=f32)


def call(kernel, outs, *args, smem=0, flops=0, limit=12, scratch=()):
    specs = [pl.BlockSpec(memory_space=pltpu.SMEM)] * smem
    specs += [pl.BlockSpec(memory_space=pltpu.VMEM)] * (len(args) - smem)
    moved = sum(a.size * a.dtype.itemsize for a in args)
    return pl.pallas_call(
        kernel,
        out_shape=[jax.ShapeDtypeStruct(shape, dtype) for shape, dtype in outs],
        in_specs=specs,
        out_specs=[pl.BlockSpec(memory_space=pltpu.VMEM)] * len(outs),
        scratch_shapes=list(scratch),
        compiler_params=pltpu.CompilerParams(vmem_limit_bytes=limit * 2**20),
        cost_estimate=pl.CostEstimate(flops=flops, bytes_accessed=moved, transcendentals=0),
    )(*args)


def row_of(shape, dim):
    return lax.broadcasted_iota(jnp.int32, shape, dim)


def digits(value, base, count):
    high = sum(jnp.where(value >= base * i, 1, 0) for i in range(1, count))
    return high, value - base * high


def placed(half, block):
    slot = row_of((SLOTS, 2 * PART), 0) - block * PART
    return jnp.where((row_of((SLOTS, 2 * PART), 1) - half * PART == slot) & (slot >= 0) & (slot < PART), 1.0, 0.0).astype(bf16)


def prepare_kernel(ids, route, hidden, gain, out, plain):
    count, steps, width = hidden.shape
    both = hidden[...].astype(f32)
    blank = jnp.zeros((META - EXPERTS, META), f32)
    spare = jnp.zeros((BLOCK - count, width), f32)
    normed, metas, held = [], [], []
    for t in range(steps):
        values = both[:, t, :]
        held += [values, spare]
        normed += [rms_scale(values, gain[...]), spare]
        share = route[t] / jnp.sum(route[t], axis=0, keepdims=True) * route_scaling
        expert = lax.broadcasted_iota(jnp.int32, (EXPERTS, count), 0)
        dense = jnp.zeros((EXPERTS, count), f32)
        for k in range(share.shape[0]):
            dense = dense + jnp.where(ids[t, k : k + 1] == expert, share[k : k + 1], 0.0)
        dense = jnp.concatenate([dense, jnp.zeros((EXPERTS, META - count), f32)], axis=1)
        dense = jnp.concatenate([dense, blank], axis=0).T
        high = dense.astype(bf16)
        low = (dense - high.astype(f32))[:, :EXPERTS].astype(bf16).astype(f32)
        meta = jnp.concatenate([high.astype(f32)[:, :EXPERTS], low, blank.T[:, EXPERTS:]], axis=1)
        metas.append(meta[:BLOCK])
    plain[...] = jnp.concatenate(held, axis=0).astype(bf16)
    out[:, :width] = jnp.concatenate(normed, axis=0).astype(bf16)
    out[:, width:] = jnp.concatenate(metas, axis=0).astype(bf16)


def select_kernel(step, place, b0, b1, b2, b3, o0, o1, o2, o3, weights):
    mine = slice(step * BLOCK, (step + 1) * BLOCK)
    held = jnp.concatenate([b[...].astype(f32)[mine] for b in (b0, b1, b2, b3)], axis=0)
    width = held.shape[1] - META
    half = width // 2
    many = SIDE * 2 * PART
    count = SIDE * BLOCK
    meta = held[:, width:]
    named = jnp.where((meta > 0) & (row_of(meta.shape, 1) < EXPERTS), 1.0, 0.0).astype(bf16)
    meta = meta.astype(bf16)
    later, sooner = row_of((count, count), 0), row_of((count, count), 1)
    same = digits(later, BLOCK, SIDE)[0] == digits(sooner, BLOCK, SIDE)[0]
    before = dot(jnp.where(same & (sooner < later), 1.0, 0.0).astype(bf16), named).astype(bf16)
    block, rest = digits(row_of((many, META), 0), 2 * PART, SIDE)
    z = place[1] + block
    expert = place[0] * SIDE + jnp.where(z >= SIDE, z - SIDE, z)
    lane = row_of((many, META), 1)
    pick_high = jnp.where(lane == expert, 1.0, 0.0).astype(bf16)
    pick_low = jnp.where(lane == expert + EXPERTS, 1.0, 0.0).astype(bf16)
    _, rest = digits(row_of((many, count), 0), 2 * PART, SIDE)
    second, slot = digits(rest, PART, 2)
    source, turn = digits(slot, CAP, SIDE)
    owner = digits(row_of((many, count), 1), BLOCK, SIDE)[0]
    here = (
        (dot(pick_high, named, NT) > 0.5)
        & (dot(pick_high, before, NT) == turn.astype(f32))
        & (source == owner)
    )
    sel = jnp.where(here, 1.0, 0.0)
    low_half = jnp.where(second > 0, 0.0, sel).astype(bf16)
    high_half = jnp.where(second > 0, sel, 0.0).astype(bf16)
    weights[0] = jnp.where(here, dot(pick_high, meta, NT), 0.0)
    weights[1] = jnp.where(here, dot(pick_low, meta, NT), 0.0)
    slots = dot(low_half, held[:, :half].astype(bf16)) + dot(high_half, held[:, half:width].astype(bf16))
    for i, o in enumerate((o0, o1, o2, o3)):
        o[...] = slots[i * 2 * PART : (i + 1) * 2 * PART].astype(bf16)


def assemble_kernel(f0, f1, f2, f3, out):
    half = f0.shape[1]
    for h in range(2):
        total = 0.0
        for i, f in enumerate((f0, f1, f2, f3)):
            total = total + dot(placed(h, i), f[...])
        out[:, h * half : (h + 1) * half] = total.astype(bf16)


def finish_kernel(own, plus, minus, la, rb, o0, o1, o2, o3):
    quarter = la.shape[0]
    half = own.shape[1] // 2
    total = [0.0] * SIDE
    for h in range(2):
        cols = slice(h * half, (h + 1) * half)
        mine = own[:, cols].astype(f32)
        first = mine[:quarter] + la[:, cols].astype(f32) + minus[:, cols].astype(f32)[:quarter]
        second = mine[quarter:] + plus[:, cols].astype(f32)[:quarter] + rb[:, cols].astype(f32)
        summed = jnp.concatenate([first, second], axis=0).astype(bf16)
        for i in range(SIDE):
            total[i] = total[i] + dot(placed(h, i), summed, TN)
    for i, o in enumerate((o0, o1, o2, o3)):
        o[...] = total[i].astype(bf16)


def pair_kernel(kept, got, own, lb, ra, plus, minus):
    total = kept[...].astype(f32) + got[...].astype(f32)
    quarter = lb.shape[0]
    piece = [total[i * quarter : (i + 1) * quarter] for i in range(8)]
    own[...] = total[: 2 * quarter].astype(bf16)
    lb[...] = piece[3].astype(bf16)
    ra[...] = piece[4].astype(bf16)
    plus[...] = jnp.concatenate([piece[5], piece[6]], axis=0).astype(bf16)
    minus[...] = jnp.concatenate([piece[2], piece[7]], axis=0).astype(bf16)


def pair_sums(kept, got):
    many, width = kept.shape
    rows = (many // 4, many // 8, many // 8, many // 4, many // 4)
    chunk = 1024
    return pl.pallas_call(
        pair_kernel,
        grid=(width // chunk,),
        out_shape=[jax.ShapeDtypeStruct((r, width), bf16) for r in rows],
        in_specs=[pl.BlockSpec((many, chunk), lambda s: (0, s))] * 2,
        out_specs=[pl.BlockSpec((r, chunk), lambda s: (0, s)) for r in rows],
        compiler_params=pltpu.CompilerParams(vmem_limit_bytes=16 * 2**20),
        cost_estimate=pl.CostEstimate(flops=many * width, bytes_accessed=6 * many * width, transcendentals=0),
    )(kept, got)


def weighted(weights, parts, h):
    second = row_of((2 * PART, SIDE * BLOCK), 0) >= PART
    mine = second if h else jnp.logical_not(second)
    total = 0.0
    for i in range(SIDE):
        rows = slice(i * 2 * PART, (i + 1) * 2 * PART)
        for k in range(2):
            share = jnp.where(mine, weights[k, rows], 0.0).astype(bf16)
            total = total + dot(share, parts[i][...], TN)
    return total


def gather_kernel(weights, f0, f1, f2, f3, out):
    half = f0.shape[1]
    for h in range(2):
        out[:, h * half : (h + 1) * half] = weighted(weights, (f0, f1, f2, f3), h)


def combine_kernel(before, weights, f0, f1, f2, f3, own, o1, o2, o3):
    half = f0.shape[1]
    for h in range(2):
        cols = slice(h * half, (h + 1) * half)
        total = weighted(weights, (f0, f1, f2, f3), h)
        for i, o in enumerate((own, o1, o2, o3)):
            rows = slice(i * BLOCK, (i + 1) * BLOCK)
            o[:, cols] = jnp.concatenate([before[rows, cols], total[rows]], axis=0).astype(o.dtype)


CHUNK = 1024


def expert_kernel(pieces, chunks, *refs):
    xs, others = refs[:pieces], refs[pieces : 2 * pieces]
    gate, up, down, mine, theirs, rows, gate_sum, up_sum, active = refs[2 * pieces :]
    step = pl.program_id(0)

    @pl.when(step == 0)
    def _():
        gate_sum[...] = jnp.zeros_like(gate_sum)
        up_sum[...] = jnp.zeros_like(up_sum)

    @pl.when(step < chunks)
    def _():
        at = 0
        for x in xs + others:
            rows[at : at + x.shape[0]] = x[...]
            at += x.shape[0]
        gate_sum[...] += dot(rows[...], gate[0])
        up_sum[...] += dot(rows[...], up[0])

    @pl.when(step == chunks)
    def _():
        value = gate_sum[...]
        active[...] = (value / (1.0 + jnp.exp(-value)) * up_sum[...]).astype(bf16)

    @pl.when(step >= chunks)
    def _():
        many = mine.shape[0]
        result = dot(active[...], down[0])
        mine[...] = result[:many].astype(bf16)
        theirs[...] = result[many:].astype(bf16)


def experts(xs, others, gate, up, down):
    pieces = len(xs)
    many = sum(x.shape[0] for x in xs)
    width, units = gate.shape[1:]
    chunks = width // CHUNK

    def first(s):
        return jnp.minimum(s, chunks - 1)

    def second(s):
        return jnp.maximum(s - chunks, 0)

    in_specs = [pl.BlockSpec((x.shape[0], CHUNK), lambda s: (0, first(s))) for x in xs + others]
    in_specs += [pl.BlockSpec((1, CHUNK, units), lambda s: (0, first(s), 0))] * 2
    in_specs += [pl.BlockSpec((1, units, CHUNK), lambda s: (0, 0, second(s)))]
    return pl.pallas_call(
        functools.partial(expert_kernel, pieces, chunks),
        grid=(2 * chunks,),
        out_shape=[jax.ShapeDtypeStruct((many, width), bf16)] * 2,
        in_specs=in_specs,
        out_specs=[pl.BlockSpec((many, CHUNK), lambda s: (0, second(s)))] * 2,
        scratch_shapes=[
            pltpu.VMEM((2 * many, CHUNK), bf16),
            pltpu.VMEM((2 * many, units), f32),
            pltpu.VMEM((2 * many, units), f32),
            pltpu.VMEM((2 * many, units), bf16),
        ],
        compiler_params=pltpu.CompilerParams(vmem_limit_bytes=20 * 2**20),
        cost_estimate=pl.CostEstimate(
            flops=12 * many * width * units, bytes_accessed=6 * width * units + 8 * many * width, transcendentals=0
        ),
    )(*xs, *others, gate, up, down)


def past_kernel(scale, lengths, queries, keys, acc, top, total):
    request = pl.program_id(0)
    length = lengths[request]
    held = keys[0]
    steps = queries.shape[0]
    for t in range(steps):
        scores = dot(queries[t, 0], held, TN) * scale
        lane = lax.broadcasted_iota(jnp.int32, scores.shape, 1)
        visible = lane < length
        scores = jnp.where(visible, scores, masked_score)
        highest = jnp.max(scores, axis=-1, keepdims=True)
        weight = jnp.where(visible, jnp.exp(scores - highest), 0.0)
        acc[0, t] = dot(weight.astype(bf16), held[:LAT], NT)
        top[0, t] = highest
        total[0, t] = jnp.sum(weight, axis=-1, keepdims=True)


def past(lengths, queries, keys, scale, start):
    count, width, context = keys.shape
    steps, _, _, heads = queries.shape
    return pl.pallas_call(
        functools.partial(past_kernel, scale),
        grid_spec=pltpu.PrefetchScalarGridSpec(
            num_scalar_prefetch=1,
            grid=(count,),
            in_specs=[
                pl.BlockSpec((steps, 1, width, heads), lambda r, _: (0, r + start, 0, 0)),
                pl.BlockSpec((1, width, context), lambda r, _: (r, 0, 0)),
            ],
            out_specs=[
                pl.BlockSpec((1, steps, heads, LAT), lambda r, _: (r, 0, 0, 0)),
                pl.BlockSpec((1, steps, heads, 1), lambda r, _: (r, 0, 0, 0)),
                pl.BlockSpec((1, steps, heads, 1), lambda r, _: (r, 0, 0, 0)),
            ],
        ),
        out_shape=[
            jax.ShapeDtypeStruct((count, steps, heads, LAT), f32),
            jax.ShapeDtypeStruct((count, steps, heads, 1), f32),
            jax.ShapeDtypeStruct((count, steps, heads, 1), f32),
        ],
        compiler_params=pltpu.CompilerParams(vmem_limit_bytes=12 * 2**20),
        cost_estimate=pl.CostEstimate(
            flops=2 * count * steps * heads * context * (width + LAT),
            bytes_accessed=count * (2 * width * (context + steps * heads) + 4 * steps * heads * LAT),
            transcendentals=count * steps * heads * context,
        ),
    )(lengths, queries, keys)


def merge_kernel(scale, count, queries, new_keys, acc, top, total, last_acc, last_top, last_total, out, rows):
    steps, _, _, heads = queries.shape
    lanes = LAT // 128
    request = pl.program_id(0)

    def one(acc, top, total):
        for t in range(steps):
            raw = dot(new_keys[0], queries[t, 0]) * scale
            pad = jnp.zeros((heads - raw.shape[0], heads), f32)
            own = jnp.concatenate([raw, pad], axis=0).T
            highest = top[0, t]
            columns = [own[:, k : k + 1] for k in range(t + 1)]
            peak = highest
            for column in columns:
                peak = jnp.maximum(peak, column)
            keep = jnp.exp(highest - peak)
            weights = [jnp.exp(column - peak) for column in columns]
            below = total[0, t] * keep + sum(weights)
            value = acc[0, t] * (keep / below)
            for k in range(t + 1):
                share = (weights[k] / below).astype(bf16).astype(f32)
                value = value + share * new_keys[0, k : k + 1, :LAT].astype(f32)
            for j in range(lanes):
                rows[pl.ds(j * steps + t, heads, stride=lanes * steps), :] = value[:, j * 128 : (j + 1) * 128]
        out[0] = rows[...].astype(bf16)

    @pl.when(request < count)
    def _():
        one(acc, top, total)

    @pl.when(request >= count)
    def _():
        one(last_acc, last_top, last_total)


def merge(queries, new_keys, first, last, scale):
    count, steps, heads, _ = first[0].shape
    rows = count + last[0].shape[0]
    width = queries.shape[2]
    per = new_keys.shape[1]
    tall = heads * steps * LAT // 128

    def early(r):
        return (jnp.minimum(r, count - 1), 0, 0, 0)

    def late(r):
        return (jnp.maximum(r - count, 0), 0, 0, 0)

    parts = [
        pl.BlockSpec((1, steps, heads, size), where) for where in (early, late) for size in (LAT, 1, 1)
    ]
    return pl.pallas_call(
        functools.partial(merge_kernel, scale, count),
        grid=(rows,),
        in_specs=[
            pl.BlockSpec((steps, 1, width, heads), lambda r: (0, r, 0, 0)),
            pl.BlockSpec((1, per, width), lambda r: (r, 0, 0)),
            *parts,
        ],
        out_specs=pl.BlockSpec((1, tall, 128), lambda r: (r, 0, 0)),
        out_shape=jax.ShapeDtypeStruct((rows, tall, 128), bf16),
        scratch_shapes=[pltpu.VMEM((tall, 128), f32)],
        compiler_params=pltpu.CompilerParams(vmem_limit_bytes=12 * 2**20),
    )(queries, new_keys, *first, *last)


def project_kernel(core, hidden, own, a, b, c, gain, kv_own, kv_other, kv_gain, turns, layer, keys, stage):
    mixture = own[...] + a[...].astype(f32) + b[...].astype(f32) + c[...].astype(f32)
    both = (hidden[...].astype(f32) + mixture).astype(bf16)
    many, width = both.shape
    wide = both.astype(f32)
    for k in range(width // 128):
        for t in range(2):
            stage[pl.ds(2 * k + t, BLOCK, stride=width // 64), :] = wide[
                t * BLOCK : (t + 1) * BLOCK, k * 128 : (k + 1) * 128
            ]
    layer[...] = stage[...].astype(bf16)
    normed = rms_scale(both, gain[...]).astype(bf16)
    half = normed.shape[1] // 2
    swapped = core[0] > 0
    low, high = normed[:, :half].astype(f32), normed[:, half:].astype(f32)
    first = jnp.where(swapped, high, low).astype(bf16)
    second = jnp.where(swapped, low, high).astype(bf16)
    projected = (dot(kv_own[...], first, NT) + dot(kv_other[...], second, NT)).T
    keys[:, :LAT] = rms_scale(projected[:, :LAT], kv_gain[...]).astype(bf16)
    rope = projected[:, LAT:]
    crossed = jnp.concatenate([-rope[:, ROPE // 2 :], rope[:, : ROPE // 2]], axis=1)
    keys[:, LAT:] = (rope * turns[0] + crossed * turns[1]).astype(bf16)


def hold(*values):
    return lax.optimization_barrier(values)


def steps_y(mine):
    return [mine, shift(mine, "y", 1), shift(mine, "y", 3), shift(mine, "y", 2)]


def ring_x(own):
    return shift(own, "x", 1), shift(own, "x", 3)


def far_x(left, right):
    half = left.shape[0] // 2
    return [shift(left[:half], "x", 1), shift(right[half:], "x", 3)]


def steps_z(parts, sign):
    return [parts[0]] + [shift(parts[i], "z", sign * i % SIDE) for i in (1, 2, 3)]


CHIPS = ("y", "z", "x")


def fresh_cut(fresh_t):
    width, context = fresh_t.shape
    count = lax.axis_size(CHIPS)
    tiles = width * context // 1024
    each = -(-tiles // count)
    cut = fresh_t.reshape(width // 8, 8, context // 128, 128).swapaxes(1, 2).reshape(tiles, 8, 128)
    cut = jnp.pad(cut, ((0, each * count - tiles), (0, 0), (0, 0)))
    return cut.reshape(count, each * 8, 128)


def fresh_join(whole, width, context):
    tiles = width * context // 1024
    whole = whole.reshape(-1, 8, 128)[:tiles].reshape(width // 8, context // 128, 8, 128)
    return whole.swapaxes(1, 2).reshape(width, context)


def around(value):
    return jnp.where(value < 0, value + SIDE, jnp.where(value >= SIDE, value - SIDE, value))


def pack_kernel(place, cut, *outs):
    for kx in range(SIDE):
        for ky in range(SIDE):
            for kz in range(SIDE):
                y, z, x = around(place[0] + ky), around(place[1] + kz), around(place[2] + kx)
                outs[kx][ky * SIDE + kz] = cut[(y * SIDE + z) * SIDE + x]


def regroup_kernel(last, *refs):
    ins, outs = refs[:SIDE], refs[SIDE:]
    for a in range(SIDE):
        for b in range(SIDE):
            for c in range(SIDE):
                if last:
                    outs[c][b * SIDE + a] = ins[a][b * SIDE + c]
                else:
                    outs[b][a * SIDE + c] = ins[a][b * SIDE + c]


def sort_kernel(order, place, here, there, *outs):
    count = here.shape[0]
    for jz in range(SIDE):
        for jy in range(SIDE):
            for jx in range(SIDE):
                y, z, x = around(place[0] + jy), around(place[1] + jz), around(place[2] + jx)
                wanted = order[place[3] * count + (y * SIDE + z) * SIDE + x]
                upper = wanted >= count
                source = jnp.where(upper, wanted - count, wanted)
                sy, sz, sx = source >> 4, (source >> 2) & 3, source & 3
                kx, ky, kz = around(place[2] - sx), around(place[0] - sy), around(place[1] - sz)
                index = (kz * SIDE + kx) * SIDE + ky
                other = jnp.where(upper, 1, 0) != place[3]
                out = outs[jz].at[jy * SIDE + jx]

                @pl.when(other)
                def _(out=out, index=index):
                    out[...] = there[index]

                @pl.when(jnp.logical_not(other))
                def _(out=out, index=index):
                    out[...] = here[index]


def unpack_kernel(place, x0, x1, x2, x3, whole):
    for jx, part in enumerate((x0, x1, x2, x3)):
        for jz in range(SIDE):
            for jy in range(SIDE):
                y, z, x = around(place[0] - jy), around(place[1] - jz), around(place[2] - jx)
                whole[(y * SIDE + z) * SIDE + x] = part[jz * SIDE + jy]


def quarters(kernel, *args, smem=0):
    rows, lanes = args[-1].shape[1:]
    return call(kernel, [((SIDE * SIDE, rows, lanes), bf16)] * SIDE, *args, smem=smem)


def regroup(last, parts):
    return quarters(functools.partial(regroup_kernel, last), *parts)


def stage(parts, axis):
    return [parts[0], *[shift(parts[i], axis, i) for i in (1, 2, 3)]]


def shards(
    hidden_in,
    ffn_gain,
    attn_gain,
    kv_gain,
    expert_ids,
    route_weight,
    expert_gate,
    expert_up,
    expert_down,
    kv_down,
    resident_cache,
    fresh_cache,
    fresh_order,
    cache_len,
    queries,
):
    steps_count, local_rows, model_width = hidden_in.shape
    resident_rows = resident_cache.shape[0]
    score_scale = (NOPE + ROPE) ** (-0.5)
    core = lax.axis_index("c").astype(jnp.int32).reshape(1)

    payload, hidden_rows = call(
        prepare_kernel,
        [((steps_count * BLOCK, model_width + META), bf16), ((steps_count * BLOCK, model_width), bf16)],
        expert_ids.swapaxes(1, 2), route_weight.swapaxes(1, 2), hidden_in.swapaxes(0, 1), ffn_gain[None],
    )

    position = jnp.stack([lax.axis_index(axis) for axis in ("y", "z", "x", "c")]).astype(jnp.int32)
    folded = ((2 * PART, model_width // 2), bf16)
    query_t = queries.swapaxes(2, 3)
    resident_t = resident_cache.swapaxes(1, 2)

    slot_half = SLOTS // 2
    rows = (steps_count * BLOCK, model_width)

    def select(step, held):
        *parts, weight = call(
            functools.partial(select_kernel, step), [folded] * SIDE + [((2, SIDE * 2 * PART, SIDE * BLOCK), f32)],
            position, *held, smem=1,
        )
        return parts, weight

    def assemble(parts):
        return call(assemble_kernel, [((SLOTS, model_width), bf16)], *parts)[0]

    def combine(*args):
        return call(combine_kernel, [(rows, f32), (rows, bf16), (rows, bf16), (rows, bf16)], *args)

    def gather_slots(weight, parts):
        return call(gather_kernel, [((SIDE * BLOCK, model_width), f32)], weight, *parts)[0]

    def back_y(own, one, two, three):
        return [own, shift(one, "y", 3), shift(two, "y", 1), shift(three, "y", 2)]

    def finish(own, plus, minus, la, rb):
        return call(finish_kernel, [folded] * SIDE, own, plus, minus, la, rb)

    def run_experts(pieces, swapped):
        return experts(list(pieces), list(swapped), expert_gate, expert_up, expert_down)

    def meet(ra, lb, plus, minus):
        return add(ra, plus[slot_half:]), add(lb, minus[slot_half:])

    held = steps_y(payload)
    moving = stage(quarters(pack_kernel, position, fresh_cut(fresh_cache[0].T), smem=1), "x")
    held, moving = hold(held, moving)
    parts, weight0 = select(0, held)
    parts = steps_z(parts, 1)
    parts1, weight1 = select(1, held)
    moving = stage(regroup(False, moving), "y")
    parts, weight0, parts1, weight1, moving = hold(parts, weight0, parts1, weight1, moving)
    own = assemble(parts)
    near = ring_x(own)
    parts = steps_z(parts1, 1)
    moving = regroup(True, moving)
    own, near, parts, moving = hold(own, near, parts, moving)
    far = far_x(*near)
    around_own = jnp.concatenate([own, *near], axis=0)
    near_swapped = swap(around_own)
    own1 = assemble(parts)
    around_own, far, near_swapped, own1, moving = hold(around_own, far, near_swapped, own1, moving)
    moving = stage(moving, "z")
    near1 = ring_x(own1)
    far_swapped = [swap(piece) for piece in far]
    kept0, sent0 = run_experts([around_own, *far], [near_swapped, *far_swapped])
    own1, near1, kept0, sent0, moving = hold(own1, near1, kept0, sent0, moving)
    far = far_x(*near1)
    got0 = swap(sent0)
    around_own = jnp.concatenate([own1, *near1], axis=0)
    near_swapped = swap(around_own)
    own0, lb0, ra0, plus0, minus0 = pair_sums(kept0, got0)
    here = jnp.concatenate(moving, axis=0)
    moving = [here, swap(here)]
    far, near_swapped, around_own, own0, lb0, ra0, plus0, minus0, moving = hold(
        far, near_swapped, around_own, own0, lb0, ra0, plus0, minus0, moving
    )
    plus0, minus0 = shift(plus0, "x", 1), shift(minus0, "x", 3)
    far_swapped = [swap(piece) for piece in far]
    kept1, sent1 = run_experts([around_own, *far], [near_swapped, *far_swapped])
    moving = quarters(sort_kernel, fresh_order, position, *moving, smem=2)
    plus0, minus0, kept1, sent1, moving = hold(plus0, minus0, kept1, sent1, moving)
    ra0, lb0 = meet(ra0, lb0, plus0, minus0)
    la0, rb0 = shift(ra0, "x", 1), shift(lb0, "x", 3)
    got1 = swap(sent1)
    own1, lb1, ra1, plus1, minus1 = pair_sums(kept1, got1)
    moving = regroup(False, stage(moving, "z"))
    la0, rb0, own1, lb1, ra1, plus1, minus1, moving = hold(
        la0, rb0, own1, lb1, ra1, plus1, minus1, moving
    )
    other_down = swap(kv_down.T)
    plus1, minus1 = shift(plus1, "x", 1), shift(minus1, "x", 3)
    parts = steps_z(finish(own0, plus0, minus0, la0, rb0), -1)
    past_resident = past(cache_len, query_t, resident_t, score_scale, 0)
    plus1, minus1, parts0, moving, past_resident, other_down = hold(
        plus1, minus1, parts, moving, past_resident, other_down
    )
    ra1, lb1 = meet(ra1, lb1, plus1, minus1)
    la1, rb1 = shift(ra1, "x", 1), shift(lb1, "x", 3)
    moving = regroup(True, stage(moving, "y"))
    total0 = gather_slots(weight0, parts0)
    la1, rb1, moving, total0 = hold(la1, rb1, moving, total0)
    parts = steps_z(finish(own1, plus1, minus1, la1, rb1), -1)
    moving = stage(moving, "x")
    parts, moving = hold(parts, moving)
    mixed = back_y(*combine(total0, weight1, *parts))
    (whole,) = call(unpack_kernel, [((SIDE**3, *moving[0].shape[1:]), bf16)], position, *moving, smem=1)
    fresh_t = fresh_join(whole, LAT + ROPE, fresh_cache.shape[1])[None]
    past_fresh = past(cache_len[resident_rows:], query_t, fresh_t, score_scale, resident_rows)
    mixed, past_fresh = hold(mixed, past_fresh)

    positions = jnp.pad(cache_len, (0, BLOCK - local_rows)).astype(f32)
    positions = (positions[None, :] + jnp.arange(steps_count).astype(f32)[:, None]).reshape(-1, 1)
    frequency = (rope_base ** (-2.0 * np.arange(ROPE // 2) / ROPE)).astype(np.float32)
    angles = positions * jnp.asarray(np.tile(frequency, 2))[None, :]
    turns = jnp.stack([jnp.cos(angles), jnp.sin(angles)])
    many = steps_count * BLOCK
    layer, keys = call(
        project_kernel,
        [((many * model_width // 128, 128), bf16), ((many, LAT + ROPE), bf16)],
        core, hidden_rows, *mixed, attn_gain[None], kv_down.T, other_down, kv_gain[None], turns,
        smem=1, limit=18, scratch=[pltpu.VMEM((many * model_width // 128, 128), f32)],
    )
    tall = model_width // 128
    layer = layer[: local_rows * steps_count * tall].reshape(local_rows, tall, steps_count, 128)
    layer_out = layer.transpose(2, 0, 1, 3).reshape(steps_count, local_rows, model_width)
    new_keys = jnp.pad(
        keys.reshape(steps_count, BLOCK, LAT + ROPE).swapaxes(0, 1), ((0, 0), (0, BLOCK - steps_count), (0, 0))
    )
    attended = merge(query_t, new_keys, past_resident, past_fresh, score_scale)
    attended = attended.reshape(local_rows, -1, steps_count, 128).transpose(2, 0, 1, 3)
    return layer_out, attended.reshape(steps_count, local_rows, -1)


def solution(mesh):
    grid = Mesh(mesh.devices.reshape(2, 4, 4, 4), ("c", "y", "z", "x"))
    every = ("c", "y", "z", "x")
    placed = (
        P(None, every, None),
        P(),
        P(),
        P(),
        P(None, every, None),
        P(None, every, None),
        P(every, None, None),
        P(every, None, None),
        P(every, None, None),
        P("c", None),
        P(every, None, None),
        P(every, None, None),
        P(),
        P(every),
        P(None, every, None, None),
    )
    return jax.shard_map(
        shards,
        mesh=grid,
        in_specs=placed,
        out_specs=(P(None, every, None), P(None, every, None)),
        check_vma=False,
    )
```

```python
import functools

import jax
import jax.numpy as jnp
import numpy as np
from jax import lax
from jax.experimental import pallas as pl
from jax.experimental.pallas import tpu as pltpu
from jax.sharding import Mesh, PartitionSpec as P

LAT = 512
ROPE = 64
NOPE = 128
EXPERTS = 16
CAP = 3
BLOCK = 8
META = 128
SIDE = 4
PART = SIDE * CAP
SLOTS = SIDE * PART


epsilon = 1e-06
route_scaling = 2.5
rope_base = 10000.0
masked_score = -1e30
f32 = jnp.float32
bf16 = jnp.bfloat16
NT = (((1,), (1,)), ((), ()))
TN = (((0,), (0,)), ((), ()))


def rms_scale(values, gain_vector):
    values = values.astype(f32)
    return (
        values
        * lax.rsqrt(jnp.mean(values * values, axis=-1, keepdims=True) + epsilon)
        * gain_vector
    )


def shift(values, axis, by):
    size = lax.axis_size(axis)
    return lax.ppermute(values, axis, [(i, (i + by) % size) for i in range(size)])


def add(*terms):
    return sum(term.astype(f32) for term in terms).astype(bf16)


def swap(values):
    return shift(values, "c", 1)


def dot(a, b, dims=(((1,), (0,)), ((), ()))):
    return lax.dot_general(a, b, dims, preferred_element_type=f32)


def call(kernel, outs, *args, smem=0, flops=0, limit=12, scratch=()):
    specs = [pl.BlockSpec(memory_space=pltpu.SMEM)] * smem
    specs += [pl.BlockSpec(memory_space=pltpu.VMEM)] * (len(args) - smem)
    moved = sum(a.size * a.dtype.itemsize for a in args)
    return pl.pallas_call(
        kernel,
        out_shape=[jax.ShapeDtypeStruct(shape, dtype) for shape, dtype in outs],
        in_specs=specs,
        out_specs=[pl.BlockSpec(memory_space=pltpu.VMEM)] * len(outs),
        scratch_shapes=list(scratch),
        compiler_params=pltpu.CompilerParams(vmem_limit_bytes=limit * 2**20),
        cost_estimate=pl.CostEstimate(flops=flops, bytes_accessed=moved, transcendentals=0),
    )(*args)


def row_of(shape, dim):
    return lax.broadcasted_iota(jnp.int32, shape, dim)


def digits(value, base, count):
    high = sum(jnp.where(value >= base * i, 1, 0) for i in range(1, count))
    return high, value - base * high


def placed(half, block):
    slot = row_of((SLOTS, 2 * PART), 0) - block * PART
    return jnp.where((row_of((SLOTS, 2 * PART), 1) - half * PART == slot) & (slot >= 0) & (slot < PART), 1.0, 0.0).astype(bf16)


def prepare_kernel(ids, route, hidden, gain, out, plain):
    count, steps, width = hidden.shape
    both = hidden[...].astype(f32)
    blank = jnp.zeros((META - EXPERTS, META), f32)
    spare = jnp.zeros((BLOCK - count, width), f32)
    normed, metas, held = [], [], []
    for t in range(steps):
        values = both[:, t, :]
        held += [values, spare]
        normed += [rms_scale(values, gain[...]), spare]
        share = route[t] / jnp.sum(route[t], axis=0, keepdims=True) * route_scaling
        expert = lax.broadcasted_iota(jnp.int32, (EXPERTS, count), 0)
        dense = jnp.zeros((EXPERTS, count), f32)
        for k in range(share.shape[0]):
            dense = dense + jnp.where(ids[t, k : k + 1] == expert, share[k : k + 1], 0.0)
        dense = jnp.concatenate([dense, jnp.zeros((EXPERTS, META - count), f32)], axis=1)
        dense = jnp.concatenate([dense, blank], axis=0).T
        high = dense.astype(bf16)
        low = (dense - high.astype(f32))[:, :EXPERTS].astype(bf16).astype(f32)
        meta = jnp.concatenate([high.astype(f32)[:, :EXPERTS], low, blank.T[:, EXPERTS:]], axis=1)
        metas.append(meta[:BLOCK])
    plain[...] = jnp.concatenate(held, axis=0).astype(bf16)
    out[:, :width] = jnp.concatenate(normed, axis=0).astype(bf16)
    out[:, width:] = jnp.concatenate(metas, axis=0).astype(bf16)


def select_kernel(step, place, b0, b1, b2, b3, o0, o1, o2, o3, weights):
    mine = slice(step * BLOCK, (step + 1) * BLOCK)
    held = jnp.concatenate([b[...].astype(f32)[mine] for b in (b0, b1, b2, b3)], axis=0)
    width = held.shape[1] - META
    half = width // 2
    many = SIDE * 2 * PART
    count = SIDE * BLOCK
    meta = held[:, width:]
    named = jnp.where((meta > 0) & (row_of(meta.shape, 1) < EXPERTS), 1.0, 0.0).astype(bf16)
    meta = meta.astype(bf16)
    later, sooner = row_of((count, count), 0), row_of((count, count), 1)
    same = digits(later, BLOCK, SIDE)[0] == digits(sooner, BLOCK, SIDE)[0]
    before = dot(jnp.where(same & (sooner < later), 1.0, 0.0).astype(bf16), named).astype(bf16)
    block, rest = digits(row_of((many, META), 0), 2 * PART, SIDE)
    z = place[1] + block
    expert = place[0] * SIDE + jnp.where(z >= SIDE, z - SIDE, z)
    lane = row_of((many, META), 1)
    pick_high = jnp.where(lane == expert, 1.0, 0.0).astype(bf16)
    pick_low = jnp.where(lane == expert + EXPERTS, 1.0, 0.0).astype(bf16)
    _, rest = digits(row_of((many, count), 0), 2 * PART, SIDE)
    second, slot = digits(rest, PART, 2)
    source, turn = digits(slot, CAP, SIDE)
    owner = digits(row_of((many, count), 1), BLOCK, SIDE)[0]
    here = (
        (dot(pick_high, named, NT) > 0.5)
        & (dot(pick_high, before, NT) == turn.astype(f32))
        & (source == owner)
    )
    sel = jnp.where(here, 1.0, 0.0)
    low_half = jnp.where(second > 0, 0.0, sel).astype(bf16)
    high_half = jnp.where(second > 0, sel, 0.0).astype(bf16)
    weights[0] = jnp.where(here, dot(pick_high, meta, NT), 0.0)
    weights[1] = jnp.where(here, dot(pick_low, meta, NT), 0.0)
    slots = dot(low_half, held[:, :half].astype(bf16)) + dot(high_half, held[:, half:width].astype(bf16))
    for i, o in enumerate((o0, o1, o2, o3)):
        o[...] = slots[i * 2 * PART : (i + 1) * 2 * PART].astype(bf16)


def assemble_kernel(f0, f1, f2, f3, out):
    half = f0.shape[1]
    for h in range(2):
        total = 0.0
        for i, f in enumerate((f0, f1, f2, f3)):
            total = total + dot(placed(h, i), f[...])
        out[:, h * half : (h + 1) * half] = total.astype(bf16)


def finish_kernel(own, plus, minus, la, rb, o0, o1, o2, o3):
    quarter = la.shape[0]
    half = own.shape[1] // 2
    total = [0.0] * SIDE
    for h in range(2):
        cols = slice(h * half, (h + 1) * half)
        mine = own[:, cols].astype(f32)
        first = mine[:quarter] + la[:, cols].astype(f32) + minus[:, cols].astype(f32)[:quarter]
        second = mine[quarter:] + plus[:, cols].astype(f32)[:quarter] + rb[:, cols].astype(f32)
        summed = jnp.concatenate([first, second], axis=0).astype(bf16)
        for i in range(SIDE):
            total[i] = total[i] + dot(placed(h, i), summed, TN)
    for i, o in enumerate((o0, o1, o2, o3)):
        o[...] = total[i].astype(bf16)


def pair_kernel(kept, got, own, lb, ra, plus, minus):
    total = kept[...].astype(f32) + got[...].astype(f32)
    quarter = lb.shape[0]
    piece = [total[i * quarter : (i + 1) * quarter] for i in range(8)]
    own[...] = total[: 2 * quarter].astype(bf16)
    lb[...] = piece[3].astype(bf16)
    ra[...] = piece[4].astype(bf16)
    plus[...] = jnp.concatenate([piece[5], piece[6]], axis=0).astype(bf16)
    minus[...] = jnp.concatenate([piece[2], piece[7]], axis=0).astype(bf16)


def pair_sums(kept, got):
    many, width = kept.shape
    rows = (many // 4, many // 8, many // 8, many // 4, many // 4)
    chunk = 1024
    return pl.pallas_call(
        pair_kernel,
        grid=(width // chunk,),
        out_shape=[jax.ShapeDtypeStruct((r, width), bf16) for r in rows],
        in_specs=[pl.BlockSpec((many, chunk), lambda s: (0, s))] * 2,
        out_specs=[pl.BlockSpec((r, chunk), lambda s: (0, s)) for r in rows],
        compiler_params=pltpu.CompilerParams(vmem_limit_bytes=16 * 2**20),
        cost_estimate=pl.CostEstimate(flops=many * width, bytes_accessed=6 * many * width, transcendentals=0),
    )(kept, got)


def weighted(weights, parts, h):
    second = row_of((2 * PART, SIDE * BLOCK), 0) >= PART
    mine = second if h else jnp.logical_not(second)
    total = 0.0
    for i in range(SIDE):
        rows = slice(i * 2 * PART, (i + 1) * 2 * PART)
        for k in range(2):
            share = jnp.where(mine, weights[k, rows], 0.0).astype(bf16)
            total = total + dot(share, parts[i][...], TN)
    return total


def combine_kernel(weights, f0, f1, f2, f3, own, o1, o2, o3):
    half = f0.shape[1]
    for h in range(2):
        cols = slice(h * half, (h + 1) * half)
        total = weighted(weights, (f0, f1, f2, f3), h)
        for i, o in enumerate((own, o1, o2, o3)):
            o[:, cols] = total[i * BLOCK : (i + 1) * BLOCK].astype(o.dtype)


CHUNK = 1792


def expert_kernel(pieces, chunks, *refs):
    xs, others = refs[:pieces], refs[pieces : 2 * pieces]
    gate, up, down, mine, theirs, rows, gate_sum, up_sum, active = refs[2 * pieces :]
    step = pl.program_id(0)

    @pl.when(step == 0)
    def _():
        gate_sum[...] = jnp.zeros_like(gate_sum)
        up_sum[...] = jnp.zeros_like(up_sum)

    @pl.when(step < chunks)
    def _():
        at = 0
        for x in xs + others:
            rows[at : at + x.shape[0]] = x[...]
            at += x.shape[0]
        gate_sum[...] += dot(rows[...], gate[0])
        up_sum[...] += dot(rows[...], up[0])

    @pl.when(step == chunks)
    def _():
        value = gate_sum[...]
        active[...] = (value / (1.0 + jnp.exp(-value)) * up_sum[...]).astype(bf16)

    @pl.when(step >= chunks)
    def _():
        many = mine.shape[0]
        result = dot(active[...], down[0])
        mine[...] = result[:many].astype(bf16)
        theirs[...] = result[many:].astype(bf16)


def experts(xs, others, gate, up, down):
    pieces = len(xs)
    many = sum(x.shape[0] for x in xs)
    width, units = gate.shape[1:]
    chunks = width // CHUNK

    def first(s):
        return jnp.minimum(s, chunks - 1)

    def second(s):
        return jnp.maximum(s - chunks, 0)

    in_specs = [pl.BlockSpec((x.shape[0], CHUNK), lambda s: (0, first(s))) for x in xs + others]
    in_specs += [pl.BlockSpec((1, CHUNK, units), lambda s: (0, first(s), 0))] * 2
    in_specs += [pl.BlockSpec((1, units, CHUNK), lambda s: (0, 0, second(s)))]
    return pl.pallas_call(
        functools.partial(expert_kernel, pieces, chunks),
        grid=(2 * chunks,),
        out_shape=[jax.ShapeDtypeStruct((many, width), bf16)] * 2,
        in_specs=in_specs,
        out_specs=[pl.BlockSpec((many, CHUNK), lambda s: (0, second(s)))] * 2,
        scratch_shapes=[
            pltpu.VMEM((2 * many, CHUNK), bf16),
            pltpu.VMEM((2 * many, units), f32),
            pltpu.VMEM((2 * many, units), f32),
            pltpu.VMEM((2 * many, units), bf16),
        ],
        compiler_params=pltpu.CompilerParams(vmem_limit_bytes=20 * 2**20),
        cost_estimate=pl.CostEstimate(
            flops=12 * many * width * units, bytes_accessed=6 * width * units + 8 * many * width, transcendentals=0
        ),
    )(*xs, *others, gate, up, down)


def past_kernel(scale, lengths, queries, keys, acc, top, total):
    request = pl.program_id(0)
    length = lengths[request]
    held = keys[0]
    steps = queries.shape[0]
    for t in range(steps):
        scores = dot(queries[t, 0], held, TN) * scale
        lane = lax.broadcasted_iota(jnp.int32, scores.shape, 1)
        visible = lane < length
        scores = jnp.where(visible, scores, masked_score)
        highest = jnp.max(scores, axis=-1, keepdims=True)
        weight = jnp.where(visible, jnp.exp(scores - highest), 0.0)
        acc[0, t] = dot(weight.astype(bf16), held[:LAT], NT)
        top[0, t] = highest
        total[0, t] = jnp.sum(weight, axis=-1, keepdims=True)


def past(lengths, queries, keys, scale, start):
    count, width, context = keys.shape
    steps, _, _, heads = queries.shape
    return pl.pallas_call(
        functools.partial(past_kernel, scale),
        grid_spec=pltpu.PrefetchScalarGridSpec(
            num_scalar_prefetch=1,
            grid=(count,),
            in_specs=[
                pl.BlockSpec((steps, 1, width, heads), lambda r, _: (0, r + start, 0, 0)),
                pl.BlockSpec((1, width, context), lambda r, _: (r, 0, 0)),
            ],
            out_specs=[
                pl.BlockSpec((1, steps, heads, LAT), lambda r, _: (r, 0, 0, 0)),
                pl.BlockSpec((1, steps, heads, 1), lambda r, _: (r, 0, 0, 0)),
                pl.BlockSpec((1, steps, heads, 1), lambda r, _: (r, 0, 0, 0)),
            ],
        ),
        out_shape=[
            jax.ShapeDtypeStruct((count, steps, heads, LAT), f32),
            jax.ShapeDtypeStruct((count, steps, heads, 1), f32),
            jax.ShapeDtypeStruct((count, steps, heads, 1), f32),
        ],
        compiler_params=pltpu.CompilerParams(vmem_limit_bytes=12 * 2**20),
        cost_estimate=pl.CostEstimate(
            flops=2 * count * steps * heads * context * (width + LAT),
            bytes_accessed=count * (2 * width * (context + steps * heads) + 4 * steps * heads * LAT),
            transcendentals=count * steps * heads * context,
        ),
    )(lengths, queries, keys)


def merge_kernel(scale, queries, keys, acc, top, total, last_acc, last_top, last_total, out, rows):
    steps, count, _, heads = queries.shape
    lanes = LAT // 128
    early = acc.shape[0]
    new_keys = keys[...].astype(f32)
    for r in range(count):
        held = (acc, top, total, r) if r < early else (last_acc, last_top, last_total, r - early)
        mine = jnp.concatenate([new_keys[t * BLOCK + r : t * BLOCK + r + 1] for t in range(steps)], axis=0)
        padded = jnp.concatenate([mine, jnp.zeros((16 - steps, mine.shape[1]), f32)], axis=0).astype(bf16)
        for t in range(steps):
            raw = dot(padded, queries[t, r]) * scale
            own = jnp.concatenate([raw, jnp.zeros((heads - 16, heads), f32)], axis=0).T
            highest = held[1][held[3], t]
            columns = [own[:, k : k + 1] for k in range(t + 1)]
            peak = highest
            for column in columns:
                peak = jnp.maximum(peak, column)
            keep = jnp.exp(highest - peak)
            weights = [jnp.exp(column - peak) for column in columns]
            below = held[2][held[3], t] * keep + sum(weights)
            value = held[0][held[3], t] * (keep / below)
            for k in range(t + 1):
                share = (weights[k] / below).astype(bf16).astype(f32)
                value = value + share * mine[k : k + 1, :LAT]
            for j in range(lanes):
                rows[r % 2, pl.ds(j * steps + t, heads, stride=lanes * steps), :] = value[:, j * 128 : (j + 1) * 128]
        out[r] = rows[r % 2].astype(bf16)


def merge(queries, keys, first, last, scale):
    steps, count, _, heads = queries.shape
    tall = heads * steps * LAT // 128
    return call(
        functools.partial(merge_kernel, scale), [((count, tall, 128), bf16)], queries, keys, *first, *last,
        limit=20, scratch=[pltpu.VMEM((2, tall, 128), f32)],
    )[0]


def project_kernel(core, lengths, hidden, own0, a0, b0, c0, own1, a1, b1, c1, gain, kv_own, kv_other, kv_gain, layer, keys, stage):
    mixture = jnp.concatenate(
        [
            own[...] + a[...].astype(f32) + b[...].astype(f32) + c[...].astype(f32)
            for own, a, b, c in ((own0, a0, b0, c0), (own1, a1, b1, c1))
        ],
        axis=0,
    )
    both = (hidden[...].astype(f32) + mixture).astype(bf16)
    many, width = both.shape
    wide = both.astype(f32)
    for k in range(width // 128):
        for t in range(2):
            stage[pl.ds(2 * k + t, BLOCK, stride=width // 64), :] = wide[
                t * BLOCK : (t + 1) * BLOCK, k * 128 : (k + 1) * 128
            ]
    layer[...] = stage[...].astype(bf16)[: layer.shape[0]]
    normed = rms_scale(both, gain[...]).astype(bf16)
    half = normed.shape[1] // 2
    swapped = core[0] > 0
    low, high = normed[:, :half].astype(f32), normed[:, half:].astype(f32)
    first = jnp.where(swapped, high, low).astype(bf16)
    second = jnp.where(swapped, low, high).astype(bf16)
    projected = (dot(kv_own[...], first, NT) + dot(kv_other[...], second, NT)).T
    keys[:, :LAT] = rms_scale(projected[:, :LAT], kv_gain[...]).astype(bf16)
    rope = projected[:, LAT:]
    crossed = jnp.concatenate([-rope[:, ROPE // 2 :], rope[:, : ROPE // 2]], axis=1)
    step, row = digits(row_of(rope.shape, 0), BLOCK, many // BLOCK)
    position = step
    for r in range(lengths.shape[0]):
        position = position + jnp.where(row == r, lengths[r], 0)
    lane = row_of(rope.shape, 1)
    pair = jnp.where(lane < ROPE // 2, lane, lane - ROPE // 2).astype(f32)
    angle = position.astype(f32) * jnp.exp(pair * np.float32(-2.0 * np.log(rope_base) / ROPE))
    keys[:, LAT:] = (rope * jnp.cos(angle) + crossed * jnp.sin(angle)).astype(bf16)


def hold(*values):
    return lax.optimization_barrier(values)


def steps_y(mine):
    return [mine, shift(mine, "y", 1), shift(mine, "y", 3), shift(mine, "y", 2)]


def ring_x(own):
    return shift(own, "x", 1), shift(own, "x", 3)


def far_x(left, right):
    half = left.shape[0] // 2
    return [shift(left[:half], "x", 1), shift(right[half:], "x", 3)]


def steps_z(parts, sign):
    return [parts[0]] + [shift(parts[i], "z", sign * i % SIDE) for i in (1, 2, 3)]


CHIPS = ("y", "z", "x")


def fresh_cut(fresh_t):
    width, context = fresh_t.shape
    count = lax.axis_size(CHIPS)
    tiles = width * context // 1024
    each = -(-tiles // count)
    cut = fresh_t.reshape(width // 8, 8, context // 128, 128).swapaxes(1, 2).reshape(tiles, 8, 128)
    cut = jnp.pad(cut, ((0, each * count - tiles), (0, 0), (0, 0)))
    return cut.reshape(count, each * 8, 128)


def fresh_join(whole, width, context):
    tiles = width * context // 1024
    whole = whole.reshape(-1, 8, 128)[:tiles].reshape(width // 8, context // 128, 8, 128)
    return whole.swapaxes(1, 2).reshape(width, context)


def around(value):
    return jnp.where(value < 0, value + SIDE, jnp.where(value >= SIDE, value - SIDE, value))


def pack_kernel(place, cut, *outs):
    for kx in range(SIDE):
        for ky in range(SIDE):
            for kz in range(SIDE):
                y, z, x = around(place[0] + ky), around(place[1] + kz), around(place[2] + kx)
                outs[kx][ky * SIDE + kz] = cut[(y * SIDE + z) * SIDE + x]


def regroup_kernel(last, *refs):
    ins, outs = refs[:SIDE], refs[SIDE:]
    for a in range(SIDE):
        for b in range(SIDE):
            for c in range(SIDE):
                if last:
                    outs[c][b * SIDE + a] = ins[a][b * SIDE + c]
                else:
                    outs[b][a * SIDE + c] = ins[a][b * SIDE + c]


def sort_kernel(order, place, here, there, *outs):
    count = here.shape[0]
    for jz in range(SIDE):
        for jy in range(SIDE):
            for jx in range(SIDE):
                y, z, x = around(place[0] + jy), around(place[1] + jz), around(place[2] + jx)
                wanted = order[place[3] * count + (y * SIDE + z) * SIDE + x]
                upper = wanted >= count
                source = jnp.where(upper, wanted - count, wanted)
                sy, sz, sx = source >> 4, (source >> 2) & 3, source & 3
                kx, ky, kz = around(place[2] - sx), around(place[0] - sy), around(place[1] - sz)
                index = (kz * SIDE + kx) * SIDE + ky
                other = jnp.where(upper, 1, 0) != place[3]
                out = outs[jz].at[jy * SIDE + jx]

                @pl.when(other)
                def _(out=out, index=index):
                    out[...] = there[index]

                @pl.when(jnp.logical_not(other))
                def _(out=out, index=index):
                    out[...] = here[index]


def unpack_kernel(place, x0, x1, x2, x3, whole):
    for jx, part in enumerate((x0, x1, x2, x3)):
        for jz in range(SIDE):
            for jy in range(SIDE):
                y, z, x = around(place[0] - jy), around(place[1] - jz), around(place[2] - jx)
                whole[(y * SIDE + z) * SIDE + x] = part[jz * SIDE + jy]


def quarters(kernel, *args, smem=0):
    rows, lanes = args[-1].shape[1:]
    return call(kernel, [((SIDE * SIDE, rows, lanes), bf16)] * SIDE, *args, smem=smem)


def regroup(last, parts):
    return quarters(functools.partial(regroup_kernel, last), *parts)


def stage(parts, axis):
    return [parts[0], *[shift(parts[i], axis, i) for i in (1, 2, 3)]]


def shards(
    hidden_in,
    ffn_gain,
    attn_gain,
    kv_gain,
    expert_ids,
    route_weight,
    expert_gate,
    expert_up,
    expert_down,
    kv_down,
    resident_cache,
    fresh_cache,
    fresh_order,
    cache_len,
    queries,
):
    steps_count, local_rows, model_width = hidden_in.shape
    resident_rows = resident_cache.shape[0]
    score_scale = (NOPE + ROPE) ** (-0.5)
    core = lax.axis_index("c").astype(jnp.int32).reshape(1)

    payload, hidden_rows = call(
        prepare_kernel,
        [((steps_count * BLOCK, model_width + META), bf16), ((steps_count * BLOCK, model_width), bf16)],
        expert_ids.swapaxes(1, 2), route_weight.swapaxes(1, 2), hidden_in.swapaxes(0, 1), ffn_gain[None],
    )

    position = jnp.stack([lax.axis_index(axis) for axis in ("y", "z", "x", "c")]).astype(jnp.int32)
    folded = ((2 * PART, model_width // 2), bf16)
    query_t = queries.swapaxes(2, 3)
    resident_t = resident_cache.swapaxes(1, 2)

    slot_half = SLOTS // 2
    rows = (BLOCK, model_width)

    def select(step, held):
        *parts, weight = call(
            functools.partial(select_kernel, step), [folded] * SIDE + [((2, SIDE * 2 * PART, SIDE * BLOCK), f32)],
            position, *held, smem=1,
        )
        return parts, weight

    def assemble(parts):
        return call(assemble_kernel, [((SLOTS, model_width), bf16)], *parts)[0]

    def combine(weight, parts):
        return call(combine_kernel, [(rows, f32), (rows, bf16), (rows, bf16), (rows, bf16)], weight, *parts)

    def back_y(own, one, two, three):
        return [own, shift(one, "y", 3), shift(two, "y", 1), shift(three, "y", 2)]

    def finish(own, plus, minus, la, rb):
        return call(finish_kernel, [folded] * SIDE, own, plus, minus, la, rb)

    def run_experts(pieces, swapped):
        return experts(list(pieces), list(swapped), expert_gate, expert_up, expert_down)

    def meet(ra, lb, plus, minus):
        return add(ra, plus[slot_half:]), add(lb, minus[slot_half:])

    payload, prefilled = hold(payload, fresh_cache)
    held = steps_y(payload)
    moving = stage(quarters(pack_kernel, position, fresh_cut(prefilled[0].T), smem=1), "x")
    held, moving = hold(held, moving)
    parts, weight0 = select(0, held)
    parts = steps_z(parts, 1)
    parts1, weight1 = select(1, held)
    moving = stage(regroup(False, moving), "y")
    parts, weight0, parts1, weight1, moving = hold(parts, weight0, parts1, weight1, moving)
    own = assemble(parts)
    near = ring_x(own)
    parts = steps_z(parts1, 1)
    moving = regroup(True, moving)
    own, near, parts, moving = hold(own, near, parts, moving)
    far = far_x(*near)
    around_own = jnp.concatenate([own, *near], axis=0)
    near_swapped = swap(around_own)
    own1 = assemble(parts)
    around_own, far, near_swapped, own1, moving = hold(around_own, far, near_swapped, own1, moving)
    moving = stage(moving, "z")
    near1 = ring_x(own1)
    far_swapped = [swap(piece) for piece in far]
    kept0, sent0 = run_experts([around_own, *far], [near_swapped, *far_swapped])
    own1, near1, kept0, sent0, moving = hold(own1, near1, kept0, sent0, moving)
    far = far_x(*near1)
    got0 = swap(sent0)
    around_own = jnp.concatenate([own1, *near1], axis=0)
    near_swapped = swap(around_own)
    own0, lb0, ra0, plus0, minus0 = pair_sums(kept0, got0)
    here = jnp.concatenate(moving, axis=0)
    moving = quarters(sort_kernel, fresh_order, position, here, swap(here), smem=2)
    far, near_swapped, around_own, own0, lb0, ra0, plus0, minus0, moving = hold(
        far, near_swapped, around_own, own0, lb0, ra0, plus0, minus0, moving
    )
    plus0, minus0 = shift(plus0, "x", 1), shift(minus0, "x", 3)
    far_swapped = [swap(piece) for piece in far]
    kept1, sent1 = run_experts([around_own, *far], [near_swapped, *far_swapped])
    moving = stage(moving, "z")
    plus0, minus0, kept1, sent1, moving = hold(plus0, minus0, kept1, sent1, moving)
    ra0, lb0 = meet(ra0, lb0, plus0, minus0)
    la0, rb0 = shift(ra0, "x", 1), shift(lb0, "x", 3)
    got1, moving = hold(swap(sent1), moving)
    moving = stage(regroup(False, moving), "y")
    own1, lb1, ra1, plus1, minus1 = pair_sums(kept1, got1)
    la0, rb0, own1, lb1, ra1, plus1, minus1, moving = hold(
        la0, rb0, own1, lb1, ra1, plus1, minus1, moving
    )
    plus1, minus1 = shift(plus1, "x", 1), shift(minus1, "x", 3)
    parts = steps_z(finish(own0, plus0, minus0, la0, rb0), -1)
    moving = regroup(True, moving)
    past_resident = past(cache_len, query_t, resident_t, score_scale, 0)
    plus1, minus1, parts0, moving, past_resident = hold(plus1, minus1, parts, moving, past_resident)
    ra1, lb1 = meet(ra1, lb1, plus1, minus1)
    la1, rb1 = shift(ra1, "x", 1), shift(lb1, "x", 3)
    mixed0 = back_y(*combine(weight0, parts0))
    la1, rb1, mixed0, moving = hold(la1, rb1, mixed0, moving)
    parts = steps_z(finish(own1, plus1, minus1, la1, rb1), -1)
    moving = stage(moving, "x")
    parts, moving, kv_t = hold(parts, moving, kv_down.T)
    other_down = swap(kv_t)
    mixed = [*mixed0, *back_y(*combine(weight1, parts))]
    (whole,) = call(unpack_kernel, [((SIDE**3, *moving[0].shape[1:]), bf16)], position, *moving, smem=1)
    fresh_t = fresh_join(whole, LAT + ROPE, fresh_cache.shape[1])[None]
    past_fresh = past(cache_len[resident_rows:], query_t, fresh_t, score_scale, resident_rows)
    mixed, past_fresh, other_down = hold(mixed, past_fresh, other_down)

    many = steps_count * BLOCK
    layer, keys = call(
        project_kernel,
        [((local_rows * steps_count * model_width // 128, 128), bf16), ((many, LAT + ROPE), bf16)],
        core, cache_len, hidden_rows, *mixed, attn_gain[None], kv_t, other_down, kv_gain[None],
        smem=2, limit=18, scratch=[pltpu.VMEM((many * model_width // 128, 128), f32)],
    )
    tall = model_width // 128
    layer = layer.reshape(local_rows, tall, steps_count, 128)
    layer_out = layer.transpose(2, 0, 1, 3).reshape(steps_count, local_rows, model_width)
    attended = merge(query_t, keys, past_resident, past_fresh, score_scale)
    attended = attended.reshape(local_rows, -1, steps_count, 128).transpose(2, 0, 1, 3)
    return layer_out, attended.reshape(steps_count, local_rows, -1)


def solution(mesh):
    grid = Mesh(mesh.devices.reshape(2, 4, 4, 4), ("c", "y", "z", "x"))
    every = ("c", "y", "z", "x")
    placed = (
        P(None, every, None),
        P(),
        P(),
        P(),
        P(None, every, None),
        P(None, every, None),
        P(every, None, None),
        P(every, None, None),
        P(every, None, None),
        P("c", None),
        P(every, None, None),
        P(every, None, None),
        P(),
        P(every),
        P(None, every, None, None),
    )
    return jax.shard_map(
        shards,
        mesh=grid,
        in_specs=placed,
        out_specs=(P(None, every, None), P(None, every, None)),
        check_vma=False,
    )
```

```python
import functools

import jax
import jax.numpy as jnp
import numpy as np
from jax import lax
from jax.experimental import pallas as pl
from jax.experimental.pallas import tpu as pltpu
from jax.sharding import Mesh, PartitionSpec as P

LAT = 512
ROPE = 64
NOPE = 128
EXPERTS = 16
CAP = 3
BLOCK = 8
META = 128
SIDE = 4
PART = SIDE * CAP
SLOTS = SIDE * PART


epsilon = 1e-06
route_scaling = 2.5
rope_base = 10000.0
masked_score = -1e30
f32 = jnp.float32
bf16 = jnp.bfloat16
NT = (((1,), (1,)), ((), ()))
TN = (((0,), (0,)), ((), ()))


def rms_scale(values, gain_vector):
    values = values.astype(f32)
    return (
        values
        * lax.rsqrt(jnp.mean(values * values, axis=-1, keepdims=True) + epsilon)
        * gain_vector
    )


def shift(values, axis, by):
    size = lax.axis_size(axis)
    return lax.ppermute(values, axis, [(i, (i + by) % size) for i in range(size)])


def add(*terms):
    return sum(term.astype(f32) for term in terms).astype(bf16)


def swap(values):
    return shift(values, "c", 1)


def dot(a, b, dims=(((1,), (0,)), ((), ()))):
    return lax.dot_general(a, b, dims, preferred_element_type=f32)


def call(kernel, outs, *args, smem=0, flops=0, limit=12, scratch=()):
    specs = [pl.BlockSpec(memory_space=pltpu.SMEM)] * smem
    specs += [pl.BlockSpec(memory_space=pltpu.VMEM)] * (len(args) - smem)
    moved = sum(a.size * a.dtype.itemsize for a in args)
    return pl.pallas_call(
        kernel,
        out_shape=[jax.ShapeDtypeStruct(shape, dtype) for shape, dtype in outs],
        in_specs=specs,
        out_specs=[pl.BlockSpec(memory_space=pltpu.VMEM)] * len(outs),
        scratch_shapes=list(scratch),
        compiler_params=pltpu.CompilerParams(vmem_limit_bytes=limit * 2**20),
        cost_estimate=pl.CostEstimate(flops=flops, bytes_accessed=moved, transcendentals=0),
    )(*args)


def row_of(shape, dim):
    return lax.broadcasted_iota(jnp.int32, shape, dim)


def digits(value, base, count):
    high = sum(jnp.where(value >= base * i, 1, 0) for i in range(1, count))
    return high, value - base * high


def placed(half, block):
    slot = row_of((SLOTS, 2 * PART), 0) - block * PART
    return jnp.where((row_of((SLOTS, 2 * PART), 1) - half * PART == slot) & (slot >= 0) & (slot < PART), 1.0, 0.0).astype(bf16)


def prepare_kernel(ids, route, hidden, gain, out, plain):
    count, steps, width = hidden.shape
    both = hidden[...].astype(f32)
    blank = jnp.zeros((META - EXPERTS, META), f32)
    spare = jnp.zeros((BLOCK - count, width), f32)
    normed, metas, held = [], [], []
    for t in range(steps):
        values = both[:, t, :]
        held += [values, spare]
        normed += [rms_scale(values, gain[...]), spare]
        share = route[t] / jnp.sum(route[t], axis=0, keepdims=True) * route_scaling
        expert = lax.broadcasted_iota(jnp.int32, (EXPERTS, count), 0)
        dense = jnp.zeros((EXPERTS, count), f32)
        for k in range(share.shape[0]):
            dense = dense + jnp.where(ids[t, k : k + 1] == expert, share[k : k + 1], 0.0)
        dense = jnp.concatenate([dense, jnp.zeros((EXPERTS, META - count), f32)], axis=1)
        dense = jnp.concatenate([dense, blank], axis=0).T
        high = dense.astype(bf16)
        low = (dense - high.astype(f32))[:, :EXPERTS].astype(bf16).astype(f32)
        meta = jnp.concatenate([high.astype(f32)[:, :EXPERTS], low, blank.T[:, EXPERTS:]], axis=1)
        metas.append(meta[:BLOCK])
    plain[...] = jnp.concatenate(held, axis=0).astype(bf16)
    out[:, :width] = jnp.concatenate(normed, axis=0).astype(bf16)
    out[:, width:] = jnp.concatenate(metas, axis=0).astype(bf16)


def select_kernel(step, place, b0, b1, b2, b3, o0, o1, o2, o3, weights):
    mine = slice(step * BLOCK, (step + 1) * BLOCK)
    held = jnp.concatenate([b[...].astype(f32)[mine] for b in (b0, b1, b2, b3)], axis=0)
    width = held.shape[1] - META
    half = width // 2
    many = SIDE * 2 * PART
    count = SIDE * BLOCK
    meta = held[:, width:]
    named = jnp.where((meta > 0) & (row_of(meta.shape, 1) < EXPERTS), 1.0, 0.0).astype(bf16)
    meta = meta.astype(bf16)
    later, sooner = row_of((count, count), 0), row_of((count, count), 1)
    same = digits(later, BLOCK, SIDE)[0] == digits(sooner, BLOCK, SIDE)[0]
    before = dot(jnp.where(same & (sooner < later), 1.0, 0.0).astype(bf16), named).astype(bf16)
    block, rest = digits(row_of((many, META), 0), 2 * PART, SIDE)
    z = place[1] + block
    expert = place[0] * SIDE + jnp.where(z >= SIDE, z - SIDE, z)
    lane = row_of((many, META), 1)
    pick_high = jnp.where(lane == expert, 1.0, 0.0).astype(bf16)
    pick_low = jnp.where(lane == expert + EXPERTS, 1.0, 0.0).astype(bf16)
    _, rest = digits(row_of((many, count), 0), 2 * PART, SIDE)
    second, slot = digits(rest, PART, 2)
    source, turn = digits(slot, CAP, SIDE)
    owner = digits(row_of((many, count), 1), BLOCK, SIDE)[0]
    here = (
        (dot(pick_high, named, NT) > 0.5)
        & (dot(pick_high, before, NT) == turn.astype(f32))
        & (source == owner)
    )
    sel = jnp.where(here, 1.0, 0.0)
    low_half = jnp.where(second > 0, 0.0, sel).astype(bf16)
    high_half = jnp.where(second > 0, sel, 0.0).astype(bf16)
    weights[0] = jnp.where(here, dot(pick_high, meta, NT), 0.0)
    weights[1] = jnp.where(here, dot(pick_low, meta, NT), 0.0)
    slots = dot(low_half, held[:, :half].astype(bf16)) + dot(high_half, held[:, half:width].astype(bf16))
    for i, o in enumerate((o0, o1, o2, o3)):
        o[...] = slots[i * 2 * PART : (i + 1) * 2 * PART].astype(bf16)


def assemble_kernel(f0, f1, f2, f3, out):
    half = f0.shape[1]
    for h in range(2):
        total = 0.0
        for i, f in enumerate((f0, f1, f2, f3)):
            total = total + dot(placed(h, i), f[...])
        out[:, h * half : (h + 1) * half] = total.astype(bf16)


def finish_kernel(own, plus, minus, la, rb, o0, o1, o2, o3):
    quarter = la.shape[0]
    half = own.shape[1] // 2
    total = [0.0] * SIDE
    for h in range(2):
        cols = slice(h * half, (h + 1) * half)
        mine = own[:, cols].astype(f32)
        first = mine[:quarter] + la[:, cols].astype(f32) + minus[:, cols].astype(f32)[:quarter]
        second = mine[quarter:] + plus[:, cols].astype(f32)[:quarter] + rb[:, cols].astype(f32)
        summed = jnp.concatenate([first, second], axis=0).astype(bf16)
        for i in range(SIDE):
            total[i] = total[i] + dot(placed(h, i), summed, TN)
    for i, o in enumerate((o0, o1, o2, o3)):
        o[...] = total[i].astype(bf16)


def pair_kernel(kept, got, own, lb, ra, plus, minus):
    total = kept[...].astype(f32) + got[...].astype(f32)
    quarter = lb.shape[0]
    piece = [total[i * quarter : (i + 1) * quarter] for i in range(8)]
    own[...] = total[: 2 * quarter].astype(bf16)
    lb[...] = piece[3].astype(bf16)
    ra[...] = piece[4].astype(bf16)
    plus[...] = jnp.concatenate([piece[5], piece[6]], axis=0).astype(bf16)
    minus[...] = jnp.concatenate([piece[2], piece[7]], axis=0).astype(bf16)


def pair_sums(kept, got):
    many, width = kept.shape
    rows = (many // 4, many // 8, many // 8, many // 4, many // 4)
    chunk = 1024
    return pl.pallas_call(
        pair_kernel,
        grid=(width // chunk,),
        out_shape=[jax.ShapeDtypeStruct((r, width), bf16) for r in rows],
        in_specs=[pl.BlockSpec((many, chunk), lambda s: (0, s))] * 2,
        out_specs=[pl.BlockSpec((r, chunk), lambda s: (0, s)) for r in rows],
        compiler_params=pltpu.CompilerParams(vmem_limit_bytes=16 * 2**20),
        cost_estimate=pl.CostEstimate(flops=many * width, bytes_accessed=6 * many * width, transcendentals=0),
    )(kept, got)


def weighted(weights, parts, h):
    second = row_of((2 * PART, SIDE * BLOCK), 0) >= PART
    mine = second if h else jnp.logical_not(second)
    total = 0.0
    for i in range(SIDE):
        rows = slice(i * 2 * PART, (i + 1) * 2 * PART)
        for k in range(2):
            share = jnp.where(mine, weights[k, rows], 0.0).astype(bf16)
            total = total + dot(share, parts[i][...], TN)
    return total


def combine_kernel(weights, f0, f1, f2, f3, own, o1, o2, o3):
    half = f0.shape[1]
    for h in range(2):
        cols = slice(h * half, (h + 1) * half)
        total = weighted(weights, (f0, f1, f2, f3), h)
        for i, o in enumerate((own, o1, o2, o3)):
            o[:, cols] = total[i * BLOCK : (i + 1) * BLOCK].astype(o.dtype)


CHUNK = 1792


def expert_kernel(pieces, chunks, *refs):
    xs, others = refs[:pieces], refs[pieces : 2 * pieces]
    gate, up, down, mine, theirs, rows, gate_sum, up_sum, active = refs[2 * pieces :]
    step = pl.program_id(0)

    @pl.when(step == 0)
    def _():
        gate_sum[...] = jnp.zeros_like(gate_sum)
        up_sum[...] = jnp.zeros_like(up_sum)

    @pl.when(step < chunks)
    def _():
        at = 0
        for x in xs + others:
            rows[at : at + x.shape[0]] = x[...]
            at += x.shape[0]
        gate_sum[...] += dot(rows[...], gate[0])
        up_sum[...] += dot(rows[...], up[0])

    @pl.when(step == chunks)
    def _():
        value = gate_sum[...]
        active[...] = (value / (1.0 + jnp.exp(-value)) * up_sum[...]).astype(bf16)

    @pl.when(step >= chunks)
    def _():
        many = mine.shape[0]
        result = dot(active[...], down[0])
        mine[...] = result[:many].astype(bf16)
        theirs[...] = result[many:].astype(bf16)


def experts(xs, others, gate, up, down):
    pieces = len(xs)
    many = sum(x.shape[0] for x in xs)
    width, units = gate.shape[1:]
    chunks = width // CHUNK

    def first(s):
        return jnp.minimum(s, chunks - 1)

    def second(s):
        return jnp.maximum(s - chunks, 0)

    in_specs = [pl.BlockSpec((x.shape[0], CHUNK), lambda s: (0, first(s))) for x in xs + others]
    in_specs += [pl.BlockSpec((1, CHUNK, units), lambda s: (0, first(s), 0))] * 2
    in_specs += [pl.BlockSpec((1, units, CHUNK), lambda s: (0, 0, second(s)))]
    return pl.pallas_call(
        functools.partial(expert_kernel, pieces, chunks),
        grid=(2 * chunks,),
        out_shape=[jax.ShapeDtypeStruct((many, width), bf16)] * 2,
        in_specs=in_specs,
        out_specs=[pl.BlockSpec((many, CHUNK), lambda s: (0, second(s)))] * 2,
        scratch_shapes=[
            pltpu.VMEM((2 * many, CHUNK), bf16),
            pltpu.VMEM((2 * many, units), f32),
            pltpu.VMEM((2 * many, units), f32),
            pltpu.VMEM((2 * many, units), bf16),
        ],
        compiler_params=pltpu.CompilerParams(vmem_limit_bytes=20 * 2**20),
        cost_estimate=pl.CostEstimate(
            flops=12 * many * width * units, bytes_accessed=6 * width * units + 8 * many * width, transcendentals=0
        ),
    )(*xs, *others, gate, up, down)


def past_kernel(scale, lengths, queries, keys, acc, top, total):
    request = pl.program_id(0)
    length = lengths[request]
    held = keys[0]
    steps = queries.shape[0]
    for t in range(steps):
        scores = dot(queries[t, 0], held, TN) * scale
        lane = lax.broadcasted_iota(jnp.int32, scores.shape, 1)
        visible = lane < length
        scores = jnp.where(visible, scores, masked_score)
        highest = jnp.max(scores, axis=-1, keepdims=True)
        weight = jnp.where(visible, jnp.exp(scores - highest), 0.0)
        acc[0, t] = dot(weight.astype(bf16), held[:LAT], NT)
        top[0, t] = highest
        total[0, t] = jnp.sum(weight, axis=-1, keepdims=True)


def past(lengths, queries, keys, scale, start):
    count, width, context = keys.shape
    steps, _, _, heads = queries.shape
    return pl.pallas_call(
        functools.partial(past_kernel, scale),
        grid_spec=pltpu.PrefetchScalarGridSpec(
            num_scalar_prefetch=1,
            grid=(count,),
            in_specs=[
                pl.BlockSpec((steps, 1, width, heads), lambda r, _: (0, r + start, 0, 0)),
                pl.BlockSpec((1, width, context), lambda r, _: (r, 0, 0)),
            ],
            out_specs=[
                pl.BlockSpec((1, steps, heads, LAT), lambda r, _: (r, 0, 0, 0)),
                pl.BlockSpec((1, steps, heads, 1), lambda r, _: (r, 0, 0, 0)),
                pl.BlockSpec((1, steps, heads, 1), lambda r, _: (r, 0, 0, 0)),
            ],
        ),
        out_shape=[
            jax.ShapeDtypeStruct((count, steps, heads, LAT), f32),
            jax.ShapeDtypeStruct((count, steps, heads, 1), f32),
            jax.ShapeDtypeStruct((count, steps, heads, 1), f32),
        ],
        compiler_params=pltpu.CompilerParams(vmem_limit_bytes=12 * 2**20),
        cost_estimate=pl.CostEstimate(
            flops=2 * count * steps * heads * context * (width + LAT),
            bytes_accessed=count * (2 * width * (context + steps * heads) + 4 * steps * heads * LAT),
            transcendentals=count * steps * heads * context,
        ),
    )(lengths, queries, keys)


def merge_kernel(scale, count, queries, new_keys, acc, top, total, last_acc, last_top, last_total, out, rows):
    steps, _, _, heads = queries.shape
    lanes = LAT // 128
    request = pl.program_id(0)

    def one(acc, top, total):
        for t in range(steps):
            raw = dot(new_keys[0], queries[t, 0]) * scale
            pad = jnp.zeros((heads - raw.shape[0], heads), f32)
            own = jnp.concatenate([raw, pad], axis=0).T
            highest = top[0, t]
            columns = [own[:, k : k + 1] for k in range(t + 1)]
            peak = highest
            for column in columns:
                peak = jnp.maximum(peak, column)
            keep = jnp.exp(highest - peak)
            weights = [jnp.exp(column - peak) for column in columns]
            below = total[0, t] * keep + sum(weights)
            value = acc[0, t] * (keep / below)
            for k in range(t + 1):
                share = (weights[k] / below).astype(bf16).astype(f32)
                value = value + share * new_keys[0, k : k + 1, :LAT].astype(f32)
            for j in range(lanes):
                rows[pl.ds(j * steps + t, heads, stride=lanes * steps), :] = value[:, j * 128 : (j + 1) * 128]
        out[0] = rows[...].astype(bf16)

    @pl.when(request < count)
    def _():
        one(acc, top, total)

    @pl.when(request >= count)
    def _():
        one(last_acc, last_top, last_total)


def merge(queries, new_keys, first, last, scale):
    count, steps, heads, _ = first[0].shape
    rows = count + last[0].shape[0]
    width = queries.shape[2]
    per = new_keys.shape[1]
    tall = heads * steps * LAT // 128

    def early(r):
        return (jnp.minimum(r, count - 1), 0, 0, 0)

    def late(r):
        return (jnp.maximum(r - count, 0), 0, 0, 0)

    parts = [
        pl.BlockSpec((1, steps, heads, size), where) for where in (early, late) for size in (LAT, 1, 1)
    ]
    return pl.pallas_call(
        functools.partial(merge_kernel, scale, count),
        grid=(rows,),
        in_specs=[
            pl.BlockSpec((steps, 1, width, heads), lambda r: (0, r, 0, 0)),
            pl.BlockSpec((1, per, width), lambda r: (r, 0, 0)),
            *parts,
        ],
        out_specs=pl.BlockSpec((1, tall, 128), lambda r: (r, 0, 0)),
        out_shape=jax.ShapeDtypeStruct((rows, tall, 128), bf16),
        scratch_shapes=[pltpu.VMEM((tall, 128), f32)],
        compiler_params=pltpu.CompilerParams(vmem_limit_bytes=12 * 2**20),
    )(queries, new_keys, *first, *last)


def project_kernel(core, lengths, hidden, own0, a0, b0, c0, own1, a1, b1, c1, gain, kv_own, kv_other, kv_gain, layer, keys, stage):
    mixture = jnp.concatenate(
        [
            own[...] + a[...].astype(f32) + b[...].astype(f32) + c[...].astype(f32)
            for own, a, b, c in ((own0, a0, b0, c0), (own1, a1, b1, c1))
        ],
        axis=0,
    )
    both = (hidden[...].astype(f32) + mixture).astype(bf16)
    many, width = both.shape
    wide = both.astype(f32)
    for k in range(width // 128):
        for t in range(2):
            stage[pl.ds(2 * k + t, BLOCK, stride=width // 64), :] = wide[
                t * BLOCK : (t + 1) * BLOCK, k * 128 : (k + 1) * 128
            ]
    layer[...] = stage[...].astype(bf16)[: layer.shape[0]]
    normed = rms_scale(both, gain[...]).astype(bf16)
    half = normed.shape[1] // 2
    swapped = core[0] > 0
    low, high = normed[:, :half].astype(f32), normed[:, half:].astype(f32)
    first = jnp.where(swapped, high, low).astype(bf16)
    second = jnp.where(swapped, low, high).astype(bf16)
    projected = (dot(kv_own[...], first, NT) + dot(kv_other[...], second, NT)).T
    keys[:, :LAT] = rms_scale(projected[:, :LAT], kv_gain[...]).astype(bf16)
    rope = projected[:, LAT:]
    crossed = jnp.concatenate([-rope[:, ROPE // 2 :], rope[:, : ROPE // 2]], axis=1)
    step, row = digits(row_of(rope.shape, 0), BLOCK, many // BLOCK)
    position = step
    for r in range(lengths.shape[0]):
        position = position + jnp.where(row == r, lengths[r], 0)
    lane = row_of(rope.shape, 1)
    pair = jnp.where(lane < ROPE // 2, lane, lane - ROPE // 2).astype(f32)
    angle = position.astype(f32) * jnp.exp(pair * np.float32(-2.0 * np.log(rope_base) / ROPE))
    keys[:, LAT:] = (rope * jnp.cos(angle) + crossed * jnp.sin(angle)).astype(bf16)


def hold(*values):
    return lax.optimization_barrier(values)


def steps_y(mine):
    return [mine, shift(mine, "y", 1), shift(mine, "y", 3), shift(mine, "y", 2)]


def ring_x(own):
    return shift(own, "x", 1), shift(own, "x", 3)


def far_x(left, right):
    half = left.shape[0] // 2
    return [shift(left[:half], "x", 1), shift(right[half:], "x", 3)]


def steps_z(parts, sign):
    return [parts[0]] + [shift(parts[i], "z", sign * i % SIDE) for i in (1, 2, 3)]


CHIPS = ("y", "z", "x")


def fresh_cut(fresh_t):
    width, context = fresh_t.shape
    count = lax.axis_size(CHIPS)
    tiles = width * context // 1024
    each = -(-tiles // count)
    cut = fresh_t.reshape(width // 8, 8, context // 128, 128).swapaxes(1, 2).reshape(tiles, 8, 128)
    cut = jnp.pad(cut, ((0, each * count - tiles), (0, 0), (0, 0)))
    return cut.reshape(count, each * 8, 128)


def fresh_join(whole, width, context):
    tiles = width * context // 1024
    whole = whole.reshape(-1, 8, 128)[:tiles].reshape(width // 8, context // 128, 8, 128)
    return whole.swapaxes(1, 2).reshape(width, context)


def around(value):
    return jnp.where(value < 0, value + SIDE, jnp.where(value >= SIDE, value - SIDE, value))


def pack_kernel(place, cut, *outs):
    for kx in range(SIDE):
        for ky in range(SIDE):
            for kz in range(SIDE):
                y, z, x = around(place[0] + ky), around(place[1] + kz), around(place[2] + kx)
                outs[kx][ky * SIDE + kz] = cut[(y * SIDE + z) * SIDE + x]


def regroup_kernel(last, *refs):
    ins, outs = refs[:SIDE], refs[SIDE:]
    for a in range(SIDE):
        for b in range(SIDE):
            for c in range(SIDE):
                if last:
                    outs[c][b * SIDE + a] = ins[a][b * SIDE + c]
                else:
                    outs[b][a * SIDE + c] = ins[a][b * SIDE + c]


def sort_kernel(order, place, here, there, *outs):
    count = here.shape[0]
    for jz in range(SIDE):
        for jy in range(SIDE):
            for jx in range(SIDE):
                y, z, x = around(place[0] + jy), around(place[1] + jz), around(place[2] + jx)
                wanted = order[place[3] * count + (y * SIDE + z) * SIDE + x]
                upper = wanted >= count
                source = jnp.where(upper, wanted - count, wanted)
                sy, sz, sx = source >> 4, (source >> 2) & 3, source & 3
                kx, ky, kz = around(place[2] - sx), around(place[0] - sy), around(place[1] - sz)
                index = (kz * SIDE + kx) * SIDE + ky
                other = jnp.where(upper, 1, 0) != place[3]
                out = outs[jz].at[jy * SIDE + jx]

                @pl.when(other)
                def _(out=out, index=index):
                    out[...] = there[index]

                @pl.when(jnp.logical_not(other))
                def _(out=out, index=index):
                    out[...] = here[index]


def unpack_kernel(place, x0, x1, x2, x3, whole):
    for jx, part in enumerate((x0, x1, x2, x3)):
        for jz in range(SIDE):
            for jy in range(SIDE):
                y, z, x = around(place[0] - jy), around(place[1] - jz), around(place[2] - jx)
                whole[(y * SIDE + z) * SIDE + x] = part[jz * SIDE + jy]


def quarters(kernel, *args, smem=0):
    rows, lanes = args[-1].shape[1:]
    return call(kernel, [((SIDE * SIDE, rows, lanes), bf16)] * SIDE, *args, smem=smem)


def regroup(last, parts):
    return quarters(functools.partial(regroup_kernel, last), *parts)


def stage(parts, axis):
    return [parts[0], *[shift(parts[i], axis, i) for i in (1, 2, 3)]]


def shards(
    hidden_in,
    ffn_gain,
    attn_gain,
    kv_gain,
    expert_ids,
    route_weight,
    expert_gate,
    expert_up,
    expert_down,
    kv_down,
    resident_cache,
    fresh_cache,
    fresh_order,
    cache_len,
    queries,
):
    steps_count, local_rows, model_width = hidden_in.shape
    resident_rows = resident_cache.shape[0]
    score_scale = (NOPE + ROPE) ** (-0.5)
    core = lax.axis_index("c").astype(jnp.int32).reshape(1)

    payload, hidden_rows = call(
        prepare_kernel,
        [((steps_count * BLOCK, model_width + META), bf16), ((steps_count * BLOCK, model_width), bf16)],
        expert_ids.swapaxes(1, 2), route_weight.swapaxes(1, 2), hidden_in.swapaxes(0, 1), ffn_gain[None],
    )

    position = jnp.stack([lax.axis_index(axis) for axis in ("y", "z", "x", "c")]).astype(jnp.int32)
    folded = ((2 * PART, model_width // 2), bf16)
    query_t = queries.swapaxes(2, 3)
    resident_t = resident_cache.swapaxes(1, 2)

    slot_half = SLOTS // 2
    rows = (BLOCK, model_width)

    def select(step, held):
        *parts, weight = call(
            functools.partial(select_kernel, step), [folded] * SIDE + [((2, SIDE * 2 * PART, SIDE * BLOCK), f32)],
            position, *held, smem=1,
        )
        return parts, weight

    def assemble(parts):
        return call(assemble_kernel, [((SLOTS, model_width), bf16)], *parts)[0]

    def combine(weight, parts):
        return call(combine_kernel, [(rows, f32), (rows, bf16), (rows, bf16), (rows, bf16)], weight, *parts)

    def back_y(own, one, two, three):
        return [own, shift(one, "y", 3), shift(two, "y", 1), shift(three, "y", 2)]

    def finish(own, plus, minus, la, rb):
        return call(finish_kernel, [folded] * SIDE, own, plus, minus, la, rb)

    def run_experts(pieces, swapped):
        return experts(list(pieces), list(swapped), expert_gate, expert_up, expert_down)

    def meet(ra, lb, plus, minus):
        return add(ra, plus[slot_half:]), add(lb, minus[slot_half:])

    payload, prefilled = hold(payload, fresh_cache)
    held = steps_y(payload)
    moving = stage(quarters(pack_kernel, position, fresh_cut(prefilled[0].T), smem=1), "x")
    held, moving = hold(held, moving)
    parts, weight0 = select(0, held)
    parts = steps_z(parts, 1)
    parts1, weight1 = select(1, held)
    moving = stage(regroup(False, moving), "y")
    parts, weight0, parts1, weight1, moving = hold(parts, weight0, parts1, weight1, moving)
    own = assemble(parts)
    near = ring_x(own)
    parts = steps_z(parts1, 1)
    moving = regroup(True, moving)
    own, near, parts, moving = hold(own, near, parts, moving)
    far = far_x(*near)
    around_own = jnp.concatenate([own, *near], axis=0)
    near_swapped = swap(around_own)
    own1 = assemble(parts)
    around_own, far, near_swapped, own1, moving = hold(around_own, far, near_swapped, own1, moving)
    moving = stage(moving, "z")
    near1 = ring_x(own1)
    far_swapped = [swap(piece) for piece in far]
    kept0, sent0 = run_experts([around_own, *far], [near_swapped, *far_swapped])
    own1, near1, kept0, sent0, moving = hold(own1, near1, kept0, sent0, moving)
    far = far_x(*near1)
    got0 = swap(sent0)
    around_own = jnp.concatenate([own1, *near1], axis=0)
    near_swapped = swap(around_own)
    own0, lb0, ra0, plus0, minus0 = pair_sums(kept0, got0)
    here = jnp.concatenate(moving, axis=0)
    moving = quarters(sort_kernel, fresh_order, position, here, swap(here), smem=2)
    far, near_swapped, around_own, own0, lb0, ra0, plus0, minus0, moving = hold(
        far, near_swapped, around_own, own0, lb0, ra0, plus0, minus0, moving
    )
    plus0, minus0 = shift(plus0, "x", 1), shift(minus0, "x", 3)
    far_swapped = [swap(piece) for piece in far]
    kept1, sent1 = run_experts([around_own, *far], [near_swapped, *far_swapped])
    moving = stage(moving, "z")
    plus0, minus0, kept1, sent1, moving = hold(plus0, minus0, kept1, sent1, moving)
    ra0, lb0 = meet(ra0, lb0, plus0, minus0)
    la0, rb0 = shift(ra0, "x", 1), shift(lb0, "x", 3)
    got1, moving = hold(swap(sent1), moving)
    moving = stage(regroup(False, moving), "y")
    own1, lb1, ra1, plus1, minus1 = pair_sums(kept1, got1)
    la0, rb0, own1, lb1, ra1, plus1, minus1, moving = hold(
        la0, rb0, own1, lb1, ra1, plus1, minus1, moving
    )
    plus1, minus1 = shift(plus1, "x", 1), shift(minus1, "x", 3)
    parts = steps_z(finish(own0, plus0, minus0, la0, rb0), -1)
    moving = regroup(True, moving)
    past_resident = past(cache_len, query_t, resident_t, score_scale, 0)
    plus1, minus1, parts0, moving, past_resident = hold(plus1, minus1, parts, moving, past_resident)
    ra1, lb1 = meet(ra1, lb1, plus1, minus1)
    la1, rb1 = shift(ra1, "x", 1), shift(lb1, "x", 3)
    mixed0 = back_y(*combine(weight0, parts0))
    la1, rb1, mixed0, moving = hold(la1, rb1, mixed0, moving)
    parts = steps_z(finish(own1, plus1, minus1, la1, rb1), -1)
    moving = stage(moving, "x")
    parts, moving, kv_t = hold(parts, moving, kv_down.T)
    other_down = swap(kv_t)
    mixed = [*mixed0, *back_y(*combine(weight1, parts))]
    (whole,) = call(unpack_kernel, [((SIDE**3, *moving[0].shape[1:]), bf16)], position, *moving, smem=1)
    fresh_t = fresh_join(whole, LAT + ROPE, fresh_cache.shape[1])[None]
    past_fresh = past(cache_len[resident_rows:], query_t, fresh_t, score_scale, resident_rows)
    mixed, past_fresh, other_down = hold(mixed, past_fresh, other_down)

    many = steps_count * BLOCK
    layer, keys = call(
        project_kernel,
        [((local_rows * steps_count * model_width // 128, 128), bf16), ((many, LAT + ROPE), bf16)],
        core, cache_len, hidden_rows, *mixed, attn_gain[None], kv_t, other_down, kv_gain[None],
        smem=2, limit=18, scratch=[pltpu.VMEM((many * model_width // 128, 128), f32)],
    )
    tall = model_width // 128
    layer = layer.reshape(local_rows, tall, steps_count, 128)
    layer_out = layer.transpose(2, 0, 1, 3).reshape(steps_count, local_rows, model_width)
    new_keys = jnp.pad(
        keys.reshape(steps_count, BLOCK, LAT + ROPE).swapaxes(0, 1), ((0, 0), (0, BLOCK - steps_count), (0, 0))
    )
    attended = merge(query_t, new_keys, past_resident, past_fresh, score_scale)
    attended = attended.reshape(local_rows, -1, steps_count, 128).transpose(2, 0, 1, 3)
    return layer_out, attended.reshape(steps_count, local_rows, -1)


def solution(mesh):
    grid = Mesh(mesh.devices.reshape(2, 4, 4, 4), ("c", "y", "z", "x"))
    every = ("c", "y", "z", "x")
    placed = (
        P(None, every, None),
        P(),
        P(),
        P(),
        P(None, every, None),
        P(None, every, None),
        P(every, None, None),
        P(every, None, None),
        P(every, None, None),
        P("c", None),
        P(every, None, None),
        P(every, None, None),
        P(),
        P(every),
        P(None, every, None, None),
    )
    return jax.shard_map(
        shards,
        mesh=grid,
        in_specs=placed,
        out_specs=(P(None, every, None), P(None, every, None)),
        check_vma=False,
    )
```

```python
import functools

import jax
import jax.numpy as jnp
import numpy as np
from jax import lax
from jax.experimental import pallas as pl
from jax.experimental.pallas import tpu as pltpu
from jax.sharding import Mesh, PartitionSpec as P

LAT = 512
ROPE = 64
NOPE = 128
EXPERTS = 16
CAP = 3
BLOCK = 8
META = 128
SIDE = 4
PART = SIDE * CAP
SLOTS = SIDE * PART


epsilon = 1e-06
route_scaling = 2.5
rope_base = 10000.0
masked_score = -1e30
f32 = jnp.float32
bf16 = jnp.bfloat16
NT = (((1,), (1,)), ((), ()))
TN = (((0,), (0,)), ((), ()))


def rms_scale(values, gain_vector):
    values = values.astype(f32)
    return (
        values
        * lax.rsqrt(jnp.mean(values * values, axis=-1, keepdims=True) + epsilon)
        * gain_vector
    )


def shift(values, axis, by):
    size = lax.axis_size(axis)
    return lax.ppermute(values, axis, [(i, (i + by) % size) for i in range(size)])


def add(*terms):
    return sum(term.astype(f32) for term in terms).astype(bf16)


def swap(values):
    return shift(values, "c", 1)


def dot(a, b, dims=(((1,), (0,)), ((), ()))):
    return lax.dot_general(a, b, dims, preferred_element_type=f32)


def call(kernel, outs, *args, smem=0, flops=0, limit=12, scratch=()):
    specs = [pl.BlockSpec(memory_space=pltpu.SMEM)] * smem
    specs += [pl.BlockSpec(memory_space=pltpu.VMEM)] * (len(args) - smem)
    moved = sum(a.size * a.dtype.itemsize for a in args)
    return pl.pallas_call(
        kernel,
        out_shape=[jax.ShapeDtypeStruct(shape, dtype) for shape, dtype in outs],
        in_specs=specs,
        out_specs=[pl.BlockSpec(memory_space=pltpu.VMEM)] * len(outs),
        scratch_shapes=list(scratch),
        compiler_params=pltpu.CompilerParams(vmem_limit_bytes=limit * 2**20),
        cost_estimate=pl.CostEstimate(flops=flops, bytes_accessed=moved, transcendentals=0),
    )(*args)


def row_of(shape, dim):
    return lax.broadcasted_iota(jnp.int32, shape, dim)


def digits(value, base, count):
    high = sum(jnp.where(value >= base * i, 1, 0) for i in range(1, count))
    return high, value - base * high


def placed(half, block):
    slot = row_of((SLOTS, 2 * PART), 0) - block * PART
    return jnp.where((row_of((SLOTS, 2 * PART), 1) - half * PART == slot) & (slot >= 0) & (slot < PART), 1.0, 0.0).astype(bf16)


def prepare_kernel(ids, route, hidden, gain, out, plain):
    count, steps, width = hidden.shape
    both = hidden[...].astype(f32)
    blank = jnp.zeros((META - EXPERTS, META), f32)
    spare = jnp.zeros((BLOCK - count, width), f32)
    normed, metas, held = [], [], []
    for t in range(steps):
        values = both[:, t, :]
        held += [values, spare]
        normed += [rms_scale(values, gain[...]), spare]
        share = route[t] / jnp.sum(route[t], axis=0, keepdims=True) * route_scaling
        expert = lax.broadcasted_iota(jnp.int32, (EXPERTS, count), 0)
        dense = jnp.zeros((EXPERTS, count), f32)
        for k in range(share.shape[0]):
            dense = dense + jnp.where(ids[t, k : k + 1] == expert, share[k : k + 1], 0.0)
        dense = jnp.concatenate([dense, jnp.zeros((EXPERTS, META - count), f32)], axis=1)
        dense = jnp.concatenate([dense, blank], axis=0).T
        high = dense.astype(bf16)
        low = (dense - high.astype(f32))[:, :EXPERTS].astype(bf16).astype(f32)
        meta = jnp.concatenate([high.astype(f32)[:, :EXPERTS], low, blank.T[:, EXPERTS:]], axis=1)
        metas.append(meta[:BLOCK])
    plain[...] = jnp.concatenate(held, axis=0).astype(bf16)
    out[:, :width] = jnp.concatenate(normed, axis=0).astype(bf16)
    out[:, width:] = jnp.concatenate(metas, axis=0).astype(bf16)


def select_kernel(step, place, b0, b1, b2, b3, o0, o1, o2, o3, weights):
    mine = slice(step * BLOCK, (step + 1) * BLOCK)
    held = jnp.concatenate([b[...].astype(f32)[mine] for b in (b0, b1, b2, b3)], axis=0)
    width = held.shape[1] - META
    half = width // 2
    many = SIDE * 2 * PART
    count = SIDE * BLOCK
    meta = held[:, width:]
    named = jnp.where((meta > 0) & (row_of(meta.shape, 1) < EXPERTS), 1.0, 0.0).astype(bf16)
    meta = meta.astype(bf16)
    later, sooner = row_of((count, count), 0), row_of((count, count), 1)
    same = digits(later, BLOCK, SIDE)[0] == digits(sooner, BLOCK, SIDE)[0]
    before = dot(jnp.where(same & (sooner < later), 1.0, 0.0).astype(bf16), named).astype(bf16)
    block, rest = digits(row_of((many, META), 0), 2 * PART, SIDE)
    z = place[1] + block
    expert = place[0] * SIDE + jnp.where(z >= SIDE, z - SIDE, z)
    lane = row_of((many, META), 1)
    pick_high = jnp.where(lane == expert, 1.0, 0.0).astype(bf16)
    pick_low = jnp.where(lane == expert + EXPERTS, 1.0, 0.0).astype(bf16)
    _, rest = digits(row_of((many, count), 0), 2 * PART, SIDE)
    second, slot = digits(rest, PART, 2)
    source, turn = digits(slot, CAP, SIDE)
    owner = digits(row_of((many, count), 1), BLOCK, SIDE)[0]
    here = (
        (dot(pick_high, named, NT) > 0.5)
        & (dot(pick_high, before, NT) == turn.astype(f32))
        & (source == owner)
    )
    sel = jnp.where(here, 1.0, 0.0)
    low_half = jnp.where(second > 0, 0.0, sel).astype(bf16)
    high_half = jnp.where(second > 0, sel, 0.0).astype(bf16)
    weights[0] = jnp.where(here, dot(pick_high, meta, NT), 0.0)
    weights[1] = jnp.where(here, dot(pick_low, meta, NT), 0.0)
    slots = dot(low_half, held[:, :half].astype(bf16)) + dot(high_half, held[:, half:width].astype(bf16))
    for i, o in enumerate((o0, o1, o2, o3)):
        o[...] = slots[i * 2 * PART : (i + 1) * 2 * PART].astype(bf16)


def assemble_kernel(f0, f1, f2, f3, out):
    half = f0.shape[1]
    for h in range(2):
        total = 0.0
        for i, f in enumerate((f0, f1, f2, f3)):
            total = total + dot(placed(h, i), f[...])
        out[:, h * half : (h + 1) * half] = total.astype(bf16)


def finish_kernel(own, plus, minus, la, rb, o0, o1, o2, o3):
    quarter = la.shape[0]
    half = own.shape[1] // 2
    total = [0.0] * SIDE
    for h in range(2):
        cols = slice(h * half, (h + 1) * half)
        mine = own[:, cols].astype(f32)
        first = mine[:quarter] + la[:, cols].astype(f32) + minus[:, cols].astype(f32)[:quarter]
        second = mine[quarter:] + plus[:, cols].astype(f32)[:quarter] + rb[:, cols].astype(f32)
        summed = jnp.concatenate([first, second], axis=0).astype(bf16)
        for i in range(SIDE):
            total[i] = total[i] + dot(placed(h, i), summed, TN)
    for i, o in enumerate((o0, o1, o2, o3)):
        o[...] = total[i].astype(bf16)


def pair_kernel(kept, got, own, lb, ra, plus, minus):
    total = kept[...].astype(f32) + got[...].astype(f32)
    quarter = lb.shape[0]
    piece = [total[i * quarter : (i + 1) * quarter] for i in range(8)]
    own[...] = total[: 2 * quarter].astype(bf16)
    lb[...] = piece[3].astype(bf16)
    ra[...] = piece[4].astype(bf16)
    plus[...] = jnp.concatenate([piece[5], piece[6]], axis=0).astype(bf16)
    minus[...] = jnp.concatenate([piece[2], piece[7]], axis=0).astype(bf16)


def pair_sums(kept, got):
    many, width = kept.shape
    rows = (many // 4, many // 8, many // 8, many // 4, many // 4)
    chunk = 1024
    return pl.pallas_call(
        pair_kernel,
        grid=(width // chunk,),
        out_shape=[jax.ShapeDtypeStruct((r, width), bf16) for r in rows],
        in_specs=[pl.BlockSpec((many, chunk), lambda s: (0, s))] * 2,
        out_specs=[pl.BlockSpec((r, chunk), lambda s: (0, s)) for r in rows],
        compiler_params=pltpu.CompilerParams(vmem_limit_bytes=16 * 2**20),
        cost_estimate=pl.CostEstimate(flops=many * width, bytes_accessed=6 * many * width, transcendentals=0),
    )(kept, got)


def weighted(weights, parts, h):
    second = row_of((2 * PART, SIDE * BLOCK), 0) >= PART
    mine = second if h else jnp.logical_not(second)
    total = 0.0
    for i in range(SIDE):
        rows = slice(i * 2 * PART, (i + 1) * 2 * PART)
        for k in range(2):
            share = jnp.where(mine, weights[k, rows], 0.0).astype(bf16)
            total = total + dot(share, parts[i][...], TN)
    return total


def combine_kernel(weights, f0, f1, f2, f3, own, o1, o2, o3):
    half = f0.shape[1]
    for h in range(2):
        cols = slice(h * half, (h + 1) * half)
        total = weighted(weights, (f0, f1, f2, f3), h)
        for i, o in enumerate((own, o1, o2, o3)):
            o[:, cols] = total[i * BLOCK : (i + 1) * BLOCK].astype(o.dtype)


CHUNK = 1792


def expert_kernel(pieces, chunks, *refs):
    xs, others = refs[:pieces], refs[pieces : 2 * pieces]
    gate, up, down, mine, theirs, rows, gate_sum, up_sum, active = refs[2 * pieces :]
    step = pl.program_id(0)

    @pl.when(step == 0)
    def _():
        gate_sum[...] = jnp.zeros_like(gate_sum)
        up_sum[...] = jnp.zeros_like(up_sum)

    @pl.when(step < chunks)
    def _():
        at = 0
        for x in xs + others:
            rows[at : at + x.shape[0]] = x[...]
            at += x.shape[0]
        gate_sum[...] += dot(rows[...], gate[0])
        up_sum[...] += dot(rows[...], up[0])

    @pl.when(step == chunks)
    def _():
        value = gate_sum[...]
        active[...] = (value / (1.0 + jnp.exp(-value)) * up_sum[...]).astype(bf16)

    @pl.when(step >= chunks)
    def _():
        many = mine.shape[0]
        result = dot(active[...], down[0])
        mine[...] = result[:many].astype(bf16)
        theirs[...] = result[many:].astype(bf16)


def experts(xs, others, gate, up, down):
    pieces = len(xs)
    many = sum(x.shape[0] for x in xs)
    width, units = gate.shape[1:]
    chunks = width // CHUNK

    def first(s):
        return jnp.minimum(s, chunks - 1)

    def second(s):
        return jnp.maximum(s - chunks, 0)

    in_specs = [pl.BlockSpec((x.shape[0], CHUNK), lambda s: (0, first(s))) for x in xs + others]
    in_specs += [pl.BlockSpec((1, CHUNK, units), lambda s: (0, first(s), 0))] * 2
    in_specs += [pl.BlockSpec((1, units, CHUNK), lambda s: (0, 0, second(s)))]
    return pl.pallas_call(
        functools.partial(expert_kernel, pieces, chunks),
        grid=(2 * chunks,),
        out_shape=[jax.ShapeDtypeStruct((many, width), bf16)] * 2,
        in_specs=in_specs,
        out_specs=[pl.BlockSpec((many, CHUNK), lambda s: (0, second(s)))] * 2,
        scratch_shapes=[
            pltpu.VMEM((2 * many, CHUNK), bf16),
            pltpu.VMEM((2 * many, units), f32),
            pltpu.VMEM((2 * many, units), f32),
            pltpu.VMEM((2 * many, units), bf16),
        ],
        compiler_params=pltpu.CompilerParams(vmem_limit_bytes=20 * 2**20),
        cost_estimate=pl.CostEstimate(
            flops=12 * many * width * units, bytes_accessed=6 * width * units + 8 * many * width, transcendentals=0
        ),
    )(*xs, *others, gate, up, down)


def past_kernel(scale, lengths, queries, keys, acc, top, total):
    request = pl.program_id(0)
    length = lengths[request]
    held = keys[0]
    steps = queries.shape[0]
    for t in range(steps):
        scores = dot(queries[t, 0], held, TN) * scale
        lane = lax.broadcasted_iota(jnp.int32, scores.shape, 1)
        visible = lane < length
        scores = jnp.where(visible, scores, masked_score)
        highest = jnp.max(scores, axis=-1, keepdims=True)
        weight = jnp.where(visible, jnp.exp(scores - highest), 0.0)
        acc[0, t] = dot(weight.astype(bf16), held[:LAT], NT)
        top[0, t] = highest
        total[0, t] = jnp.sum(weight, axis=-1, keepdims=True)


def past(lengths, queries, keys, scale, start):
    count, width, context = keys.shape
    steps, _, _, heads = queries.shape
    return pl.pallas_call(
        functools.partial(past_kernel, scale),
        grid_spec=pltpu.PrefetchScalarGridSpec(
            num_scalar_prefetch=1,
            grid=(count,),
            in_specs=[
                pl.BlockSpec((steps, 1, width, heads), lambda r, _: (0, r + start, 0, 0)),
                pl.BlockSpec((1, width, context), lambda r, _: (r, 0, 0)),
            ],
            out_specs=[
                pl.BlockSpec((1, steps, heads, LAT), lambda r, _: (r, 0, 0, 0)),
                pl.BlockSpec((1, steps, heads, 1), lambda r, _: (r, 0, 0, 0)),
                pl.BlockSpec((1, steps, heads, 1), lambda r, _: (r, 0, 0, 0)),
            ],
        ),
        out_shape=[
            jax.ShapeDtypeStruct((count, steps, heads, LAT), f32),
            jax.ShapeDtypeStruct((count, steps, heads, 1), f32),
            jax.ShapeDtypeStruct((count, steps, heads, 1), f32),
        ],
        compiler_params=pltpu.CompilerParams(vmem_limit_bytes=12 * 2**20),
        cost_estimate=pl.CostEstimate(
            flops=2 * count * steps * heads * context * (width + LAT),
            bytes_accessed=count * (2 * width * (context + steps * heads) + 4 * steps * heads * LAT),
            transcendentals=count * steps * heads * context,
        ),
    )(lengths, queries, keys)


def merge_kernel(scale, queries, keys, acc, top, total, last_acc, last_top, last_total, out, rows):
    steps, count, _, heads = queries.shape
    lanes = LAT // 128
    early = acc.shape[0]
    new_keys = keys[...].astype(f32)
    for r in range(count):
        held = (acc, top, total, r) if r < early else (last_acc, last_top, last_total, r - early)
        mine = jnp.concatenate([new_keys[t * BLOCK + r : t * BLOCK + r + 1] for t in range(steps)], axis=0)
        padded = jnp.concatenate([mine, jnp.zeros((16 - steps, mine.shape[1]), f32)], axis=0).astype(bf16)
        for t in range(steps):
            raw = dot(padded, queries[t, r]) * scale
            own = jnp.concatenate([raw, jnp.zeros((heads - 16, heads), f32)], axis=0).T
            highest = held[1][held[3], t]
            columns = [own[:, k : k + 1] for k in range(t + 1)]
            peak = highest
            for column in columns:
                peak = jnp.maximum(peak, column)
            keep = jnp.exp(highest - peak)
            weights = [jnp.exp(column - peak) for column in columns]
            below = held[2][held[3], t] * keep + sum(weights)
            value = held[0][held[3], t] * (keep / below)
            for k in range(t + 1):
                share = (weights[k] / below).astype(bf16).astype(f32)
                value = value + share * mine[k : k + 1, :LAT]
            for j in range(lanes):
                rows[r % 2, pl.ds(j * steps + t, heads, stride=lanes * steps), :] = value[:, j * 128 : (j + 1) * 128]
        out[r] = rows[r % 2].astype(bf16)


def merge(queries, keys, first, last, scale):
    steps, count, _, heads = queries.shape
    tall = heads * steps * LAT // 128
    return call(
        functools.partial(merge_kernel, scale), [((count, tall, 128), bf16)], queries, keys, *first, *last,
        limit=20, scratch=[pltpu.VMEM((2, tall, 128), f32)],
    )[0]


def project_kernel(core, lengths, hidden, own0, a0, b0, c0, own1, a1, b1, c1, gain, kv_own, kv_other, kv_gain, layer, keys, stage):
    mixture = jnp.concatenate(
        [
            own[...] + a[...].astype(f32) + b[...].astype(f32) + c[...].astype(f32)
            for own, a, b, c in ((own0, a0, b0, c0), (own1, a1, b1, c1))
        ],
        axis=0,
    )
    both = (hidden[...].astype(f32) + mixture).astype(bf16)
    many, width = both.shape
    wide = both.astype(f32)
    for k in range(width // 128):
        for t in range(2):
            stage[pl.ds(2 * k + t, BLOCK, stride=width // 64), :] = wide[
                t * BLOCK : (t + 1) * BLOCK, k * 128 : (k + 1) * 128
            ]
    layer[...] = stage[...].astype(bf16)
    normed = rms_scale(both, gain[...]).astype(bf16)
    half = normed.shape[1] // 2
    swapped = core[0] > 0
    low, high = normed[:, :half].astype(f32), normed[:, half:].astype(f32)
    first = jnp.where(swapped, high, low).astype(bf16)
    second = jnp.where(swapped, low, high).astype(bf16)
    projected = (dot(kv_own[...], first, NT) + dot(kv_other[...], second, NT)).T
    keys[:, :LAT] = rms_scale(projected[:, :LAT], kv_gain[...]).astype(bf16)
    rope = projected[:, LAT:]
    crossed = jnp.concatenate([-rope[:, ROPE // 2 :], rope[:, : ROPE // 2]], axis=1)
    step, row = digits(row_of(rope.shape, 0), BLOCK, many // BLOCK)
    position = step
    for r in range(lengths.shape[0]):
        position = position + jnp.where(row == r, lengths[r], 0)
    lane = row_of(rope.shape, 1)
    pair = jnp.where(lane < ROPE // 2, lane, lane - ROPE // 2).astype(f32)
    angle = position.astype(f32) * jnp.exp(pair * np.float32(-2.0 * np.log(rope_base) / ROPE))
    keys[:, LAT:] = (rope * jnp.cos(angle) + crossed * jnp.sin(angle)).astype(bf16)


def hold(*values):
    return lax.optimization_barrier(values)


def steps_y(mine):
    return [mine, shift(mine, "y", 1), shift(mine, "y", 3), shift(mine, "y", 2)]


def ring_x(own):
    return shift(own, "x", 1), shift(own, "x", 3)


def far_x(left, right):
    half = left.shape[0] // 2
    return [shift(left[:half], "x", 1), shift(right[half:], "x", 3)]


def steps_z(parts, sign):
    return [parts[0]] + [shift(parts[i], "z", sign * i % SIDE) for i in (1, 2, 3)]


CHIPS = ("y", "z", "x")


def fresh_cut(fresh_t):
    width, context = fresh_t.shape
    count = lax.axis_size(CHIPS)
    tiles = width * context // 1024
    each = -(-tiles // count)
    cut = fresh_t.reshape(width // 8, 8, context // 128, 128).swapaxes(1, 2).reshape(tiles, 8, 128)
    cut = jnp.pad(cut, ((0, each * count - tiles), (0, 0), (0, 0)))
    return cut.reshape(count, each * 8, 128)


def fresh_join(whole, width, context):
    tiles = width * context // 1024
    whole = whole.reshape(-1, 8, 128)[:tiles].reshape(width // 8, context // 128, 8, 128)
    return whole.swapaxes(1, 2).reshape(width, context)


def around(value):
    return jnp.where(value < 0, value + SIDE, jnp.where(value >= SIDE, value - SIDE, value))


def pack_kernel(place, cut, *outs):
    for kx in range(SIDE):
        for ky in range(SIDE):
            for kz in range(SIDE):
                y, z, x = around(place[0] + ky), around(place[1] + kz), around(place[2] + kx)
                outs[kx][ky * SIDE + kz] = cut[(y * SIDE + z) * SIDE + x]


def regroup_kernel(last, *refs):
    ins, outs = refs[:SIDE], refs[SIDE:]
    for a in range(SIDE):
        for b in range(SIDE):
            for c in range(SIDE):
                if last:
                    outs[c][b * SIDE + a] = ins[a][b * SIDE + c]
                else:
                    outs[b][a * SIDE + c] = ins[a][b * SIDE + c]


def sort_kernel(order, place, here, there, *outs):
    count = here.shape[0]
    for jz in range(SIDE):
        for jy in range(SIDE):
            for jx in range(SIDE):
                y, z, x = around(place[0] + jy), around(place[1] + jz), around(place[2] + jx)
                wanted = order[place[3] * count + (y * SIDE + z) * SIDE + x]
                upper = wanted >= count
                source = jnp.where(upper, wanted - count, wanted)
                sy, sz, sx = source >> 4, (source >> 2) & 3, source & 3
                kx, ky, kz = around(place[2] - sx), around(place[0] - sy), around(place[1] - sz)
                index = (kz * SIDE + kx) * SIDE + ky
                other = jnp.where(upper, 1, 0) != place[3]
                out = outs[jz].at[jy * SIDE + jx]

                @pl.when(other)
                def _(out=out, index=index):
                    out[...] = there[index]

                @pl.when(jnp.logical_not(other))
                def _(out=out, index=index):
                    out[...] = here[index]


def unpack_kernel(place, x0, x1, x2, x3, whole):
    for jx, part in enumerate((x0, x1, x2, x3)):
        for jz in range(SIDE):
            for jy in range(SIDE):
                y, z, x = around(place[0] - jy), around(place[1] - jz), around(place[2] - jx)
                whole[(y * SIDE + z) * SIDE + x] = part[jz * SIDE + jy]


def quarters(kernel, *args, smem=0):
    rows, lanes = args[-1].shape[1:]
    return call(kernel, [((SIDE * SIDE, rows, lanes), bf16)] * SIDE, *args, smem=smem)


def regroup(last, parts):
    return quarters(functools.partial(regroup_kernel, last), *parts)


def stage(parts, axis):
    return [parts[0], *[shift(parts[i], axis, i) for i in (1, 2, 3)]]


def shards(
    hidden_in,
    ffn_gain,
    attn_gain,
    kv_gain,
    expert_ids,
    route_weight,
    expert_gate,
    expert_up,
    expert_down,
    kv_down,
    resident_cache,
    fresh_cache,
    fresh_order,
    cache_len,
    queries,
):
    steps_count, local_rows, model_width = hidden_in.shape
    resident_rows = resident_cache.shape[0]
    score_scale = (NOPE + ROPE) ** (-0.5)
    core = lax.axis_index("c").astype(jnp.int32).reshape(1)

    payload, hidden_rows = call(
        prepare_kernel,
        [((steps_count * BLOCK, model_width + META), bf16), ((steps_count * BLOCK, model_width), bf16)],
        expert_ids.swapaxes(1, 2), route_weight.swapaxes(1, 2), hidden_in.swapaxes(0, 1), ffn_gain[None],
    )

    position = jnp.stack([lax.axis_index(axis) for axis in ("y", "z", "x", "c")]).astype(jnp.int32)
    folded = ((2 * PART, model_width // 2), bf16)
    query_t = queries.swapaxes(2, 3)
    resident_t = resident_cache.swapaxes(1, 2)

    slot_half = SLOTS // 2
    rows = (BLOCK, model_width)

    def select(step, held):
        *parts, weight = call(
            functools.partial(select_kernel, step), [folded] * SIDE + [((2, SIDE * 2 * PART, SIDE * BLOCK), f32)],
            position, *held, smem=1,
        )
        return parts, weight

    def assemble(parts):
        return call(assemble_kernel, [((SLOTS, model_width), bf16)], *parts)[0]

    def combine(weight, parts):
        return call(combine_kernel, [(rows, f32), (rows, bf16), (rows, bf16), (rows, bf16)], weight, *parts)

    def back_y(own, one, two, three):
        return [own, shift(one, "y", 3), shift(two, "y", 1), shift(three, "y", 2)]

    def finish(own, plus, minus, la, rb):
        return call(finish_kernel, [folded] * SIDE, own, plus, minus, la, rb)

    def run_experts(pieces, swapped):
        return experts(list(pieces), list(swapped), expert_gate, expert_up, expert_down)

    def meet(ra, lb, plus, minus):
        return add(ra, plus[slot_half:]), add(lb, minus[slot_half:])

    payload, prefilled = hold(payload, fresh_cache)
    held = steps_y(payload)
    moving = stage(quarters(pack_kernel, position, fresh_cut(prefilled[0].T), smem=1), "x")
    held, moving = hold(held, moving)
    parts, weight0 = select(0, held)
    parts = steps_z(parts, 1)
    parts1, weight1 = select(1, held)
    moving = stage(regroup(False, moving), "y")
    parts, weight0, parts1, weight1, moving = hold(parts, weight0, parts1, weight1, moving)
    own = assemble(parts)
    near = ring_x(own)
    parts = steps_z(parts1, 1)
    moving = regroup(True, moving)
    own, near, parts, moving = hold(own, near, parts, moving)
    far = far_x(*near)
    around_own = jnp.concatenate([own, *near], axis=0)
    near_swapped = swap(around_own)
    own1 = assemble(parts)
    around_own, far, near_swapped, own1, moving = hold(around_own, far, near_swapped, own1, moving)
    moving = stage(moving, "z")
    near1 = ring_x(own1)
    far_swapped = [swap(piece) for piece in far]
    kept0, sent0 = run_experts([around_own, *far], [near_swapped, *far_swapped])
    own1, near1, kept0, sent0, moving = hold(own1, near1, kept0, sent0, moving)
    far = far_x(*near1)
    got0 = swap(sent0)
    around_own = jnp.concatenate([own1, *near1], axis=0)
    near_swapped = swap(around_own)
    own0, lb0, ra0, plus0, minus0 = pair_sums(kept0, got0)
    here = jnp.concatenate(moving, axis=0)
    moving = quarters(sort_kernel, fresh_order, position, here, swap(here), smem=2)
    far, near_swapped, around_own, own0, lb0, ra0, plus0, minus0, moving = hold(
        far, near_swapped, around_own, own0, lb0, ra0, plus0, minus0, moving
    )
    plus0, minus0 = shift(plus0, "x", 1), shift(minus0, "x", 3)
    far_swapped = [swap(piece) for piece in far]
    kept1, sent1 = run_experts([around_own, *far], [near_swapped, *far_swapped])
    moving = stage(moving, "z")
    plus0, minus0, kept1, sent1, moving = hold(plus0, minus0, kept1, sent1, moving)
    ra0, lb0 = meet(ra0, lb0, plus0, minus0)
    la0, rb0 = shift(ra0, "x", 1), shift(lb0, "x", 3)
    got1, moving = hold(swap(sent1), moving)
    moving = stage(regroup(False, moving), "y")
    own1, lb1, ra1, plus1, minus1 = pair_sums(kept1, got1)
    la0, rb0, own1, lb1, ra1, plus1, minus1, moving = hold(
        la0, rb0, own1, lb1, ra1, plus1, minus1, moving
    )
    plus1, minus1 = shift(plus1, "x", 1), shift(minus1, "x", 3)
    parts = steps_z(finish(own0, plus0, minus0, la0, rb0), -1)
    moving = regroup(True, moving)
    past_resident = past(cache_len, query_t, resident_t, score_scale, 0)
    plus1, minus1, parts0, moving, past_resident = hold(plus1, minus1, parts, moving, past_resident)
    ra1, lb1 = meet(ra1, lb1, plus1, minus1)
    la1, rb1 = shift(ra1, "x", 1), shift(lb1, "x", 3)
    mixed0 = back_y(*combine(weight0, parts0))
    la1, rb1, mixed0, moving = hold(la1, rb1, mixed0, moving)
    parts = steps_z(finish(own1, plus1, minus1, la1, rb1), -1)
    moving = stage(moving, "x")
    parts, moving, kv_t = hold(parts, moving, kv_down.T)
    other_down = swap(kv_t)
    mixed = [*mixed0, *back_y(*combine(weight1, parts))]
    (whole,) = call(unpack_kernel, [((SIDE**3, *moving[0].shape[1:]), bf16)], position, *moving, smem=1)
    fresh_t = fresh_join(whole, LAT + ROPE, fresh_cache.shape[1])[None]
    past_fresh = past(cache_len[resident_rows:], query_t, fresh_t, score_scale, resident_rows)
    mixed, past_fresh, other_down = hold(mixed, past_fresh, other_down)

    many = steps_count * BLOCK
    layer, keys = call(
        project_kernel,
        [((many * model_width // 128, 128), bf16), ((many, LAT + ROPE), bf16)],
        core, cache_len, hidden_rows, *mixed, attn_gain[None], kv_t, other_down, kv_gain[None],
        smem=2, limit=18, scratch=[pltpu.VMEM((many * model_width // 128, 128), f32)],
    )
    tall = model_width // 128
    layer = layer[: local_rows * steps_count * tall].reshape(local_rows, tall, steps_count, 128)
    layer_out = layer.transpose(2, 0, 1, 3).reshape(steps_count, local_rows, model_width)
    attended = merge(query_t, keys, past_resident, past_fresh, score_scale)
    attended = attended.reshape(local_rows, -1, steps_count, 128).transpose(2, 0, 1, 3)
    return layer_out, attended.reshape(steps_count, local_rows, -1)


def solution(mesh):
    grid = Mesh(mesh.devices.reshape(2, 4, 4, 4), ("c", "y", "z", "x"))
    every = ("c", "y", "z", "x")
    placed = (
        P(None, every, None),
        P(),
        P(),
        P(),
        P(None, every, None),
        P(None, every, None),
        P(every, None, None),
        P(every, None, None),
        P(every, None, None),
        P("c", None),
        P(every, None, None),
        P(every, None, None),
        P(),
        P(every),
        P(None, every, None, None),
    )
    return jax.shard_map(
        shards,
        mesh=grid,
        in_specs=placed,
        out_specs=(P(None, every, None), P(None, every, None)),
        check_vma=False,
    )
```

```python
import functools

import jax
import jax.numpy as jnp
import numpy as np
from jax import lax
from jax.experimental import pallas as pl
from jax.experimental.pallas import tpu as pltpu
from jax.sharding import Mesh, PartitionSpec as P

LAT = 512
ROPE = 64
NOPE = 128
EXPERTS = 16
CAP = 3
BLOCK = 8
META = 128
SIDE = 4
PART = SIDE * CAP
SLOTS = SIDE * PART


epsilon = 1e-06
route_scaling = 2.5
rope_base = 10000.0
masked_score = -1e30
f32 = jnp.float32
bf16 = jnp.bfloat16
NT = (((1,), (1,)), ((), ()))
TN = (((0,), (0,)), ((), ()))


def rms_scale(values, gain_vector):
    values = values.astype(f32)
    return (
        values
        * lax.rsqrt(jnp.mean(values * values, axis=-1, keepdims=True) + epsilon)
        * gain_vector
    )


def shift(values, axis, by):
    size = lax.axis_size(axis)
    return lax.ppermute(values, axis, [(i, (i + by) % size) for i in range(size)])


def add(*terms):
    return sum(term.astype(f32) for term in terms).astype(bf16)


def swap(values):
    return shift(values, "c", 1)


def dot(a, b, dims=(((1,), (0,)), ((), ()))):
    return lax.dot_general(a, b, dims, preferred_element_type=f32)


def call(kernel, outs, *args, smem=0, flops=0, limit=12, scratch=()):
    specs = [pl.BlockSpec(memory_space=pltpu.SMEM)] * smem
    specs += [pl.BlockSpec(memory_space=pltpu.VMEM)] * (len(args) - smem)
    moved = sum(a.size * a.dtype.itemsize for a in args)
    return pl.pallas_call(
        kernel,
        out_shape=[jax.ShapeDtypeStruct(shape, dtype) for shape, dtype in outs],
        in_specs=specs,
        out_specs=[pl.BlockSpec(memory_space=pltpu.VMEM)] * len(outs),
        scratch_shapes=list(scratch),
        compiler_params=pltpu.CompilerParams(vmem_limit_bytes=limit * 2**20),
        cost_estimate=pl.CostEstimate(flops=flops, bytes_accessed=moved, transcendentals=0),
    )(*args)


def row_of(shape, dim):
    return lax.broadcasted_iota(jnp.int32, shape, dim)


def digits(value, base, count):
    high = sum(jnp.where(value >= base * i, 1, 0) for i in range(1, count))
    return high, value - base * high


def placed(half, block):
    slot = row_of((SLOTS, 2 * PART), 0) - block * PART
    return jnp.where((row_of((SLOTS, 2 * PART), 1) - half * PART == slot) & (slot >= 0) & (slot < PART), 1.0, 0.0).astype(bf16)


def prepare_kernel(ids, route, hidden, gain, out, plain):
    count, steps, width = hidden.shape
    both = hidden[...].astype(f32)
    blank = jnp.zeros((META - EXPERTS, META), f32)
    spare = jnp.zeros((BLOCK - count, width), f32)
    normed, metas, held = [], [], []
    for t in range(steps):
        values = both[:, t, :]
        held += [values, spare]
        normed += [rms_scale(values, gain[...]), spare]
        share = route[t] / jnp.sum(route[t], axis=0, keepdims=True) * route_scaling
        expert = lax.broadcasted_iota(jnp.int32, (EXPERTS, count), 0)
        dense = jnp.zeros((EXPERTS, count), f32)
        for k in range(share.shape[0]):
            dense = dense + jnp.where(ids[t, k : k + 1] == expert, share[k : k + 1], 0.0)
        dense = jnp.concatenate([dense, jnp.zeros((EXPERTS, META - count), f32)], axis=1)
        dense = jnp.concatenate([dense, blank], axis=0).T
        high = dense.astype(bf16)
        low = (dense - high.astype(f32))[:, :EXPERTS].astype(bf16).astype(f32)
        meta = jnp.concatenate([high.astype(f32)[:, :EXPERTS], low, blank.T[:, EXPERTS:]], axis=1)
        metas.append(meta[:BLOCK])
    plain[...] = jnp.concatenate(held, axis=0).astype(bf16)
    out[:, :width] = jnp.concatenate(normed, axis=0).astype(bf16)
    out[:, width:] = jnp.concatenate(metas, axis=0).astype(bf16)


def select_kernel(step, place, b0, b1, b2, b3, o0, o1, o2, o3, weights):
    mine = slice(step * BLOCK, (step + 1) * BLOCK)
    held = jnp.concatenate([b[...].astype(f32)[mine] for b in (b0, b1, b2, b3)], axis=0)
    width = held.shape[1] - META
    half = width // 2
    many = SIDE * 2 * PART
    count = SIDE * BLOCK
    meta = held[:, width:]
    named = jnp.where((meta > 0) & (row_of(meta.shape, 1) < EXPERTS), 1.0, 0.0).astype(bf16)
    meta = meta.astype(bf16)
    later, sooner = row_of((count, count), 0), row_of((count, count), 1)
    same = digits(later, BLOCK, SIDE)[0] == digits(sooner, BLOCK, SIDE)[0]
    before = dot(jnp.where(same & (sooner < later), 1.0, 0.0).astype(bf16), named).astype(bf16)
    block, rest = digits(row_of((many, META), 0), 2 * PART, SIDE)
    z = place[1] + block
    expert = place[0] * SIDE + jnp.where(z >= SIDE, z - SIDE, z)
    lane = row_of((many, META), 1)
    pick_high = jnp.where(lane == expert, 1.0, 0.0).astype(bf16)
    pick_low = jnp.where(lane == expert + EXPERTS, 1.0, 0.0).astype(bf16)
    _, rest = digits(row_of((many, count), 0), 2 * PART, SIDE)
    second, slot = digits(rest, PART, 2)
    source, turn = digits(slot, CAP, SIDE)
    owner = digits(row_of((many, count), 1), BLOCK, SIDE)[0]
    here = (
        (dot(pick_high, named, NT) > 0.5)
        & (dot(pick_high, before, NT) == turn.astype(f32))
        & (source == owner)
    )
    sel = jnp.where(here, 1.0, 0.0)
    low_half = jnp.where(second > 0, 0.0, sel).astype(bf16)
    high_half = jnp.where(second > 0, sel, 0.0).astype(bf16)
    weights[0] = jnp.where(here, dot(pick_high, meta, NT), 0.0)
    weights[1] = jnp.where(here, dot(pick_low, meta, NT), 0.0)
    slots = dot(low_half, held[:, :half].astype(bf16)) + dot(high_half, held[:, half:width].astype(bf16))
    for i, o in enumerate((o0, o1, o2, o3)):
        o[...] = slots[i * 2 * PART : (i + 1) * 2 * PART].astype(bf16)


def assemble_kernel(f0, f1, f2, f3, out):
    half = f0.shape[1]
    for h in range(2):
        total = 0.0
        for i, f in enumerate((f0, f1, f2, f3)):
            total = total + dot(placed(h, i), f[...])
        out[:, h * half : (h + 1) * half] = total.astype(bf16)


def finish_kernel(own, plus, minus, la, rb, o0, o1, o2, o3):
    quarter = la.shape[0]
    half = own.shape[1] // 2
    total = [0.0] * SIDE
    for h in range(2):
        cols = slice(h * half, (h + 1) * half)
        mine = own[:, cols].astype(f32)
        first = mine[:quarter] + la[:, cols].astype(f32) + minus[:, cols].astype(f32)[:quarter]
        second = mine[quarter:] + plus[:, cols].astype(f32)[:quarter] + rb[:, cols].astype(f32)
        summed = jnp.concatenate([first, second], axis=0).astype(bf16)
        for i in range(SIDE):
            total[i] = total[i] + dot(placed(h, i), summed, TN)
    for i, o in enumerate((o0, o1, o2, o3)):
        o[...] = total[i].astype(bf16)


def pair_kernel(kept, got, own, lb, ra, plus, minus):
    total = kept[...].astype(f32) + got[...].astype(f32)
    quarter = lb.shape[0]
    piece = [total[i * quarter : (i + 1) * quarter] for i in range(8)]
    own[...] = total[: 2 * quarter].astype(bf16)
    lb[...] = piece[3].astype(bf16)
    ra[...] = piece[4].astype(bf16)
    plus[...] = jnp.concatenate([piece[5], piece[6]], axis=0).astype(bf16)
    minus[...] = jnp.concatenate([piece[2], piece[7]], axis=0).astype(bf16)


def pair_sums(kept, got):
    many, width = kept.shape
    rows = (many // 4, many // 8, many // 8, many // 4, many // 4)
    chunk = 1024
    return pl.pallas_call(
        pair_kernel,
        grid=(width // chunk,),
        out_shape=[jax.ShapeDtypeStruct((r, width), bf16) for r in rows],
        in_specs=[pl.BlockSpec((many, chunk), lambda s: (0, s))] * 2,
        out_specs=[pl.BlockSpec((r, chunk), lambda s: (0, s)) for r in rows],
        compiler_params=pltpu.CompilerParams(vmem_limit_bytes=16 * 2**20),
        cost_estimate=pl.CostEstimate(flops=many * width, bytes_accessed=6 * many * width, transcendentals=0),
    )(kept, got)


def weighted(weights, parts, h):
    second = row_of((2 * PART, SIDE * BLOCK), 0) >= PART
    mine = second if h else jnp.logical_not(second)
    total = 0.0
    for i in range(SIDE):
        rows = slice(i * 2 * PART, (i + 1) * 2 * PART)
        for k in range(2):
            share = jnp.where(mine, weights[k, rows], 0.0).astype(bf16)
            total = total + dot(share, parts[i][...], TN)
    return total


def combine_kernel(weights, f0, f1, f2, f3, own, o1, o2, o3):
    half = f0.shape[1]
    for h in range(2):
        cols = slice(h * half, (h + 1) * half)
        total = weighted(weights, (f0, f1, f2, f3), h)
        for i, o in enumerate((own, o1, o2, o3)):
            o[:, cols] = total[i * BLOCK : (i + 1) * BLOCK].astype(o.dtype)


CHUNK = 1792


def expert_kernel(pieces, chunks, *refs):
    xs, others = refs[:pieces], refs[pieces : 2 * pieces]
    gate, up, down, mine, theirs, rows, gate_sum, up_sum, active = refs[2 * pieces :]
    step = pl.program_id(0)

    @pl.when(step == 0)
    def _():
        gate_sum[...] = jnp.zeros_like(gate_sum)
        up_sum[...] = jnp.zeros_like(up_sum)

    @pl.when(step < chunks)
    def _():
        at = 0
        for x in xs + others:
            rows[at : at + x.shape[0]] = x[...]
            at += x.shape[0]
        gate_sum[...] += dot(rows[...], gate[0])
        up_sum[...] += dot(rows[...], up[0])

    @pl.when(step == chunks)
    def _():
        value = gate_sum[...]
        active[...] = (value / (1.0 + jnp.exp(-value)) * up_sum[...]).astype(bf16)

    @pl.when(step >= chunks)
    def _():
        many = mine.shape[0]
        result = dot(active[...], down[0])
        mine[...] = result[:many].astype(bf16)
        theirs[...] = result[many:].astype(bf16)


def experts(xs, others, gate, up, down):
    pieces = len(xs)
    many = sum(x.shape[0] for x in xs)
    width, units = gate.shape[1:]
    chunks = width // CHUNK

    def first(s):
        return jnp.minimum(s, chunks - 1)

    def second(s):
        return jnp.maximum(s - chunks, 0)

    in_specs = [pl.BlockSpec((x.shape[0], CHUNK), lambda s: (0, first(s))) for x in xs + others]
    in_specs += [pl.BlockSpec((1, CHUNK, units), lambda s: (0, first(s), 0))] * 2
    in_specs += [pl.BlockSpec((1, units, CHUNK), lambda s: (0, 0, second(s)))]
    return pl.pallas_call(
        functools.partial(expert_kernel, pieces, chunks),
        grid=(2 * chunks,),
        out_shape=[jax.ShapeDtypeStruct((many, width), bf16)] * 2,
        in_specs=in_specs,
        out_specs=[pl.BlockSpec((many, CHUNK), lambda s: (0, second(s)))] * 2,
        scratch_shapes=[
            pltpu.VMEM((2 * many, CHUNK), bf16),
            pltpu.VMEM((2 * many, units), f32),
            pltpu.VMEM((2 * many, units), f32),
            pltpu.VMEM((2 * many, units), bf16),
        ],
        compiler_params=pltpu.CompilerParams(vmem_limit_bytes=20 * 2**20),
        cost_estimate=pl.CostEstimate(
            flops=12 * many * width * units, bytes_accessed=6 * width * units + 8 * many * width, transcendentals=0
        ),
    )(*xs, *others, gate, up, down)


def past_kernel(scale, lengths, queries, keys, acc, top, total):
    request = pl.program_id(0)
    length = lengths[request]
    held = keys[0]
    steps = queries.shape[0]
    for t in range(steps):
        scores = dot(queries[t, 0], held, TN) * scale
        lane = lax.broadcasted_iota(jnp.int32, scores.shape, 1)
        visible = lane < length
        scores = jnp.where(visible, scores, masked_score)
        highest = jnp.max(scores, axis=-1, keepdims=True)
        weight = jnp.where(visible, jnp.exp(scores - highest), 0.0)
        acc[0, t] = dot(weight.astype(bf16), held[:LAT], NT)
        top[0, t] = highest
        total[0, t] = jnp.sum(weight, axis=-1, keepdims=True)


def past(lengths, queries, keys, scale, start):
    count, width, context = keys.shape
    steps, _, _, heads = queries.shape
    return pl.pallas_call(
        functools.partial(past_kernel, scale),
        grid_spec=pltpu.PrefetchScalarGridSpec(
            num_scalar_prefetch=1,
            grid=(count,),
            in_specs=[
                pl.BlockSpec((steps, 1, width, heads), lambda r, _: (0, r + start, 0, 0)),
                pl.BlockSpec((1, width, context), lambda r, _: (r, 0, 0)),
            ],
            out_specs=[
                pl.BlockSpec((1, steps, heads, LAT), lambda r, _: (r, 0, 0, 0)),
                pl.BlockSpec((1, steps, heads, 1), lambda r, _: (r, 0, 0, 0)),
                pl.BlockSpec((1, steps, heads, 1), lambda r, _: (r, 0, 0, 0)),
            ],
        ),
        out_shape=[
            jax.ShapeDtypeStruct((count, steps, heads, LAT), f32),
            jax.ShapeDtypeStruct((count, steps, heads, 1), f32),
            jax.ShapeDtypeStruct((count, steps, heads, 1), f32),
        ],
        compiler_params=pltpu.CompilerParams(vmem_limit_bytes=12 * 2**20),
        cost_estimate=pl.CostEstimate(
            flops=2 * count * steps * heads * context * (width + LAT),
            bytes_accessed=count * (2 * width * (context + steps * heads) + 4 * steps * heads * LAT),
            transcendentals=count * steps * heads * context,
        ),
    )(lengths, queries, keys)


def merge_kernel(scale, queries, keys, acc, top, total, last_acc, last_top, last_total, out, rows):
    steps, count, _, heads = queries.shape
    lanes = LAT // 128
    early = acc.shape[0]
    new_keys = keys[...].astype(f32)
    for r in range(count):
        held = (acc, top, total, r) if r < early else (last_acc, last_top, last_total, r - early)
        mine = jnp.concatenate([new_keys[t * BLOCK + r : t * BLOCK + r + 1] for t in range(steps)], axis=0)
        padded = jnp.concatenate([mine, jnp.zeros((16 - steps, mine.shape[1]), f32)], axis=0).astype(bf16)
        for t in range(steps):
            raw = dot(padded, queries[t, r]) * scale
            own = jnp.concatenate([raw, jnp.zeros((heads - 16, heads), f32)], axis=0).T
            highest = held[1][held[3], t]
            columns = [own[:, k : k + 1] for k in range(t + 1)]
            peak = highest
            for column in columns:
                peak = jnp.maximum(peak, column)
            keep = jnp.exp(highest - peak)
            weights = [jnp.exp(column - peak) for column in columns]
            below = held[2][held[3], t] * keep + sum(weights)
            value = held[0][held[3], t] * (keep / below)
            for k in range(t + 1):
                share = (weights[k] / below).astype(bf16).astype(f32)
                value = value + share * mine[k : k + 1, :LAT]
            for j in range(lanes):
                rows[r % 2, pl.ds(j * steps + t, heads, stride=lanes * steps), :] = value[:, j * 128 : (j + 1) * 128]
        out[r] = rows[r % 2].astype(bf16)


def merge(queries, keys, first, last, scale):
    steps, count, _, heads = queries.shape
    tall = heads * steps * LAT // 128
    return call(
        functools.partial(merge_kernel, scale), [((count, tall, 128), bf16)], queries, keys, *first, *last,
        limit=20, scratch=[pltpu.VMEM((2, tall, 128), f32)],
    )[0]


def project_kernel(core, hidden, own0, a0, b0, c0, own1, a1, b1, c1, gain, kv_own, kv_other, kv_gain, turns, layer, keys, stage):
    mixture = jnp.concatenate(
        [
            own[...] + a[...].astype(f32) + b[...].astype(f32) + c[...].astype(f32)
            for own, a, b, c in ((own0, a0, b0, c0), (own1, a1, b1, c1))
        ],
        axis=0,
    )
    both = (hidden[...].astype(f32) + mixture).astype(bf16)
    many, width = both.shape
    wide = both.astype(f32)
    for k in range(width // 128):
        for t in range(2):
            stage[pl.ds(2 * k + t, BLOCK, stride=width // 64), :] = wide[
                t * BLOCK : (t + 1) * BLOCK, k * 128 : (k + 1) * 128
            ]
    layer[...] = stage[...].astype(bf16)
    normed = rms_scale(both, gain[...]).astype(bf16)
    half = normed.shape[1] // 2
    swapped = core[0] > 0
    low, high = normed[:, :half].astype(f32), normed[:, half:].astype(f32)
    first = jnp.where(swapped, high, low).astype(bf16)
    second = jnp.where(swapped, low, high).astype(bf16)
    projected = (dot(kv_own[...], first, NT) + dot(kv_other[...], second, NT)).T
    keys[:, :LAT] = rms_scale(projected[:, :LAT], kv_gain[...]).astype(bf16)
    rope = projected[:, LAT:]
    crossed = jnp.concatenate([-rope[:, ROPE // 2 :], rope[:, : ROPE // 2]], axis=1)
    keys[:, LAT:] = (rope * turns[0] + crossed * turns[1]).astype(bf16)


def hold(*values):
    return lax.optimization_barrier(values)


def steps_y(mine):
    return [mine, shift(mine, "y", 1), shift(mine, "y", 3), shift(mine, "y", 2)]


def ring_x(own):
    return shift(own, "x", 1), shift(own, "x", 3)


def far_x(left, right):
    half = left.shape[0] // 2
    return [shift(left[:half], "x", 1), shift(right[half:], "x", 3)]


def steps_z(parts, sign):
    return [parts[0]] + [shift(parts[i], "z", sign * i % SIDE) for i in (1, 2, 3)]


CHIPS = ("y", "z", "x")


def fresh_cut(fresh_t):
    width, context = fresh_t.shape
    count = lax.axis_size(CHIPS)
    tiles = width * context // 1024
    each = -(-tiles // count)
    cut = fresh_t.reshape(width // 8, 8, context // 128, 128).swapaxes(1, 2).reshape(tiles, 8, 128)
    cut = jnp.pad(cut, ((0, each * count - tiles), (0, 0), (0, 0)))
    return cut.reshape(count, each * 8, 128)


def fresh_join(whole, width, context):
    tiles = width * context // 1024
    whole = whole.reshape(-1, 8, 128)[:tiles].reshape(width // 8, context // 128, 8, 128)
    return whole.swapaxes(1, 2).reshape(width, context)


def around(value):
    return jnp.where(value < 0, value + SIDE, jnp.where(value >= SIDE, value - SIDE, value))


def pack_kernel(place, cut, *outs):
    for kx in range(SIDE):
        for ky in range(SIDE):
            for kz in range(SIDE):
                y, z, x = around(place[0] + ky), around(place[1] + kz), around(place[2] + kx)
                outs[kx][ky * SIDE + kz] = cut[(y * SIDE + z) * SIDE + x]


def regroup_kernel(last, *refs):
    ins, outs = refs[:SIDE], refs[SIDE:]
    for a in range(SIDE):
        for b in range(SIDE):
            for c in range(SIDE):
                if last:
                    outs[c][b * SIDE + a] = ins[a][b * SIDE + c]
                else:
                    outs[b][a * SIDE + c] = ins[a][b * SIDE + c]


def sort_kernel(order, place, here, there, *outs):
    count = here.shape[0]
    for jz in range(SIDE):
        for jy in range(SIDE):
            for jx in range(SIDE):
                y, z, x = around(place[0] + jy), around(place[1] + jz), around(place[2] + jx)
                wanted = order[place[3] * count + (y * SIDE + z) * SIDE + x]
                upper = wanted >= count
                source = jnp.where(upper, wanted - count, wanted)
                sy, sz, sx = source >> 4, (source >> 2) & 3, source & 3
                kx, ky, kz = around(place[2] - sx), around(place[0] - sy), around(place[1] - sz)
                index = (kz * SIDE + kx) * SIDE + ky
                other = jnp.where(upper, 1, 0) != place[3]
                out = outs[jz].at[jy * SIDE + jx]

                @pl.when(other)
                def _(out=out, index=index):
                    out[...] = there[index]

                @pl.when(jnp.logical_not(other))
                def _(out=out, index=index):
                    out[...] = here[index]


def unpack_kernel(place, x0, x1, x2, x3, whole):
    for jx, part in enumerate((x0, x1, x2, x3)):
        for jz in range(SIDE):
            for jy in range(SIDE):
                y, z, x = around(place[0] - jy), around(place[1] - jz), around(place[2] - jx)
                whole[(y * SIDE + z) * SIDE + x] = part[jz * SIDE + jy]


def quarters(kernel, *args, smem=0):
    rows, lanes = args[-1].shape[1:]
    return call(kernel, [((SIDE * SIDE, rows, lanes), bf16)] * SIDE, *args, smem=smem)


def regroup(last, parts):
    return quarters(functools.partial(regroup_kernel, last), *parts)


def stage(parts, axis):
    return [parts[0], *[shift(parts[i], axis, i) for i in (1, 2, 3)]]


def shards(
    hidden_in,
    ffn_gain,
    attn_gain,
    kv_gain,
    expert_ids,
    route_weight,
    expert_gate,
    expert_up,
    expert_down,
    kv_down,
    resident_cache,
    fresh_cache,
    fresh_order,
    cache_len,
    queries,
):
    steps_count, local_rows, model_width = hidden_in.shape
    resident_rows = resident_cache.shape[0]
    score_scale = (NOPE + ROPE) ** (-0.5)
    core = lax.axis_index("c").astype(jnp.int32).reshape(1)

    payload, hidden_rows = call(
        prepare_kernel,
        [((steps_count * BLOCK, model_width + META), bf16), ((steps_count * BLOCK, model_width), bf16)],
        expert_ids.swapaxes(1, 2), route_weight.swapaxes(1, 2), hidden_in.swapaxes(0, 1), ffn_gain[None],
    )

    position = jnp.stack([lax.axis_index(axis) for axis in ("y", "z", "x", "c")]).astype(jnp.int32)
    folded = ((2 * PART, model_width // 2), bf16)
    query_t = queries.swapaxes(2, 3)
    resident_t = resident_cache.swapaxes(1, 2)

    slot_half = SLOTS // 2
    rows = (BLOCK, model_width)

    def select(step, held):
        *parts, weight = call(
            functools.partial(select_kernel, step), [folded] * SIDE + [((2, SIDE * 2 * PART, SIDE * BLOCK), f32)],
            position, *held, smem=1,
        )
        return parts, weight

    def assemble(parts):
        return call(assemble_kernel, [((SLOTS, model_width), bf16)], *parts)[0]

    def combine(weight, parts):
        return call(combine_kernel, [(rows, f32), (rows, bf16), (rows, bf16), (rows, bf16)], weight, *parts)

    def back_y(own, one, two, three):
        return [own, shift(one, "y", 3), shift(two, "y", 1), shift(three, "y", 2)]

    def finish(own, plus, minus, la, rb):
        return call(finish_kernel, [folded] * SIDE, own, plus, minus, la, rb)

    def run_experts(pieces, swapped):
        return experts(list(pieces), list(swapped), expert_gate, expert_up, expert_down)

    def meet(ra, lb, plus, minus):
        return add(ra, plus[slot_half:]), add(lb, minus[slot_half:])

    held = steps_y(payload)
    moving = stage(quarters(pack_kernel, position, fresh_cut(fresh_cache[0].T), smem=1), "x")
    held, moving = hold(held, moving)
    parts, weight0 = select(0, held)
    parts = steps_z(parts, 1)
    parts1, weight1 = select(1, held)
    moving = stage(regroup(False, moving), "y")
    parts, weight0, parts1, weight1, moving = hold(parts, weight0, parts1, weight1, moving)
    own = assemble(parts)
    near = ring_x(own)
    parts = steps_z(parts1, 1)
    moving = regroup(True, moving)
    own, near, parts, moving = hold(own, near, parts, moving)
    far = far_x(*near)
    around_own = jnp.concatenate([own, *near], axis=0)
    near_swapped = swap(around_own)
    own1 = assemble(parts)
    around_own, far, near_swapped, own1, moving = hold(around_own, far, near_swapped, own1, moving)
    moving = stage(moving, "z")
    near1 = ring_x(own1)
    far_swapped = [swap(piece) for piece in far]
    kept0, sent0 = run_experts([around_own, *far], [near_swapped, *far_swapped])
    own1, near1, kept0, sent0, moving = hold(own1, near1, kept0, sent0, moving)
    far = far_x(*near1)
    got0 = swap(sent0)
    around_own = jnp.concatenate([own1, *near1], axis=0)
    near_swapped = swap(around_own)
    own0, lb0, ra0, plus0, minus0 = pair_sums(kept0, got0)
    here = jnp.concatenate(moving, axis=0)
    moving = quarters(sort_kernel, fresh_order, position, here, swap(here), smem=2)
    far, near_swapped, around_own, own0, lb0, ra0, plus0, minus0, moving = hold(
        far, near_swapped, around_own, own0, lb0, ra0, plus0, minus0, moving
    )
    plus0, minus0 = shift(plus0, "x", 1), shift(minus0, "x", 3)
    far_swapped = [swap(piece) for piece in far]
    kept1, sent1 = run_experts([around_own, *far], [near_swapped, *far_swapped])
    moving = stage(moving, "z")
    plus0, minus0, kept1, sent1, moving = hold(plus0, minus0, kept1, sent1, moving)
    ra0, lb0 = meet(ra0, lb0, plus0, minus0)
    la0, rb0 = shift(ra0, "x", 1), shift(lb0, "x", 3)
    got1, moving = hold(swap(sent1), moving)
    moving = stage(regroup(False, moving), "y")
    own1, lb1, ra1, plus1, minus1 = pair_sums(kept1, got1)
    la0, rb0, own1, lb1, ra1, plus1, minus1, moving = hold(
        la0, rb0, own1, lb1, ra1, plus1, minus1, moving
    )
    plus1, minus1 = shift(plus1, "x", 1), shift(minus1, "x", 3)
    parts = steps_z(finish(own0, plus0, minus0, la0, rb0), -1)
    moving = regroup(True, moving)
    past_resident = past(cache_len, query_t, resident_t, score_scale, 0)
    other_down = swap(kv_down.T)
    plus1, minus1, parts0, moving, past_resident, other_down = hold(
        plus1, minus1, parts, moving, past_resident, other_down
    )
    ra1, lb1 = meet(ra1, lb1, plus1, minus1)
    la1, rb1 = shift(ra1, "x", 1), shift(lb1, "x", 3)
    mixed0 = back_y(*combine(weight0, parts0))
    la1, rb1, mixed0, moving = hold(la1, rb1, mixed0, moving)
    parts = steps_z(finish(own1, plus1, minus1, la1, rb1), -1)
    moving = stage(moving, "x")
    parts, moving = hold(parts, moving)
    mixed = [*mixed0, *back_y(*combine(weight1, parts))]
    (whole,) = call(unpack_kernel, [((SIDE**3, *moving[0].shape[1:]), bf16)], position, *moving, smem=1)
    fresh_t = fresh_join(whole, LAT + ROPE, fresh_cache.shape[1])[None]
    past_fresh = past(cache_len[resident_rows:], query_t, fresh_t, score_scale, resident_rows)
    mixed, past_fresh = hold(mixed, past_fresh)

    positions = jnp.pad(cache_len, (0, BLOCK - local_rows)).astype(f32)
    positions = (positions[None, :] + jnp.arange(steps_count).astype(f32)[:, None]).reshape(-1, 1)
    frequency = (rope_base ** (-2.0 * np.arange(ROPE // 2) / ROPE)).astype(np.float32)
    angles = positions * jnp.asarray(np.tile(frequency, 2))[None, :]
    turns = jnp.stack([jnp.cos(angles), jnp.sin(angles)])
    many = steps_count * BLOCK
    layer, keys = call(
        project_kernel,
        [((many * model_width // 128, 128), bf16), ((many, LAT + ROPE), bf16)],
        core, hidden_rows, *mixed, attn_gain[None], kv_down.T, other_down, kv_gain[None], turns,
        smem=1, limit=18, scratch=[pltpu.VMEM((many * model_width // 128, 128), f32)],
    )
    tall = model_width // 128
    layer = layer[: local_rows * steps_count * tall].reshape(local_rows, tall, steps_count, 128)
    layer_out = layer.transpose(2, 0, 1, 3).reshape(steps_count, local_rows, model_width)
    attended = merge(query_t, keys, past_resident, past_fresh, score_scale)
    attended = attended.reshape(local_rows, -1, steps_count, 128).transpose(2, 0, 1, 3)
    return layer_out, attended.reshape(steps_count, local_rows, -1)


def solution(mesh):
    grid = Mesh(mesh.devices.reshape(2, 4, 4, 4), ("c", "y", "z", "x"))
    every = ("c", "y", "z", "x")
    placed = (
        P(None, every, None),
        P(),
        P(),
        P(),
        P(None, every, None),
        P(None, every, None),
        P(every, None, None),
        P(every, None, None),
        P(every, None, None),
        P("c", None),
        P(every, None, None),
        P(every, None, None),
        P(),
        P(every),
        P(None, every, None, None),
    )
    return jax.shard_map(
        shards,
        mesh=grid,
        in_specs=placed,
        out_specs=(P(None, every, None), P(None, every, None)),
        check_vma=False,
    )
```
